512 devices in a mesh: dp: 32 (over z, core), crow: 4 (over x), ccol: 4 (over y).
Axes of the slice: x: 4, y: 4, z: 16, core: 2. Of those that a mesh axis runs over, the one named last changes fastest.
Arguments:
- data: float32 [16, 262144], P(None, ('dp', 'crow')), may hold values from 0 to 1
- centres: float32 [16, 3072], P(None, 'ccol'), may hold values from 0 to 1
- scales: float32 [16], replicated, may hold values from 0.5 to 1.2
- factor: float32 [3072, 3072], P('crow', 'ccol'), may hold values from -1 to 1, as said below
- block_inv: float32 [12, 256, 256], P('crow'), may hold values from -1 to 2
- iterate: float32 [8, 3072], replicated, may hold values from -6 to 6
- residual: float32 [8, 3072], replicated, may hold values from -6 to 6
- direction: float32 [8, 3072], replicated, may hold values from -6 to 6
Outputs:
- new_iterate: float32 [8, 3072], replicated
- new_residual: float32 [8, 3072], replicated
- new_direction: float32 [8, 3072], replicated
The draws below stay inside these ranges and needn't reach their ends.
Inputs may be any that keep to these rules, and one draw needn't show every extreme that they name: `factor`: blocks of 256 x 256 on and above the block diagonal are zero.
All inputs are finite; a program needn't handle non-finite values.
Results may differ from the reference program's by a relative error of at most 0.0001.
Values sent between devices are 32-bit elements; how exact they have to be, the bound alone decides.
A program may use at most 64 MiB of HBM per device.

```python
import math
import jax
import jax.numpy as jnp
from jax import lax

INPUTS = 16
BLOCK = 256
NBLK = 12
CENTRES = 3072
NRHS = 8
RBLK = 1024
NROWS = 262144


def draw_factor(key, part):
    total = BLOCK * NBLK
    values = jax.random.normal(key, (total, total), jnp.float32)
    row_block = jnp.arange(total)[:, None] // BLOCK
    col_block = jnp.arange(total)[None, :] // BLOCK
    scaled = values * (0.5 / math.sqrt(total))
    return jnp.where(row_block > col_block, scaled, 0.0).astype(jnp.float32)


def draw_block_inv(key, part):
    first = jax.random.fold_in(key, 11)
    second = jax.random.fold_in(key, 23)
    identity = jnp.eye(BLOCK, dtype=jnp.float32)
    leading = jax.random.uniform(first, (NBLK, BLOCK), jnp.float32, 0.7, 1.4)
    spread = jax.random.normal(second, (NBLK, BLOCK, BLOCK), jnp.float32)
    spread = spread * (0.35 / math.sqrt(BLOCK))
    return (spread * (1.0 - identity) + identity * leading[:, :, None]).astype(jnp.float32)


def shard_levels(rng, extent, split, low, largest):
    def one(axis_at, shards_of):
        steps = jax.random.uniform(jax.random.fold_in(jax.random.fold_in(rng, 6), axis_at), (shards_of,), jnp.float32, low / len(split), largest / len(split))
        return jnp.repeat(jnp.exp(steps), extent[axis_at] // shards_of).reshape((-1,) + (1,) * (len(extent) - axis_at - 1))

    factor_of = one(*split[0])
    for cut in split[1:]:
        factor_of = factor_of * one(*cut)
    return factor_of


def bell_draw(rng, dims, width, reach, kind=jnp.bfloat16):
    entries = jax.random.normal(rng, dims, jnp.float32) * width
    return jnp.minimum(jnp.maximum(entries, -reach), reach).astype(kind)


def setup_inputs(seed: int = 0) -> dict:
    streams_of = jax.random.split(jax.random.key(seed), 9)
    return {
        "data": jnp.clip(1.0 * jax.random.uniform(streams_of[0], (INPUTS, NROWS), jnp.float32) ** shard_levels(streams_of[0], (INPUTS, NROWS), ((1, 128),), -0.2, 0.2), 0.0, 1.0),
        "centres": jnp.clip(1.0 * jax.random.uniform(streams_of[1], (INPUTS, CENTRES), jnp.float32) ** shard_levels(streams_of[1], (INPUTS, CENTRES), ((1, 4),), -0.2, 0.2), 0.0, 1.0),
        "scales": jnp.clip(jnp.exp(jax.random.uniform(streams_of[2], (INPUTS,), jnp.float32, math.log(0.5), math.log(1.2))), 0.5, 1.2),
        "factor": draw_factor(jax.random.fold_in(streams_of[8], 71), 0),
        "block_inv": draw_block_inv(jax.random.fold_in(streams_of[8], 71), 0),
        "iterate": bell_draw(streams_of[5], (NRHS, CENTRES), 1.0, 6.0, jnp.float32),
        "residual": bell_draw(streams_of[6], (NRHS, CENTRES), 1.0, 6.0, jnp.float32),
        "direction": bell_draw(streams_of[7], (NRHS, CENTRES), 1.0, 6.0, jnp.float32),
    }


ridge_weight = 0.2
highest = lax.Precision.HIGHEST


def kernel_tile(sample, centre_set, scales):
    scaled_sample = sample / scales[:, None]
    scaled_centres = centre_set / scales[:, None]
    cross_terms = lax.dot_general(scaled_centres, scaled_sample, (((0,), (0,)), ((), ())), precision=highest, preferred_element_type=jnp.float32)
    distance = jnp.sum(scaled_centres * scaled_centres, axis=0)[:, None] + jnp.sum(scaled_sample * scaled_sample, axis=0)[None, :] - 2.0 * cross_terms
    return jnp.exp(-0.5 * distance)


def project(weights, tile):
    return jnp.dot(weights, tile, precision=highest, preferred_element_type=jnp.float32)


def pullback(images, tile):
    return lax.dot_general(images, tile, (((1,), (1,)), ((), ())), precision=highest, preferred_element_type=jnp.float32)


def back_solve(direction, factor, block_inv):
    solved = jnp.zeros_like(direction)
    for number in reversed(range(NBLK)):
        start = number * BLOCK
        partial_value = project(solved, factor[:, start:start + BLOCK])
        piece = project(direction[:, start:start + BLOCK] - partial_value, block_inv[number])
        solved = solved.at[:, start:start + BLOCK].set(piece)
    return solved


def fore_solve(source, factor, block_inv):
    solved = jnp.zeros_like(source)
    for number in range(NBLK):
        start = number * BLOCK
        partial_value = pullback(solved, factor[start:start + BLOCK, :])
        piece = pullback(source[:, start:start + BLOCK] - partial_value, block_inv[number])
        solved = solved.at[:, start:start + BLOCK].set(piece)
    return solved


def reference(data, centres, scales, factor, block_inv, iterate, residual, direction):
    solved = back_solve(direction, factor, block_inv)
    blocks = NROWS // RBLK
    stacked = data.reshape(INPUTS, blocks, RBLK).transpose(1, 0, 2)

    def accumulate(total, sample):
        tile = kernel_tile(sample, centres, scales)
        return total + pullback(project(solved, tile), tile), None

    summed, _ = lax.scan(accumulate, jnp.zeros((NRHS, CENTRES), jnp.float32), stacked)
    normal_image = summed / NROWS + ridge_weight * solved
    image = fore_solve(normal_image, factor, block_inv)
    gamma = jnp.sum(residual * residual, axis=1)
    curvature = jnp.sum(direction * image, axis=1)
    alpha = (gamma / curvature)[:, None]
    new_iterate = iterate + alpha * direction
    new_residual = residual - alpha * image
    gamma_next = jnp.sum(new_residual * new_residual, axis=1)
    new_direction = new_residual + (gamma_next / gamma)[:, None] * direction
    return (new_iterate, new_residual, new_direction)
```

```python
import functools

import jax
import jax.numpy as jnp
from jax import lax
from jax.experimental import pallas as pl
from jax.experimental.pallas import tpu as pltpu
from jax.sharding import PartitionSpec as P

MESH = pl.DeviceIdType.MESH
f32 = jnp.float32
bf16 = jnp.bfloat16
HIGHEST = lax.Precision.HIGHEST
ridge_weight = 0.2

NN = (((1,), (0,)), ((), ()))
NT = (((1,), (1,)), ((), ()))
TN = (((0,), (0,)), ((), ()))


def dot(a, b, dims=NN, precision=None):
    return lax.dot_general(a, b, dims, precision=precision, preferred_element_type=f32)


def split2(v):
    high = v.astype(bf16)
    return high, (v - high.astype(f32)).astype(bf16)


def split3(v):
    high = v.astype(bf16)
    rest = v - high.astype(f32)
    mid = rest.astype(bf16)
    return high, mid, (rest - mid.astype(f32)).astype(bf16)


def product(v, high, low, dims=NN):
    rows = v.shape[0]
    both = jnp.concatenate(split2(v), axis=0)
    out = dot(both, low, dims) + dot(both, high, dims)
    return out[rows:] + out[:rows]


def ring_distance(d, n):
    d = d % n
    return min(d, n - d)


class Semaphores:
    def __init__(self):
        self.count = 0

    def take(self, n):
        first = self.count
        self.count += n
        return first


S = Semaphores()
LOAD = S.take(8)
CEN_R = S.take(4)
CEN_S = S.take(3)
CENF_S = S.take(4)
P_R = S.take(4)
P_S = S.take(16)
PF_S = S.take(4)
PROD_R = S.take(4)
PROD_S = S.take(1)
N_R = S.take(1)
N_S = S.take(16)
Z_R = S.take(1)
Z_S = S.take(16)
M_R = S.take(3)
M_S = S.take(1)
IMG_R = S.take(4)
IMG_S = S.take(16)
IMGF_S = S.take(4)
BACK_R = S.take(4)
BACK_S = S.take(1)


def kernel(
    planes,
    total_rows,
    data,
    centres,
    scales,
    factor,
    block_inv,
    iterate,
    residual,
    direction,
    new_iterate,
    new_residual,
    new_direction,
    fac,
    inv,
    whi,
    wlo,
    thi,
    tlo,
    rows,
    cen,
    khi,
    klo,
    itv,
    rev,
    div,
    pulled,
    prod_out,
    prod_in,
    nsend,
    nred,
    zred,
    mout,
    min_,
    img,
    back_out,
    back_in,
    sems,
    zready,
):
    dp = lax.axis_index("dp")
    r = lax.axis_index("crow")
    c = lax.axis_index("ccol")
    core = lax.rem(dp, 2)
    z = dp // 2
    solver = core == 1
    width = fac.shape[0]
    span = rows.shape[1]
    order = inv.shape[1]
    pending = []

    def local(src, dst, k):
        return pltpu.make_async_copy(src, dst, sems.at[LOAD + k])

    def remote(src, dst, ss, rs, dev):
        return pltpu.make_async_remote_copy(
            src_ref=src,
            dst_ref=dst,
            send_sem=sems.at[ss],
            recv_sem=sems.at[rs],
            device_id=dev,
            device_id_type=MESH,
        )

    def arrived(dst, rs):
        pltpu.make_async_copy(dst, dst, sems.at[rs]).wait()

    def send(cond, src, dst, ss, rs, dev):
        remote(src(), dst(), ss, rs, dev).start()
        pending.append((cond, src, ss))

    load_fac = local(factor, fac, 0)
    load_inv = local(block_inv, inv, 1)
    load_dir = local(direction, div, 2)
    load_cen = local(centres, cen.at[c], 3)
    load_rows = local(data.at[:, pl.ds(pl.multiple_of(c * span, 128), span)], rows, 4)
    load_res = local(residual, rev, 5)
    load_it = local(iterate, itv, 6)
    diagonal = solver & (r == c)
    below = solver & (r > c)

    @pl.when(diagonal)
    def _():
        load_inv.start()

    load_dir.start()

    @pl.when(diagonal | below)
    def _():
        load_fac.start()

    load_cen.start()
    load_rows.start()
    load_res.start()
    load_it.start()

    barrier = pltpu.get_barrier_semaphore()
    near = sorted({d % planes for d in (1, 2, 3, 4, -1, -2, -3, -4)} - {0})
    relay = sorted({d % planes for d in (4, -4)}) if planes > 9 else []
    offsets = sorted(
        [(a, b) for a in range(4) for b in range(4)],
        key=lambda o: (-ring_distance(o[0], 4) - ring_distance(o[1], 4), o),
    )

    def signal(sem, dev):
        pl.semaphore_signal(sem, inc=1, device_id=dev, device_id_type=MESH)

    @pl.when(solver)
    def _():
        for a, b in offsets[:-1]:
            signal(barrier, (dp, lax.rem(r + a, 4), lax.rem(c + b, 4)))
        for d in near:
            signal(barrier, (2 * lax.rem(z + d, planes) + 1, r, c))
        signal(barrier, (dp - 1, r, c))

    @pl.when(core == 0)
    def _():
        signal(barrier, (dp + 1, r, c))

    load_dir.wait()

    first = solver & (r == 3) & (c == 3)

    @pl.when(first)
    def _():
        load_inv.wait()
        load_fac.wait()
        b = [slice(k * order, (k + 1) * order) for k in range(3)]
        base = 3 * width
        d = [div[:, base + k * order : base + (k + 1) * order] for k in range(3)]
        p2 = dot(d[2], inv[2], NN, HIGHEST)
        p1 = dot(d[1] - dot(p2, fac[b[2], b[1]], NN, HIGHEST), inv[1], NN, HIGHEST)
        t0 = d[0] - dot(p2, fac[b[2], b[0]], NN, HIGHEST)
        p0 = dot(t0 - dot(p1, fac[b[1], b[0]], NN, HIGHEST), inv[0], NN, HIGHEST)
        pulled[3, :, b[0]] = p0
        pulled[3, :, b[1]] = p1
        pulled[3, :, b[2]] = p2

    def keep(v, i, j):
        si = slice(i * order, (i + 1) * order)
        sj = slice(j * order, (j + 1) * order)
        whi[si, sj], wlo[si, sj] = split2(v)
        thi[sj, si], tlo[sj, si] = split2(v.T)

    @pl.when(below)
    def _():
        load_fac.wait()
        for i in range(3):
            for j in range(3):
                keep(fac[i * order : (i + 1) * order, j * order : (j + 1) * order], i, j)

    @pl.when(solver)
    def _():
        pl.semaphore_wait(barrier, 15 + len(near) + 1)
        for d in relay:
            signal(zready, (2 * lax.rem(z + d, planes) + 1, r, c))

    @pl.when(core == 0)
    def _():
        pl.semaphore_wait(barrier, 1)

    def spread(k, cond, buf, ss, rs, urgent):
        rest = [o for o in offsets[:-1] if ((k + o[0]) % 4, (k + o[1]) % 4) not in urgent]
        goals = urgent + [((k + a) % 4, (k + b) % 4) for a, b in rest]
        for i, (a, b) in enumerate(goals):
            send(cond, lambda: buf.at[k], lambda: buf.at[k], ss + i, rs + k, (dp, a, b))

    def give_core0(cond, buf, k, ss, rs):
        send(cond, lambda: buf.at[k], lambda: buf.at[k], ss + k, rs + k, (dp - 1, r, c))

    @pl.when(first)
    def _():
        spread(3, first, pulled, P_S, P_R, [(3, 2), (3, 1), (3, 0)])

    load_cen.wait()

    @pl.when(solver)
    def _():
        for i, d in enumerate((2, 1, 3)):
            send(solver, lambda: cen.at[c], lambda: cen.at[c], CEN_S + i, CEN_R + c, (dp, r, lax.rem(c + d, 4)))

    def invert():
        b = [slice(k * order, (k + 1) * order) for k in range(3)]
        mul = functools.partial(dot, precision=HIGHEST)
        zero = jnp.zeros((order, order), f32)
        a0, a1, a2 = inv[0], inv[1], inv[2]
        x10 = -mul(a1, mul(fac[b[1], b[0]], a0))
        x21 = -mul(a2, mul(fac[b[2], b[1]], a1))
        x20 = -mul(a2, mul(fac[b[2], b[0]], a0) + mul(fac[b[2], b[1]], x10))
        for i, row in enumerate(((a0, zero, zero), (x10, a1, zero), (x20, x21, a2))):
            for j, v in enumerate(row):
                keep(v, i, j)

    @pl.when(diagonal & (r != 3))
    def _():
        load_inv.wait()
        load_fac.wait()
        invert()

    scale_col = jnp.zeros((rows.shape[0], 1), f32)
    place = lax.broadcasted_iota(jnp.int32, (rows.shape[0], 1), 0)
    for k in range(rows.shape[0]):
        scale_col = jnp.where(place == k, scales[k], scale_col)

    load_rows.wait()

    for i, d in enumerate((1, 3, 2)):
        src = lax.rem(c + d, 4)
        arrived(cen.at[src], CEN_R + src)

        @pl.when(solver)
        def _():
            send(solver, lambda src=src: cen.at[src], lambda src=src: cen.at[src], CENF_S + i, CEN_R + src, (dp - 1, r, c))

    def tiles():
        x = rows[...] / scale_col
        xh, xm, xl = split3(x)
        right = jnp.concatenate([xh, xm, xh, xl, xh, xm], axis=0)
        xn = -0.5 * jnp.sum(x * x, axis=0)[None, :]
        for k in range(4):
            for q in range(3):
                m = cen[k, :, q * order : (q + 1) * order] / scale_col
                mh, mm, ml = split3(m)
                left = jnp.concatenate([mh, mh, mm, mh, ml, mm], axis=0)
                mn = -0.5 * jnp.sum(m * m, axis=0)[:, None]
                v = jnp.exp(dot(left, right, TN) + mn + xn)
                at = slice(k * width + q * order, k * width + (q + 1) * order)
                khi[at, :], klo[at, :] = split2(v)

    @pl.when((r != 3) | (core == 0))
    def _():
        tiles()

    images = jnp.zeros((div.shape[0], span), f32)

    for k in (3, 2, 1, 0):
        mine = solver & (r == k) & (c == k)

        if k < 3:

            @pl.when(mine)
            def _():
                t = div[:, k * width : (k + 1) * width]
                for j in range(3, k, -1):
                    arrived(prod_in.at[j], PROD_R + j)
                    t = t - prod_in[j]
                pulled[k] = product(t, whi[...], wlo[...])
                spread(k, mine, pulled, P_S, P_R, [(k, j) for j in range(k - 1, -1, -1)])

        @pl.when(jnp.logical_not(mine))
        def _():
            arrived(pulled.at[k], P_R + k)

        multiply = solver & (r == k) & (c < k)

        if k > 0:

            @pl.when(multiply)
            def _():
                prod_out[...] = product(pulled[k], whi[...], wlo[...])
                send(multiply, lambda: prod_out, lambda: prod_in.at[k], PROD_S, PROD_R + k, (dp, c, c))

        @pl.when(solver)
        def _():
            give_core0(solver, pulled, k, PF_S, P_R)

        if k == 3:

            @pl.when((r == 3) & solver)
            def _():
                tiles()

            @pl.when(first)
            def _():
                invert()

        at = slice(k * width, (k + 1) * width)
        images = images + product(pulled[k], khi[at, :], klo[at, :])

    both = jnp.concatenate(split2(images), axis=0)
    rhs = div.shape[0]
    for i, (a, b) in enumerate(offsets):
        x = lax.rem(r + a, 4)
        y = lax.rem(c + b, 4)
        gap = lax.rem(y - x + 4, 4)
        owned = gap != 2
        chunk = 3 * x + jnp.where(gap == 3, 2, gap)
        slot = 2 * i + core

        @pl.when(owned)
        def _():
            at = pl.ds(pl.multiple_of(chunk * order, order), order)
            out = dot(both, klo[at, :], NT) + dot(both, khi[at, :], NT)
            nsend[chunk] = out[rhs:] + out[:rhs]

        if i < 15:

            @pl.when(owned)
            def _():
                send(owned, lambda chunk=chunk: nsend.at[chunk], lambda: nred.at[slot], N_S + i, N_R, (2 * z + 1, x, y))

        else:

            @pl.when(owned & solver)
            def _():
                nred[31] = nsend[chunk]

            away = owned & (core == 0)

            @pl.when(away)
            def _():
                send(away, lambda chunk=chunk: nsend.at[chunk], lambda: nred.at[30], N_S + i, N_R, (2 * z + 1, x, y))

    gap = lax.rem(c - r + 4, 4)
    owner = solver & (gap != 2)
    part = jnp.where(gap == 3, 2, gap)

    if relay:

        @pl.when(solver)
        def _():
            pl.semaphore_wait(zready, len(relay))

    far = sorted(range(1, planes), key=lambda d: -ring_distance(d, planes))

    @pl.when(owner)
    def _():
        arrived(nred.at[0:31], N_R)
        total = nred[0]
        for s in range(1, 32):
            total = total + nred[s]
        zred[z] = total
        for i, d in enumerate(far):
            send(
                owner,
                lambda: zred.at[z],
                lambda: zred.at[z],
                Z_S + i,
                Z_R,
                (2 * lax.rem(z + d, planes) + 1, r, c),
            )
        arrived(zred.at[0 : planes - 1], Z_R)
        total = zred[0]
        for s in range(1, planes):
            total = total + zred[s]
        mout[...] = total * (1.0 / total_rows)

    passing = owner & (gap != 0)

    @pl.when(passing)
    def _():
        send(passing, lambda: mout, lambda: min_.at[part], M_S, M_R + part, (dp, r, r))

    @pl.when(diagonal)
    def _():
        min_[0] = mout[...]
        arrived(min_.at[1], M_R + 1)
        arrived(min_.at[2], M_R + 2)

    for k in range(4):
        mine = solver & (r == k) & (c == k)

        @pl.when(mine)
        def _():
            t = jnp.concatenate([min_[0], min_[1], min_[2]], axis=1) + ridge_weight * pulled[k]
            for j in range(k):
                arrived(back_in.at[j], BACK_R + j)
                t = t - back_in[j]
            img[k] = product(t, thi[...], tlo[...])
            spread(k, mine, img, IMG_S, IMG_R, [(j, k) for j in range(k + 1, 4)])

        @pl.when(jnp.logical_not(mine))
        def _():
            arrived(img.at[k], IMG_R + k)

        multiply = solver & (c == k) & (r > k)

        if k < 3:

            @pl.when(multiply)
            def _():
                back_out[...] = product(img[k], thi[...], tlo[...])
                send(multiply, lambda: back_out, lambda: back_in.at[k], BACK_S, BACK_R + k, (dp, r, r))

        @pl.when(solver)
        def _():
            give_core0(solver, img, k, IMGF_S, IMG_R)

    load_res.wait()
    load_it.wait()
    gamma = jnp.sum(rev[...] * rev[...], axis=1, keepdims=True)
    segs = [slice(k * width, (k + 1) * width) for k in range(4)]
    curvature = jnp.zeros((rhs, 1), f32)
    for k in range(4):
        curvature += jnp.sum(div[:, segs[k]] * img[k], axis=1, keepdims=True)
    alpha = gamma / curvature
    gamma_next = jnp.zeros((rhs, 1), f32)
    for k in range(4):
        res = rev[:, segs[k]] - alpha * img[k]
        new_residual[:, segs[k]] = res
        gamma_next += jnp.sum(res * res, axis=1, keepdims=True)
    new_iterate[...] = itv[...] + alpha * div[...]
    new_direction[...] = new_residual[...] + (gamma_next / gamma) * div[...]

    for cond, src, ss in pending:

        @pl.when(cond)
        def _():
            arrived(src(), ss)


def per_device(data, centres, scales, factor, block_inv, iterate, residual, direction):
    planes = lax.axis_size("dp") // 2
    total_rows = data.shape[1] * lax.axis_size("dp") * lax.axis_size("crow")
    inputs, width = centres.shape
    span = data.shape[1] // lax.axis_size("ccol")
    rhs, total = direction.shape
    order = block_inv.shape[1]
    whole = jax.ShapeDtypeStruct((rhs, total), f32)
    vmem = pltpu.VMEM
    hbm = pl.BlockSpec(memory_space=pl.ANY)
    square = (width, width)
    return pl.pallas_call(
        functools.partial(kernel, planes, total_rows),
        out_shape=(whole, whole, whole),
        in_specs=[hbm, hbm, pl.BlockSpec(memory_space=pltpu.SMEM)] + [hbm] * 5,
        out_specs=(pl.BlockSpec(memory_space=pltpu.VMEM),) * 3,
        scratch_shapes=[
            vmem(square, f32),
            vmem((3, order, order), f32),
            vmem(square, bf16),
            vmem(square, bf16),
            vmem(square, bf16),
            vmem(square, bf16),
            vmem((inputs, span), f32),
            vmem((4, inputs, width), f32),
            vmem((total, span), bf16),
            vmem((total, span), bf16),
            vmem((rhs, total), f32),
            vmem((rhs, total), f32),
            vmem((rhs, total), f32),
            vmem((4, rhs, width), f32),
            vmem((rhs, width), f32),
            vmem((4, rhs, width), f32),
            vmem((12, rhs, order), f32),
            vmem((32, rhs, order), f32),
            vmem((planes, rhs, order), f32),
            vmem((rhs, order), f32),
            vmem((3, rhs, order), f32),
            vmem((4, rhs, width), f32),
            vmem((rhs, width), f32),
            vmem((4, rhs, width), f32),
            pltpu.SemaphoreType.DMA((S.count,)),
            pltpu.SemaphoreType.REGULAR,
        ],
        compiler_params=pltpu.CompilerParams(
            collective_id=0, has_side_effects=True, vmem_limit_bytes=50 * 1024 * 1024
        ),
    )(data, centres, scales, factor, block_inv, iterate, residual, direction)


def solution(mesh):
    placed = (
        P(None, ("dp", "crow")),
        P(None, "ccol"),
        P(),
        P("crow", "ccol"),
        P("crow", None, None),
        P(),
        P(),
        P(),
    )
    return jax.shard_map(
        per_device, mesh=mesh, in_specs=placed, out_specs=(P(), P(), P()), check_vma=False
    )
```

```python
import functools

import jax
import jax.numpy as jnp
from jax import lax
from jax.experimental import pallas as pl
from jax.experimental.pallas import tpu as pltpu
from jax.sharding import PartitionSpec as P

MESH = pl.DeviceIdType.MESH
f32 = jnp.float32
bf16 = jnp.bfloat16
HIGHEST = lax.Precision.HIGHEST
ridge_weight = 0.2

NN = (((1,), (0,)), ((), ()))
NT = (((1,), (1,)), ((), ()))
TN = (((0,), (0,)), ((), ()))


def dot(a, b, dims=NN, precision=None):
    return lax.dot_general(a, b, dims, precision=precision, preferred_element_type=f32)


def split2(v):
    high = v.astype(bf16)
    return high, (v - high.astype(f32)).astype(bf16)


def split3(v):
    high = v.astype(bf16)
    rest = v - high.astype(f32)
    mid = rest.astype(bf16)
    return high, mid, (rest - mid.astype(f32)).astype(bf16)


def product(v, high, low, dims=NN):
    rows = v.shape[0]
    both = jnp.concatenate(split2(v), axis=0)
    out = dot(both, low, dims) + dot(both, high, dims)
    return out[rows:] + out[:rows]


def lower(v, high, low, order):
    parts = [product(v[:, j:], high[j:, j : j + order], low[j:, j : j + order]) for j in range(0, v.shape[1], order)]
    return jnp.concatenate(parts, axis=1)


def upper(v, high, low, order):
    parts = []
    for j in range(0, v.shape[1], order):
        parts.append(product(v[:, : j + order], high[: j + order, j : j + order], low[: j + order, j : j + order]))
    return jnp.concatenate(parts, axis=1)


def ring_distance(d, n):
    d = d % n
    return min(d, n - d)


class Semaphores:
    def __init__(self):
        self.count = 0

    def take(self, n):
        first = self.count
        self.count += n
        return first


OWNERS = ((1, 0), (0, 0), (2, 0), (1, 1), (1, 3), (0, 1), (3, 2), (2, 2), (0, 2), (3, 3), (3, 1), (2, 3))
LOW = (1, 0)
HIGH = (3, 2)

S = Semaphores()
LOAD = S.take(8)
CEN_R = S.take(4)
CEN_S = S.take(3)
CENF_S = S.take(4)
P_R = S.take(4)
P_S = S.take(16)
PF_S = S.take(4)
PROD_R = S.take(4)
PROD_S = S.take(1)
N_R = S.take(1)
N_S = S.take(16)
Z_R = S.take(1)
Z_S = S.take(16)
M_R = S.take(6)
M_S = S.take(1)
IMG_R = S.take(4)
IMG_S = S.take(30)
IMGF_S = S.take(4)
BACK_R = S.take(4)
BACK_S = S.take(1)
BULK_R = S.take(6)
BULK_S = S.take(3)


def kernel(
    planes,
    total_rows,
    data,
    centres,
    scales,
    factor,
    block_inv,
    residual,
    direction,
    image,
    alphas,
    betas,
    fac,
    inv,
    whi,
    wlo,
    thi,
    tlo,
    rows,
    cen,
    khi,
    klo,
    rev,
    div,
    pulled,
    prod_out,
    prod_in,
    nsend,
    nred,
    zred,
    mout,
    min_,
    img,
    back_out,
    back_in,
    aux,
    dhi,
    dlo,
    sems,
    zready,
):
    dp = lax.axis_index("dp")
    r = lax.axis_index("crow")
    c = lax.axis_index("ccol")
    core = lax.rem(dp, 2)
    z = dp // 2
    solver = core == 1
    width = fac.shape[0]
    span = rows.shape[1]
    order = inv.shape[1]
    pending = []

    def local(src, dst, k):
        return pltpu.make_async_copy(src, dst, sems.at[LOAD + k])

    def remote(src, dst, ss, rs, dev):
        return pltpu.make_async_remote_copy(
            src_ref=src,
            dst_ref=dst,
            send_sem=sems.at[ss],
            recv_sem=sems.at[rs],
            device_id=dev,
            device_id_type=MESH,
        )

    def arrived(dst, rs):
        pltpu.make_async_copy(dst, dst, sems.at[rs]).wait()

    def send(cond, src, dst, ss, rs, dev):
        remote(src(), dst(), ss, rs, dev).start()
        pending.append((cond, src, ss))

    load_fac = local(factor, fac, 0)
    load_inv = local(block_inv, inv, 1)
    load_dir = local(direction, div, 2)
    load_cen = local(centres, cen.at[c], 3)
    load_rows = local(data.at[:, pl.ds(pl.multiple_of(c * span, 128), span)], rows, 4)
    load_res = local(residual, rev, 5)
    diagonal = solver & (r == c)
    below = solver & (r > c)
    holders = [solver & (r == k) & (c == k) for k in range(4)]

    @pl.when(diagonal)
    def _():
        load_inv.start()

    load_dir.start()

    @pl.when(diagonal | below)
    def _():
        load_fac.start()

    load_cen.start()
    load_rows.start()
    load_res.start()

    barrier = pltpu.get_barrier_semaphore()
    near = sorted({d % planes for d in (1, 2, 3, 4, -1, -2, -3, -4)} - {0})
    relay = sorted({d % planes for d in (4, -4)}) if planes > 9 else []
    offsets = sorted(
        [(a, b) for a in range(4) for b in range(4)],
        key=lambda o: (-ring_distance(o[0], 4) - ring_distance(o[1], 4), o),
    )

    def signal(sem, dev):
        pl.semaphore_signal(sem, inc=1, device_id=dev, device_id_type=MESH)

    @pl.when(solver)
    def _():
        for a, b in offsets[:-1]:
            signal(barrier, (dp, lax.rem(r + a, 4), lax.rem(c + b, 4)))
        for d in near:
            signal(barrier, (2 * lax.rem(z + d, planes) + 1, r, c))
        signal(barrier, (dp - 1, r, c))

    @pl.when(core == 0)
    def _():
        signal(barrier, (dp + 1, r, c))

    load_dir.wait()

    first = solver & (r == 3) & (c == 3)

    @pl.when(first)
    def _():
        load_inv.wait()
        load_fac.wait()
        b = [slice(k * order, (k + 1) * order) for k in range(3)]
        base = 3 * width
        d = [div[:, base + k * order : base + (k + 1) * order] for k in range(3)]
        p2 = dot(d[2], inv[2], NN, HIGHEST)
        p1 = dot(d[1] - dot(p2, fac[b[2], b[1]], NN, HIGHEST), inv[1], NN, HIGHEST)
        t0 = d[0] - dot(p2, fac[b[2], b[0]], NN, HIGHEST)
        p0 = dot(t0 - dot(p1, fac[b[1], b[0]], NN, HIGHEST), inv[0], NN, HIGHEST)
        pulled[3, :, b[0]] = p0
        pulled[3, :, b[1]] = p1
        pulled[3, :, b[2]] = p2

    def keep(v, i, j):
        si = slice(i * order, (i + 1) * order)
        sj = slice(j * order, (j + 1) * order)
        whi[si, sj], wlo[si, sj] = split2(v)
        thi[sj, si], tlo[sj, si] = split2(v.T)

    @pl.when(below)
    def _():
        load_fac.wait()
        for i in range(3):
            for j in range(3):
                keep(fac[i * order : (i + 1) * order, j * order : (j + 1) * order], i, j)

    @pl.when(solver)
    def _():
        pl.semaphore_wait(barrier, 15 + len(near) + 1)
        for d in relay:
            signal(zready, (2 * lax.rem(z + d, planes) + 1, r, c))

    @pl.when(core == 0)
    def _():
        pl.semaphore_wait(barrier, 1)

    def spread(source, k, cond, buf, ss, rs, urgent, first=0, last=15):
        goals = [((source[0] + a) % 4, (source[1] + b) % 4) for a, b in offsets[:-1]]
        goals = urgent + [g for g in goals if g not in urgent]
        for i, (a, b) in enumerate(goals):
            if first <= i < last:
                send(cond, lambda: buf.at[k], lambda: buf.at[k], ss + i, rs + k, (dp, a, b))

    def give_inverse(k):
        cond = holders[k]
        goal = LOW if k < 2 else HIGH
        for i in range(3):
            at = (slice(i * order, (i + 1) * order), slice(0, (i + 1) * order))
            send(
                cond,
                lambda at=at: fac.at[at],
                lambda: aux.at[(k % 2,) + at],
                BULK_S + i,
                BULK_R + 3 * (k % 2) + i,
                (dp,) + goal,
            )

    def give_core0(cond, buf, k, ss, rs):
        send(cond, lambda: buf.at[k], lambda: buf.at[k], ss + k, rs + k, (dp - 1, r, c))

    @pl.when(first)
    def _():
        spread((3, 3), 3, first, pulled, P_S, P_R, [(3, 2), (3, 1), (3, 0)])

    load_cen.wait()

    @pl.when(solver)
    def _():
        for i, d in enumerate((2, 1, 3)):
            send(solver, lambda: cen.at[c], lambda: cen.at[c], CEN_S + i, CEN_R + c, (dp, r, lax.rem(c + d, 4)))

    def invert():
        b = [slice(k * order, (k + 1) * order) for k in range(3)]
        mul = functools.partial(dot, precision=HIGHEST)
        a0, a1, a2 = inv[0], inv[1], inv[2]
        x10 = -mul(a1, mul(fac[b[1], b[0]], a0))
        x21 = -mul(a2, mul(fac[b[2], b[1]], a1))
        x20 = -mul(a2, mul(fac[b[2], b[0]], a0) + mul(fac[b[2], b[1]], x10))
        for i, row in enumerate(((a0,), (x10, a1), (x20, x21, a2))):
            for j, v in enumerate(row):
                fac[b[i], b[j]] = v
                whi[b[i], b[j]], wlo[b[i], b[j]] = split2(v)

    @pl.when(diagonal & (r != 3))
    def _():
        load_inv.wait()
        load_fac.wait()
        invert()

    @pl.when(diagonal & (r == 0))
    def _():
        give_inverse(0)

    scale_col = jnp.zeros((rows.shape[0], 1), f32)
    place = lax.broadcasted_iota(jnp.int32, (rows.shape[0], 1), 0)
    for k in range(rows.shape[0]):
        scale_col = jnp.where(place == k, scales[k], scale_col)

    load_rows.wait()

    for i, d in enumerate((1, 3, 2)):
        src = lax.rem(c + d, 4)
        arrived(cen.at[src], CEN_R + src)

        @pl.when(solver)
        def _():
            send(solver, lambda src=src: cen.at[src], lambda src=src: cen.at[src], CENF_S + i, CEN_R + src, (dp - 1, r, c))

    def tiles():
        x = rows[...] / scale_col
        xh, xm, xl = split3(x)
        right = jnp.concatenate([xh, xm, xh, xl, xh, xm], axis=0)
        xn = -0.5 * jnp.sum(x * x, axis=0)[None, :]
        for k in range(4):
            for q in range(3):
                m = cen[k, :, q * order : (q + 1) * order] / scale_col
                mh, mm, ml = split3(m)
                left = jnp.concatenate([mh, mh, mm, mh, ml, mm], axis=0)
                mn = -0.5 * jnp.sum(m * m, axis=0)[:, None]
                v = jnp.exp(dot(left, right, TN) + mn + xn)
                at = slice(k * width + q * order, k * width + (q + 1) * order)
                khi[at, :], klo[at, :] = split2(v)

    @pl.when((r != 3) | (core == 0))
    def _():
        tiles()

    images = jnp.zeros((div.shape[0], span), f32)

    def place_of(x, y):
        chip = 4 * x + y
        q = jnp.int32(12)
        for k, (a, b) in enumerate(OWNERS):
            q = jnp.where(chip == 4 * a + b, k, q)
        return q

    for k in (3, 2, 1, 0):
        mine = solver & (r == k) & (c == k)

        if k < 3:

            @pl.when(mine)
            def _():
                t = div[:, k * width : (k + 1) * width]
                for j in range(3, k, -1):
                    arrived(prod_in.at[j], PROD_R + j)
                    t = t - prod_in[j]
                pulled[k] = lower(t, whi, wlo, order)
                spread((k, k), k, mine, pulled, P_S, P_R, [(k, j) for j in range(k - 1, -1, -1)])
                if k > 0:
                    give_inverse(k)

        @pl.when(jnp.logical_not(mine))
        def _():
            arrived(pulled.at[k], P_R + k)

        multiply = solver & (r == k) & (c < k)

        if k > 0:

            @pl.when(multiply)
            def _():
                prod_out[...] = product(pulled[k], whi[...], wlo[...])
                send(multiply, lambda: prod_out, lambda: prod_in.at[k], PROD_S, PROD_R + k, (dp, c, c))

        @pl.when(solver)
        def _():
            give_core0(solver, pulled, k, PF_S, P_R)

        if k == 3:

            @pl.when((r == 3) & solver)
            def _():
                tiles()

            @pl.when(first)
            def _():
                invert()
                give_inverse(3)

        at = slice(k * width, (k + 1) * width)
        images = images + product(pulled[k], khi[at, :], klo[at, :])

    both = jnp.concatenate(split2(images), axis=0)
    rhs = div.shape[0]
    for i, (a, b) in enumerate(offsets):
        x = lax.rem(r + a, 4)
        y = lax.rem(c + b, 4)
        chunk = place_of(x, y)
        owned = chunk < 12
        slot = 2 * i + core

        @pl.when(owned)
        def _():
            at = pl.ds(pl.multiple_of(chunk * order, order), order)
            out = dot(both, klo[at, :], NT) + dot(both, khi[at, :], NT)
            nsend[chunk] = out[rhs:] + out[:rhs]

        if i < 15:

            @pl.when(owned)
            def _():
                send(owned, lambda chunk=chunk: nsend.at[chunk], lambda: nred.at[slot], N_S + i, N_R, (2 * z + 1, x, y))

        else:

            @pl.when(owned & solver)
            def _():
                nred[31] = nsend[chunk]

            away = owned & (core == 0)

            @pl.when(away)
            def _():
                send(away, lambda chunk=chunk: nsend.at[chunk], lambda: nred.at[30], N_S + i, N_R, (2 * z + 1, x, y))

    place_here = place_of(r, c)
    owner = solver & (place_here < 12)
    at_low = solver & (r == LOW[0]) & (c == LOW[1])
    at_high = solver & (r == HIGH[0]) & (c == HIGH[1])

    if relay:

        @pl.when(solver)
        def _():
            pl.semaphore_wait(zready, len(relay))

    far = sorted(range(1, planes), key=lambda d: -ring_distance(d, planes))

    @pl.when(owner)
    def _():
        arrived(nred.at[0:31], N_R)
        total = nred[0]
        for s in range(1, 32):
            total = total + nred[s]
        zred[z] = total
        for i, d in enumerate(far):
            send(
                owner,
                lambda: zred.at[z],
                lambda: zred.at[z],
                Z_S + i,
                Z_R,
                (2 * lax.rem(z + d, planes) + 1, r, c),
            )

    @pl.when(at_low | at_high)
    def _():
        for k in range(2):
            for i in range(3):
                for j in range(i + 1):
                    si = slice(i * order, (i + 1) * order)
                    sj = slice(j * order, (j + 1) * order)
                    if j == 0:
                        at = (k, si, slice(0, (i + 1) * order))
                        arrived(aux.at[at], BULK_R + 3 * k + i)
                    dhi[k, sj, si], dlo[k, sj, si] = split2(aux[k, si, sj].T)

    @pl.when(owner)
    def _():
        arrived(zred.at[0 : planes - 1], Z_R)
        total = zred[0]
        for s in range(1, planes):
            total = total + zred[s]
        mout[...] = total * (1.0 / total_rows)

    passing = owner & jnp.logical_not(at_low | at_high)
    goal_low = place_here < 6
    part = jnp.where(goal_low, place_here, place_here - 6)

    @pl.when(passing)
    def _():
        goal = (dp, jnp.where(goal_low, LOW[0], HIGH[0]), jnp.where(goal_low, LOW[1], HIGH[1]))
        send(passing, lambda: mout, lambda: min_.at[part], M_S, M_R + part, goal)

    def normal(k):
        base = 3 * (k % 2)
        for j in range(base, base + 3):
            if j == 0:
                min_[0] = mout[...]
            else:
                arrived(min_.at[j], M_R + j)
        joined = jnp.concatenate([min_[base], min_[base + 1], min_[base + 2]], axis=1)
        return joined + ridge_weight * pulled[k]

    @pl.when(at_low)
    def _():
        img[0] = upper(normal(0), dhi.at[0], dlo.at[0], order)
        spread(LOW, 0, at_low, img, IMG_S, IMG_R, [(2, 0), (3, 0)], 0, 2)
        t = normal(1) - product(img[0], thi[...], tlo[...])
        img[1] = upper(t, dhi.at[1], dlo.at[1], order)
        spread(LOW, 1, at_low, img, IMG_S + 15, IMG_R, [(2, 1), (3, 1)], 0, 2)
        spread(LOW, 0, at_low, img, IMG_S, IMG_R, [(2, 0), (3, 0)], 2, 15)
        spread(LOW, 1, at_low, img, IMG_S + 15, IMG_R, [(2, 1), (3, 1)], 2, 15)

    for k in range(2):
        multiply = solver & (c == k) & (r >= 2)

        @pl.when(multiply)
        def _():
            arrived(img.at[k], IMG_R + k)
            back_out[...] = product(img[k], thi[...], tlo[...])
            at = 2 * (r - 2) + k
            send(multiply, lambda: back_out, lambda at=at: back_in.at[at], BACK_S, BACK_R + at, (dp,) + HIGH)

    @pl.when(at_high)
    def _():
        for k in (2, 3):
            t = normal(k)
            if k == 3:
                t = t - product(img[2], thi[...], tlo[...])
            for j in range(2):
                at = 2 * (k - 2) + j
                arrived(back_in.at[at], BACK_R + at)
                t = t - back_in[at]
            img[k] = upper(t, dhi.at[k - 2], dlo.at[k - 2], order)
            spread(HIGH, k, at_high, img, IMG_S + 15 * (k - 2), IMG_R, [])

    for k in range(4):
        known = at_low | (solver & (c == k) & (r >= 2)) if k < 2 else at_high

        @pl.when(jnp.logical_not(known))
        def _():
            arrived(img.at[k], IMG_R + k)

        @pl.when(solver)
        def _():
            give_core0(solver, img, k, IMGF_S, IMG_R)

    load_res.wait()
    gamma = jnp.sum(rev[...] * rev[...], axis=1, keepdims=True)
    segs = [slice(k * width, (k + 1) * width) for k in range(4)]
    curvature = jnp.zeros((rhs, 1), f32)
    for k in range(4):
        image[:, segs[k]] = img[k]
        curvature += jnp.sum(div[:, segs[k]] * img[k], axis=1, keepdims=True)
    alpha = gamma / curvature
    gamma_next = jnp.zeros((rhs, 1), f32)
    for k in range(4):
        res = rev[:, segs[k]] - alpha * img[k]
        gamma_next += jnp.sum(res * res, axis=1, keepdims=True)
    alphas[...] = jnp.broadcast_to(alpha, alphas.shape)
    betas[...] = jnp.broadcast_to(gamma_next / gamma, betas.shape)

    for cond, src, ss in pending:

        @pl.when(cond)
        def _():
            arrived(src(), ss)


def per_device(data, centres, scales, factor, block_inv, iterate, residual, direction):
    planes = lax.axis_size("dp") // 2
    total_rows = data.shape[1] * lax.axis_size("dp") * lax.axis_size("crow")
    inputs, width = centres.shape
    span = data.shape[1] // lax.axis_size("ccol")
    rhs, total = direction.shape
    order = block_inv.shape[1]
    whole = jax.ShapeDtypeStruct((rhs, total), f32)
    vmem = pltpu.VMEM
    hbm = pl.BlockSpec(memory_space=pl.ANY)
    square = (width, width)
    image, alphas, betas = pl.pallas_call(
        functools.partial(kernel, planes, total_rows),
        out_shape=(whole, whole, whole),
        in_specs=[hbm, hbm, pl.BlockSpec(memory_space=pltpu.SMEM)] + [hbm] * 4,
        out_specs=(pl.BlockSpec(memory_space=pltpu.VMEM),) * 3,
        scratch_shapes=[
            vmem(square, f32),
            vmem((3, order, order), f32),
            vmem(square, bf16),
            vmem(square, bf16),
            vmem(square, bf16),
            vmem(square, bf16),
            vmem((inputs, span), f32),
            vmem((4, inputs, width), f32),
            vmem((total, span), bf16),
            vmem((total, span), bf16),
            vmem((rhs, total), f32),
            vmem((rhs, total), f32),
            vmem((4, rhs, width), f32),
            vmem((rhs, width), f32),
            vmem((4, rhs, width), f32),
            vmem((12, rhs, order), f32),
            vmem((32, rhs, order), f32),
            vmem((planes, rhs, order), f32),
            vmem((rhs, order), f32),
            vmem((6, rhs, order), f32),
            vmem((4, rhs, width), f32),
            vmem((rhs, width), f32),
            vmem((4, rhs, width), f32),
            vmem((2,) + square, f32),
            vmem((2,) + square, bf16),
            vmem((2,) + square, bf16),
            pltpu.SemaphoreType.DMA((S.count,)),
            pltpu.SemaphoreType.REGULAR,
        ],
        compiler_params=pltpu.CompilerParams(
            collective_id=0, has_side_effects=True, vmem_limit_bytes=64 * 1024 * 1024 - 65536
        ),
    )(data, centres, scales, factor, block_inv, residual, direction)
    new_iterate = iterate + alphas * direction
    new_residual = residual - alphas * image
    new_direction = new_residual + betas * direction
    return new_iterate, new_residual, new_direction


def solution(mesh):
    placed = (
        P(None, ("dp", "crow")),
        P(None, "ccol"),
        P(),
        P("crow", "ccol"),
        P("crow", None, None),
        P(),
        P(),
        P(),
    )
    return jax.shard_map(
        per_device, mesh=mesh, in_specs=placed, out_specs=(P(), P(), P()), check_vma=False
    )
```

```python
import functools

import jax
import jax.numpy as jnp
from jax import lax
from jax.experimental import pallas as pl
from jax.experimental.pallas import tpu as pltpu
from jax.sharding import PartitionSpec as P

MESH = pl.DeviceIdType.MESH
f32 = jnp.float32
bf16 = jnp.bfloat16
HIGHEST = lax.Precision.HIGHEST
ridge_weight = 0.2

NN = (((1,), (0,)), ((), ()))
NT = (((1,), (1,)), ((), ()))
TN = (((0,), (0,)), ((), ()))


def dot(a, b, dims=NN, precision=None):
    return lax.dot_general(a, b, dims, precision=precision, preferred_element_type=f32)


def split2(v):
    high = v.astype(bf16)
    return high, (v - high.astype(f32)).astype(bf16)


def split3(v):
    high = v.astype(bf16)
    rest = v - high.astype(f32)
    mid = rest.astype(bf16)
    return high, mid, (rest - mid.astype(f32)).astype(bf16)


def product(v, high, low, dims=NN):
    rows = v.shape[0]
    both = jnp.concatenate(split2(v), axis=0)
    out = dot(both, low, dims) + dot(both, high, dims)
    return out[rows:] + out[:rows]


def lower(v, high, low, order):
    parts = [product(v[:, j:], high[j:, j : j + order], low[j:, j : j + order]) for j in range(0, v.shape[1], order)]
    return jnp.concatenate(parts, axis=1)


def upper(v, high, low, order):
    parts = []
    for j in range(0, v.shape[1], order):
        parts.append(product(v[:, : j + order], high[: j + order, j : j + order], low[: j + order, j : j + order]))
    return jnp.concatenate(parts, axis=1)


def ring_distance(d, n):
    d = d % n
    return min(d, n - d)


class Semaphores:
    def __init__(self):
        self.count = 0

    def take(self, n):
        first = self.count
        self.count += n
        return first


OWNERS = ((1, 0), (0, 0), (2, 0), (1, 1), (1, 3), (0, 1), (3, 2), (2, 2), (0, 2), (3, 3), (3, 1), (2, 3))
LOW = (1, 0)
HIGH = (3, 2)

S = Semaphores()
LOAD = S.take(8)
CEN_R = S.take(4)
CEN_S = S.take(3)
CENF_S = S.take(4)
P_R = S.take(4)
P_S = S.take(16)
PF_S = S.take(4)
PROD_R = S.take(4)
PROD_S = S.take(1)
N_R = S.take(1)
N_S = S.take(16)
Z_R = S.take(1)
Z_S = S.take(16)
M_R = S.take(6)
M_S = S.take(1)
IMG_R = S.take(4)
IMG_S = S.take(30)
IMGF_S = S.take(4)
BACK_R = S.take(4)
BACK_S = S.take(1)
BULK_R = S.take(6)
BULK_S = S.take(3)
LEAD_S = S.take(16)


def kernel(
    planes,
    total_rows,
    data,
    centres,
    scales,
    factor,
    block_inv,
    residual,
    direction,
    image,
    alphas,
    betas,
    fac,
    inv,
    whi,
    wlo,
    thi,
    tlo,
    rows,
    cen,
    khi,
    klo,
    rev,
    div,
    pulled,
    prod_out,
    prod_in,
    nsend,
    nred,
    zred,
    mout,
    min_,
    img,
    back_out,
    back_in,
    aux,
    dhi,
    dlo,
    sems,
    zready,
):
    dp = lax.axis_index("dp")
    r = lax.axis_index("crow")
    c = lax.axis_index("ccol")
    core = lax.rem(dp, 2)
    z = dp // 2
    solver = core == 1
    width = fac.shape[0]
    span = rows.shape[1]
    order = inv.shape[1]
    pending = []

    def local(src, dst, k):
        return pltpu.make_async_copy(src, dst, sems.at[LOAD + k])

    def remote(src, dst, ss, rs, dev):
        return pltpu.make_async_remote_copy(
            src_ref=src,
            dst_ref=dst,
            send_sem=sems.at[ss],
            recv_sem=sems.at[rs],
            device_id=dev,
            device_id_type=MESH,
        )

    def arrived(dst, rs):
        pltpu.make_async_copy(dst, dst, sems.at[rs]).wait()

    def send(cond, src, dst, ss, rs, dev):
        remote(src(), dst(), ss, rs, dev).start()
        pending.append((cond, src, ss))

    load_fac = local(factor, fac, 0)
    load_inv = local(block_inv, inv, 1)
    load_dir = local(direction, div, 2)
    load_cen = local(centres, cen.at[c], 3)
    load_rows = local(data.at[:, pl.ds(pl.multiple_of(c * span, 128), span)], rows, 4)
    load_res = local(residual, rev, 5)
    diagonal = solver & (r == c)
    below = solver & (r > c)
    at_low = solver & (r == LOW[0]) & (c == LOW[1])
    at_high = solver & (r == HIGH[0]) & (c == HIGH[1])
    lead = z == 0
    holders = [solver & (r == k) & (c == k) for k in range(4)]

    @pl.when(diagonal | at_low | at_high)
    def _():
        load_inv.start()

    load_dir.start()

    @pl.when(diagonal | below)
    def _():
        load_fac.start()

    load_cen.start()
    load_rows.start()
    load_res.start()

    barrier = pltpu.get_barrier_semaphore()
    far = sorted(range(1, planes), key=lambda d: -ring_distance(d, planes))
    offsets = sorted(
        [(a, b) for a in range(4) for b in range(4)],
        key=lambda o: (-ring_distance(o[0], 4) - ring_distance(o[1], 4), o),
    )

    def signal(sem, dev):
        pl.semaphore_signal(sem, inc=1, device_id=dev, device_id_type=MESH)

    @pl.when(solver)
    def _():
        for a, b in offsets[:-1]:
            signal(barrier, (dp, lax.rem(r + a, 4), lax.rem(c + b, 4)))
        for d in far:
            signal(barrier, (2 * lax.rem(z + d, planes), r, c))
        signal(barrier, (dp - 1, r, c))

    @pl.when(core == 0)
    def _():
        signal(barrier, (dp + 1, r, c))

    load_dir.wait()

    first = holders[3] & lead

    @pl.when(first)
    def _():
        load_inv.wait()
        load_fac.wait()
        b = [slice(k * order, (k + 1) * order) for k in range(3)]
        base = 3 * width
        d = [div[:, base + k * order : base + (k + 1) * order] for k in range(3)]
        p2 = dot(d[2], inv[2], NN, HIGHEST)
        p1 = dot(d[1] - dot(p2, fac[b[2], b[1]], NN, HIGHEST), inv[1], NN, HIGHEST)
        t0 = d[0] - dot(p2, fac[b[2], b[0]], NN, HIGHEST)
        p0 = dot(t0 - dot(p1, fac[b[1], b[0]], NN, HIGHEST), inv[0], NN, HIGHEST)
        pulled[3, :, b[0]] = p0
        pulled[3, :, b[1]] = p1
        pulled[3, :, b[2]] = p2

    def keep(v, i, j):
        si = slice(i * order, (i + 1) * order)
        sj = slice(j * order, (j + 1) * order)
        whi[si, sj], wlo[si, sj] = split2(v)
        thi[sj, si], tlo[sj, si] = split2(v.T)

    def invert():
        b = [slice(k * order, (k + 1) * order) for k in range(3)]
        mul = functools.partial(dot, precision=HIGHEST)
        a0, a1, a2 = inv[0], inv[1], inv[2]
        x10 = -mul(a1, mul(fac[b[1], b[0]], a0))
        x21 = -mul(a2, mul(fac[b[2], b[1]], a1))
        x20 = -mul(a2, mul(fac[b[2], b[0]], a0) + mul(fac[b[2], b[1]], x10))
        for i, row in enumerate(((a0,), (x10, a1), (x20, x21, a2))):
            for j, v in enumerate(row):
                fac[b[i], b[j]] = v
                whi[b[i], b[j]], wlo[b[i], b[j]] = split2(v)

    @pl.when(diagonal & jnp.logical_not(first))
    def _():
        load_inv.wait()
        load_fac.wait()
        invert()

    @pl.when(below)
    def _():
        load_fac.wait()
        for i in range(3):
            for j in range(3):
                keep(fac[i * order : (i + 1) * order, j * order : (j + 1) * order], i, j)

    @pl.when(solver)
    def _():
        pl.semaphore_wait(barrier, 16)

    @pl.when(core == 0)
    def _():
        pl.semaphore_wait(barrier, planes)
        signal(zready, (dp + 1, r, c))

    def spread(source, k, cond, buf, ss, rs, urgent, first=0, last=15):
        goals = [((source[0] + a) % 4, (source[1] + b) % 4) for a, b in offsets[:-1]]
        goals = urgent + [g for g in goals if g not in urgent]
        for i, (a, b) in enumerate(goals):
            if first <= i < last:
                send(cond, lambda: buf.at[k], lambda: buf.at[k], ss + i, rs + k, (dp, a, b))

    def give_inverse(k, cond):
        goal = LOW if k < 2 else HIGH
        for i in range(k % 2, 3):
            at = (slice(i * order, (i + 1) * order), slice(0, (i + 1 - k % 2) * order))
            send(
                cond,
                lambda at=at: fac.at[at],
                lambda: aux.at[(k % 2,) + at],
                BULK_S + i,
                BULK_R + 3 * (k % 2) + i,
                (dp,) + goal,
            )

    def give_core0(cond, buf, k, ss, rs):
        send(cond, lambda: buf.at[k], lambda: buf.at[k], ss + k, rs + k, (dp - 1, r, c))

    @pl.when(first)
    def _():
        spread((3, 3), 3, first, pulled, P_S, P_R, [(3, 2), (3, 1), (3, 0)])

    load_cen.wait()

    @pl.when(solver)
    def _():
        for i, d in enumerate((2, 1, 3)):
            send(solver, lambda: cen.at[c], lambda: cen.at[c], CEN_S + i, CEN_R + c, (dp, r, lax.rem(c + d, 4)))

    for k in range(4):
        early = holders[k] if k == 0 else holders[k] & jnp.logical_not(lead)

        @pl.when(early)
        def _():
            give_inverse(k, early)

    scale_col = jnp.zeros((rows.shape[0], 1), f32)
    place = lax.broadcasted_iota(jnp.int32, (rows.shape[0], 1), 0)
    for k in range(rows.shape[0]):
        scale_col = jnp.where(place == k, scales[k], scale_col)

    load_rows.wait()

    for i, d in enumerate((1, 3, 2)):
        src = lax.rem(c + d, 4)
        arrived(cen.at[src], CEN_R + src)

        @pl.when(solver)
        def _():
            send(solver, lambda src=src: cen.at[src], lambda src=src: cen.at[src], CENF_S + i, CEN_R + src, (dp - 1, r, c))

    def tiles():
        x = rows[...] / scale_col
        xh, xm, xl = split3(x)
        right = jnp.concatenate([xh, xm, xh, xl, xh, xm], axis=0)
        xn = -0.5 * jnp.sum(x * x, axis=0)[None, :]
        for k in range(4):
            for q in range(3):
                m = cen[k, :, q * order : (q + 1) * order] / scale_col
                mh, mm, ml = split3(m)
                left = jnp.concatenate([mh, mh, mm, mh, ml, mm], axis=0)
                mn = -0.5 * jnp.sum(m * m, axis=0)[:, None]
                v = jnp.exp(dot(left, right, TN) + mn + xn)
                at = slice(k * width + q * order, k * width + (q + 1) * order)
                khi[at, :], klo[at, :] = split2(v)

    late = solver & (r == 3) & lead

    @pl.when(jnp.logical_not(late))
    def _():
        tiles()

    images = jnp.zeros((div.shape[0], span), f32)

    def place_of(x, y):
        chip = 4 * x + y
        q = jnp.int32(12)
        for k, (a, b) in enumerate(OWNERS):
            q = jnp.where(chip == 4 * a + b, k, q)
        return q

    for k in (3, 2, 1, 0):
        mine = holders[k]
        leading = mine & lead
        led = mine & jnp.logical_not(lead)
        nearby = [(k, j) for j in range(k - 1, -1, -1)]

        if k < 3:

            @pl.when(leading)
            def _():
                t = div[:, k * width : (k + 1) * width]
                for j in range(3, k, -1):
                    arrived(prod_in.at[j], PROD_R + j)
                    t = t - prod_in[j]
                pulled[k] = lower(t, whi, wlo, order)
                spread((k, k), k, leading, pulled, P_S, P_R, nearby)
                if k > 0:
                    give_inverse(k, leading)

        @pl.when(led)
        def _():
            arrived(pulled.at[k], P_R + k)
            spread((k, k), k, led, pulled, P_S, P_R, [])

        @pl.when(jnp.logical_not(mine))
        def _():
            arrived(pulled.at[k], P_R + k)

        multiply = solver & lead & (r == k) & (c < k)

        if k > 0:

            @pl.when(multiply)
            def _():
                prod_out[...] = product(pulled[k], whi[...], wlo[...])
                send(multiply, lambda: prod_out, lambda: prod_in.at[k], PROD_S, PROD_R + k, (dp, c, c))

        @pl.when(solver)
        def _():
            give_core0(solver, pulled, k, PF_S, P_R)

        if k == 3:

            @pl.when(late)
            def _():
                tiles()

            @pl.when(first)
            def _():
                invert()
                give_inverse(3, first)

        @pl.when(leading)
        def _():
            pl.semaphore_wait(zready, 1)
            for i, d in enumerate(far):
                goal = (2 * lax.rem(z + d, planes) + 1, k, k)
                send(leading, lambda: pulled.at[k], lambda: pulled.at[k], LEAD_S + i, P_R + k, goal)

        at = slice(k * width, (k + 1) * width)
        images = images + product(pulled[k], khi[at, :], klo[at, :])

    both = jnp.concatenate(split2(images), axis=0)
    rhs = div.shape[0]
    for i, (a, b) in enumerate(offsets):
        x = lax.rem(r + a, 4)
        y = lax.rem(c + b, 4)
        chunk = place_of(x, y)
        owned = chunk < 12
        slot = 2 * i + core

        @pl.when(owned)
        def _():
            at = pl.ds(pl.multiple_of(chunk * order, order), order)
            out = dot(both, klo[at, :], NT) + dot(both, khi[at, :], NT)
            nsend[chunk] = out[rhs:] + out[:rhs]

        if i < 15:

            @pl.when(owned)
            def _():
                send(owned, lambda chunk=chunk: nsend.at[chunk], lambda: nred.at[slot], N_S + i, N_R, (2 * z + 1, x, y))

        else:

            @pl.when(owned & solver)
            def _():
                nred[31] = nsend[chunk]

            away = owned & (core == 0)

            @pl.when(away)
            def _():
                send(away, lambda chunk=chunk: nsend.at[chunk], lambda: nred.at[30], N_S + i, N_R, (2 * z + 1, x, y))

    place_here = place_of(r, c)
    owner = solver & (place_here < 12)

    @pl.when(solver & jnp.logical_not(diagonal & lead))
    def _():
        pl.semaphore_wait(zready, 1)

    @pl.when(owner)
    def _():
        arrived(nred.at[0:31], N_R)
        total = nred[0]
        for s in range(1, 32):
            total = total + nred[s]
        zred[z] = total
        for i, d in enumerate(far):
            send(
                owner,
                lambda: zred.at[z],
                lambda: zred.at[z],
                Z_S + i,
                Z_R,
                (2 * lax.rem(z + d, planes) + 1, r, c),
            )

    @pl.when(at_low | at_high)
    def _():
        load_inv.wait()
        for k in range(2):
            for i in range(3):
                for j in range(i + 1):
                    si = slice(i * order, (i + 1) * order)
                    sj = slice(j * order, (j + 1) * order)
                    if j == 0 and i >= k:
                        at = (k, si, slice(0, (i + 1 - k) * order))
                        arrived(aux.at[at], BULK_R + 3 * k + i)
                    block = inv[i] if i == j and k == 1 else aux[k, si, sj]
                    dhi[k, sj, si], dlo[k, sj, si] = split2(block.T)

    @pl.when(owner)
    def _():
        arrived(zred.at[0 : planes - 1], Z_R)
        total = zred[0]
        for s in range(1, planes):
            total = total + zred[s]
        mout[...] = total * (1.0 / total_rows)

    passing = owner & jnp.logical_not(at_low | at_high)
    goal_low = place_here < 6
    part = jnp.where(goal_low, place_here, place_here - 6)

    @pl.when(passing)
    def _():
        goal = (dp, jnp.where(goal_low, LOW[0], HIGH[0]), jnp.where(goal_low, LOW[1], HIGH[1]))
        send(passing, lambda: mout, lambda: min_.at[part], M_S, M_R + part, goal)

    def normal(k):
        base = 3 * (k % 2)
        for j in range(base, base + 3):
            if j == 0:
                min_[0] = mout[...]
            else:
                arrived(min_.at[j], M_R + j)
        joined = jnp.concatenate([min_[base], min_[base + 1], min_[base + 2]], axis=1)
        return joined + ridge_weight * pulled[k]

    @pl.when(at_low)
    def _():
        img[0] = upper(normal(0), dhi.at[0], dlo.at[0], order)
        spread(LOW, 0, at_low, img, IMG_S, IMG_R, [(2, 0), (3, 0)], 0, 2)
        t = normal(1) - product(img[0], thi[...], tlo[...])
        img[1] = upper(t, dhi.at[1], dlo.at[1], order)
        spread(LOW, 1, at_low, img, IMG_S + 15, IMG_R, [(2, 1), (3, 1)], 0, 2)
        spread(LOW, 0, at_low, img, IMG_S, IMG_R, [(2, 0), (3, 0)], 2, 15)
        spread(LOW, 1, at_low, img, IMG_S + 15, IMG_R, [(2, 1), (3, 1)], 2, 15)

    for k in range(2):
        multiply = solver & (c == k) & (r >= 2)

        @pl.when(multiply)
        def _():
            arrived(img.at[k], IMG_R + k)
            back_out[...] = product(img[k], thi[...], tlo[...])
            at = 2 * (r - 2) + k
            send(multiply, lambda: back_out, lambda at=at: back_in.at[at], BACK_S, BACK_R + at, (dp,) + HIGH)

    @pl.when(at_high)
    def _():
        for k in (2, 3):
            t = normal(k)
            if k == 3:
                t = t - product(img[2], thi[...], tlo[...])
            for j in range(2):
                at = 2 * (k - 2) + j
                arrived(back_in.at[at], BACK_R + at)
                t = t - back_in[at]
            img[k] = upper(t, dhi.at[k - 2], dlo.at[k - 2], order)
            spread(HIGH, k, at_high, img, IMG_S + 15 * (k - 2), IMG_R, [])

    for k in range(4):
        known = at_low | (solver & (c == k) & (r >= 2)) if k < 2 else at_high

        @pl.when(jnp.logical_not(known))
        def _():
            arrived(img.at[k], IMG_R + k)

        @pl.when(solver)
        def _():
            give_core0(solver, img, k, IMGF_S, IMG_R)

    load_res.wait()
    gamma = jnp.sum(rev[...] * rev[...], axis=1, keepdims=True)
    segs = [slice(k * width, (k + 1) * width) for k in range(4)]
    curvature = jnp.zeros((rhs, 1), f32)
    for k in range(4):
        image[:, segs[k]] = img[k]
        curvature += jnp.sum(div[:, segs[k]] * img[k], axis=1, keepdims=True)
    alpha = gamma / curvature
    gamma_next = jnp.zeros((rhs, 1), f32)
    for k in range(4):
        res = rev[:, segs[k]] - alpha * img[k]
        gamma_next += jnp.sum(res * res, axis=1, keepdims=True)
    alphas[...] = jnp.broadcast_to(alpha, alphas.shape)
    betas[...] = jnp.broadcast_to(gamma_next / gamma, betas.shape)

    for cond, src, ss in pending:

        @pl.when(cond)
        def _():
            arrived(src(), ss)


def per_device(data, centres, scales, factor, block_inv, iterate, residual, direction):
    planes = lax.axis_size("dp") // 2
    total_rows = data.shape[1] * lax.axis_size("dp") * lax.axis_size("crow")
    inputs, width = centres.shape
    span = data.shape[1] // lax.axis_size("ccol")
    rhs, total = direction.shape
    order = block_inv.shape[1]
    whole = jax.ShapeDtypeStruct((rhs, total), f32)
    vmem = pltpu.VMEM
    hbm = pl.BlockSpec(memory_space=pl.ANY)
    square = (width, width)
    image, alphas, betas = pl.pallas_call(
        functools.partial(kernel, planes, total_rows),
        out_shape=(whole, whole, whole),
        in_specs=[hbm, hbm, pl.BlockSpec(memory_space=pltpu.SMEM)] + [hbm] * 4,
        out_specs=(pl.BlockSpec(memory_space=pltpu.VMEM),) * 3,
        scratch_shapes=[
            vmem(square, f32),
            vmem((3, order, order), f32),
            vmem(square, bf16),
            vmem(square, bf16),
            vmem(square, bf16),
            vmem(square, bf16),
            vmem((inputs, span), f32),
            vmem((4, inputs, width), f32),
            vmem((total, span), bf16),
            vmem((total, span), bf16),
            vmem((rhs, total), f32),
            vmem((rhs, total), f32),
            vmem((4, rhs, width), f32),
            vmem((rhs, width), f32),
            vmem((4, rhs, width), f32),
            vmem((12, rhs, order), f32),
            vmem((32, rhs, order), f32),
            vmem((planes, rhs, order), f32),
            vmem((rhs, order), f32),
            vmem((6, rhs, order), f32),
            vmem((4, rhs, width), f32),
            vmem((rhs, width), f32),
            vmem((4, rhs, width), f32),
            vmem((2,) + square, f32),
            vmem((2,) + square, bf16),
            vmem((2,) + square, bf16),
            pltpu.SemaphoreType.DMA((S.count,)),
            pltpu.SemaphoreType.REGULAR,
        ],
        compiler_params=pltpu.CompilerParams(
            collective_id=0, has_side_effects=True, vmem_limit_bytes=64 * 1024 * 1024 - 65536
        ),
    )(data, centres, scales, factor, block_inv, residual, direction)
    new_iterate = iterate + alphas * direction
    new_residual = residual - alphas * image
    new_direction = new_residual + betas * direction
    return new_iterate, new_residual, new_direction


def solution(mesh):
    placed = (
        P(None, ("dp", "crow")),
        P(None, "ccol"),
        P(),
        P("crow", "ccol"),
        P("crow", None, None),
        P(),
        P(),
        P(),
    )
    return jax.shard_map(
        per_device, mesh=mesh, in_specs=placed, out_specs=(P(), P(), P()), check_vma=False
    )
```

```python
import functools

import jax
import jax.numpy as jnp
from jax import lax
from jax.experimental import pallas as pl
from jax.experimental.pallas import tpu as pltpu
from jax.sharding import PartitionSpec as P

MESH = pl.DeviceIdType.MESH
f32 = jnp.float32
bf16 = jnp.bfloat16
HIGHEST = lax.Precision.HIGHEST
ridge_weight = 0.2

NN = (((1,), (0,)), ((), ()))
NT = (((1,), (1,)), ((), ()))
TN = (((0,), (0,)), ((), ()))


def dot(a, b, dims=NN, precision=None):
    return lax.dot_general(a, b, dims, precision=precision, preferred_element_type=f32)


def split2(v):
    high = v.astype(bf16)
    return high, (v - high.astype(f32)).astype(bf16)


def split3(v):
    high = v.astype(bf16)
    rest = v - high.astype(f32)
    mid = rest.astype(bf16)
    return high, mid, (rest - mid.astype(f32)).astype(bf16)


def product(v, high, low, dims=NN):
    rows = v.shape[0]
    both = jnp.concatenate(split2(v), axis=0)
    out = dot(both, low, dims) + dot(both, high, dims)
    return out[rows:] + out[:rows]


def lower(v, high, low, order):
    parts = [product(v[:, j:], high[j:, j : j + order], low[j:, j : j + order]) for j in range(0, v.shape[1], order)]
    return jnp.concatenate(parts, axis=1)


def upper(v, high, low, order):
    parts = []
    for j in range(0, v.shape[1], order):
        parts.append(product(v[:, : j + order], high[: j + order, j : j + order], low[: j + order, j : j + order]))
    return jnp.concatenate(parts, axis=1)


def ring_distance(d, n):
    d = d % n
    return min(d, n - d)


class Semaphores:
    def __init__(self):
        self.count = 0

    def take(self, n):
        first = self.count
        self.count += n
        return first


OWNERS = ((1, 0), (0, 0), (2, 0), (1, 1), (1, 3), (0, 1), (3, 2), (2, 2), (0, 2), (3, 3), (3, 1), (2, 3))
PLACES = ((1, 0), (2, 0), (2, 1), (0, 0), (1, 1), (2, 2))
LOW = (1, 0)
HIGH = (3, 2)

S = Semaphores()
LOAD = S.take(8)
CEN_R = S.take(4)
CEN_S = S.take(3)
CENF_S = S.take(4)
P_R = S.take(4)
P_S = S.take(16)
PF_S = S.take(4)
PROD_R = S.take(4)
PROD_S = S.take(1)
N_R = S.take(1)
N_S = S.take(16)
Z_R = S.take(1)
Z_S = S.take(16)
M_R = S.take(6)
M_S = S.take(1)
IMG_R = S.take(4)
IMG_S = S.take(30)
IMGF_S = S.take(4)
BACK_R = S.take(4)
BACK_S = S.take(1)
BULK_R = S.take(2)
BULK_S = S.take(1)


def kernel(
    planes,
    total_rows,
    data,
    centres,
    scales,
    factor,
    block_inv,
    residual,
    direction,
    image,
    alphas,
    betas,
    fac,
    inv,
    whi,
    wlo,
    thi,
    tlo,
    rows,
    cen,
    khi,
    klo,
    rev,
    div,
    pulled,
    prod_out,
    prod_in,
    nsend,
    nred,
    zred,
    mout,
    min_,
    img,
    back_out,
    back_in,
    blocks,
    aux,
    dhi,
    dlo,
    sems,
    zready,
):
    dp = lax.axis_index("dp")
    r = lax.axis_index("crow")
    c = lax.axis_index("ccol")
    core = lax.rem(dp, 2)
    z = dp // 2
    solver = core == 1
    width = fac.shape[0]
    span = rows.shape[1]
    order = inv.shape[1]
    pending = []

    def local(src, dst, k):
        return pltpu.make_async_copy(src, dst, sems.at[LOAD + k])

    def remote(src, dst, ss, rs, dev):
        return pltpu.make_async_remote_copy(
            src_ref=src,
            dst_ref=dst,
            send_sem=sems.at[ss],
            recv_sem=sems.at[rs],
            device_id=dev,
            device_id_type=MESH,
        )

    def arrived(dst, rs):
        pltpu.make_async_copy(dst, dst, sems.at[rs]).wait()

    def send(cond, src, dst, ss, rs, dev):
        remote(src(), dst(), ss, rs, dev).start()
        pending.append((cond, src, ss))

    def flush():
        groups = {}
        for cond, src, ss in pending:
            groups.setdefault(id(cond), (cond, []))[1].append((src, ss))
        pending.clear()
        for cond, sends in groups.values():

            @pl.when(cond)
            def _():
                for src, ss in sends:
                    arrived(src(), ss)

    load_fac = local(factor, fac, 0)
    load_inv = local(block_inv, inv, 1)
    load_dir = local(direction, div, 2)
    load_cen = local(centres, cen.at[c], 3)
    load_rows = local(data.at[:, pl.ds(pl.multiple_of(c * span, 128), span)], rows, 4)
    load_res = local(residual, rev, 5)
    diagonal = solver & (r == c)
    below = solver & (r > c)
    at_low = solver & (r == LOW[0]) & (c == LOW[1])
    at_high = solver & (r == HIGH[0]) & (c == HIGH[1])
    holders = [solver & (r == k) & (c == k) for k in range(4)]

    @pl.when(diagonal | at_low | at_high)
    def _():
        load_inv.start()

    load_dir.start()

    @pl.when(diagonal | below)
    def _():
        load_fac.start()

    load_cen.start()
    load_rows.start()
    load_res.start()

    barrier = pltpu.get_barrier_semaphore()
    far = sorted(range(1, planes), key=lambda d: -ring_distance(d, planes))
    offsets = sorted(
        [(a, b) for a in range(4) for b in range(4)],
        key=lambda o: (-ring_distance(o[0], 4) - ring_distance(o[1], 4), o),
    )

    def signal(sem, dev):
        pl.semaphore_signal(sem, inc=1, device_id=dev, device_id_type=MESH)

    @pl.when(solver)
    def _():
        for a, b in offsets[:-1]:
            signal(barrier, (dp, lax.rem(r + a, 4), lax.rem(c + b, 4)))
        for d in far:
            signal(barrier, (2 * lax.rem(z + d, planes), r, c))
        signal(barrier, (dp - 1, r, c))

    @pl.when(core == 0)
    def _():
        signal(barrier, (dp + 1, r, c))

    load_dir.wait()

    first = holders[3]

    @pl.when(first)
    def _():
        load_inv.wait()
        load_fac.wait()
        b = [slice(k * order, (k + 1) * order) for k in range(3)]
        base = 3 * width
        d = [div[:, base + k * order : base + (k + 1) * order] for k in range(3)]
        p2 = dot(d[2], inv[2], NN, HIGHEST)
        p1 = dot(d[1] - dot(p2, fac[b[2], b[1]], NN, HIGHEST), inv[1], NN, HIGHEST)
        t0 = d[0] - dot(p2, fac[b[2], b[0]], NN, HIGHEST)
        p0 = dot(t0 - dot(p1, fac[b[1], b[0]], NN, HIGHEST), inv[0], NN, HIGHEST)
        pulled[3, :, b[0]] = p0
        pulled[3, :, b[1]] = p1
        pulled[3, :, b[2]] = p2

    def keep(v, i, j):
        si = slice(i * order, (i + 1) * order)
        sj = slice(j * order, (j + 1) * order)
        whi[si, sj], wlo[si, sj] = split2(v)
        thi[sj, si], tlo[sj, si] = split2(v.T)

    def invert():
        b = [slice(k * order, (k + 1) * order) for k in range(3)]
        mul = functools.partial(dot, precision=HIGHEST)
        a0, a1, a2 = inv[0], inv[1], inv[2]
        x10 = -mul(a1, mul(fac[b[1], b[0]], a0))
        x21 = -mul(a2, mul(fac[b[2], b[1]], a1))
        x20 = -mul(a2, mul(fac[b[2], b[0]], a0) + mul(fac[b[2], b[1]], x10))
        for i, row in enumerate(((a0,), (x10, a1), (x20, x21, a2))):
            for j, v in enumerate(row):
                blocks[PLACES.index((i, j))] = v
                whi[b[i], b[j]], wlo[b[i], b[j]] = split2(v)

    @pl.when(diagonal & jnp.logical_not(first))
    def _():
        load_inv.wait()
        load_fac.wait()
        invert()

    @pl.when(below)
    def _():
        load_fac.wait()
        for i in range(3):
            for j in range(3):
                keep(fac[i * order : (i + 1) * order, j * order : (j + 1) * order], i, j)

    @pl.when(solver)
    def _():
        pl.semaphore_wait(barrier, 16)

    @pl.when(core == 0)
    def _():
        pl.semaphore_wait(barrier, planes)
        signal(zready, (dp + 1, r, c))

    def spread(source, k, cond, buf, ss, rs, urgent, first=0, last=15):
        goals = [((source[0] + a) % 4, (source[1] + b) % 4) for a, b in offsets[:-1]]
        goals = urgent + [g for g in goals if g not in urgent]
        for i, (a, b) in enumerate(goals):
            if first <= i < last:
                send(cond, lambda: buf.at[k], lambda: buf.at[k], ss + i, rs + k, (dp, a, b))

    def give_inverse(k, cond):
        goal = LOW if k < 2 else HIGH
        n = 6 - 3 * (k % 2)
        src = lambda: blocks.at[0:n]
        send(cond, src, lambda: aux.at[k % 2, 0:n], BULK_S, BULK_R + k % 2, (dp,) + goal)

    def give_core0(cond, buf, k, ss, rs):
        send(cond, lambda: buf.at[k], lambda: buf.at[k], ss + k, rs + k, (dp - 1, r, c))

    @pl.when(first)
    def _():
        spread((3, 3), 3, first, pulled, P_S, P_R, [(3, 2), (3, 1), (3, 0)])

    load_cen.wait()

    @pl.when(solver)
    def _():
        for i, d in enumerate((2, 1, 3)):
            send(solver, lambda: cen.at[c], lambda: cen.at[c], CEN_S + i, CEN_R + c, (dp, r, lax.rem(c + d, 4)))

    for k in (0, 2):

        @pl.when(holders[k])
        def _():
            give_inverse(k, holders[k])

    scale_col = jnp.zeros((rows.shape[0], 1), f32)
    place = lax.broadcasted_iota(jnp.int32, (rows.shape[0], 1), 0)
    for k in range(rows.shape[0]):
        scale_col = jnp.where(place == k, scales[k], scale_col)

    load_rows.wait()

    for i, d in enumerate((1, 3, 2)):
        src = lax.rem(c + d, 4)
        arrived(cen.at[src], CEN_R + src)

        @pl.when(solver)
        def _():
            send(solver, lambda src=src: cen.at[src], lambda src=src: cen.at[src], CENF_S + i, CEN_R + src, (dp - 1, r, c))

    def tiles():
        x = rows[...] / scale_col
        xh, xm, xl = split3(x)
        right = jnp.concatenate([xh, xm, xh, xl, xh, xm], axis=0)
        xn = -0.5 * jnp.sum(x * x, axis=0)[None, :]
        for k in range(4):
            for q in range(3):
                m = cen[k, :, q * order : (q + 1) * order] / scale_col
                mh, mm, ml = split3(m)
                left = jnp.concatenate([mh, mh, mm, mh, ml, mm], axis=0)
                mn = -0.5 * jnp.sum(m * m, axis=0)[:, None]
                v = jnp.exp(dot(left, right, TN) + mn + xn)
                at = slice(k * width + q * order, k * width + (q + 1) * order)
                khi[at, :], klo[at, :] = split2(v)

    late = solver & (r == 3)

    @pl.when(jnp.logical_not(late))
    def _():
        tiles()

    images = jnp.zeros((div.shape[0], span), f32)

    def place_of(x, y):
        chip = 4 * x + y
        q = jnp.int32(12)
        for k, (a, b) in enumerate(OWNERS):
            q = jnp.where(chip == 4 * a + b, k, q)
        return q

    for k in (3, 2, 1, 0):
        mine = holders[k]
        nearby = [(k, j) for j in range(k - 1, -1, -1)]

        if k < 3:

            @pl.when(mine)
            def _():
                t = div[:, k * width : (k + 1) * width]
                for j in range(3, k, -1):
                    arrived(prod_in.at[j], PROD_R + j)
                    t = t - prod_in[j]
                pulled[k] = lower(t, whi, wlo, order)
                spread((k, k), k, mine, pulled, P_S, P_R, nearby)
                if k == 1:
                    give_inverse(k, mine)

        @pl.when(jnp.logical_not(mine))
        def _():
            arrived(pulled.at[k], P_R + k)

        multiply = solver & (r == k) & (c < k)

        if k > 0:

            @pl.when(multiply)
            def _():
                prod_out[...] = product(pulled[k], whi[...], wlo[...])
                send(multiply, lambda: prod_out, lambda: prod_in.at[k], PROD_S, PROD_R + k, (dp, c, c))

        @pl.when(solver)
        def _():
            give_core0(solver, pulled, k, PF_S, P_R)

        if k == 3:

            @pl.when(late)
            def _():
                tiles()

            @pl.when(first)
            def _():
                invert()
                give_inverse(3, first)

        at = slice(k * width, (k + 1) * width)
        images = images + product(pulled[k], khi[at, :], klo[at, :])

    both = jnp.concatenate(split2(images), axis=0)
    rhs = div.shape[0]
    for i, (a, b) in enumerate(offsets):
        x = lax.rem(r + a, 4)
        y = lax.rem(c + b, 4)
        chunk = place_of(x, y)
        owned = chunk < 12
        slot = 2 * i + core

        @pl.when(owned)
        def _():
            at = pl.ds(pl.multiple_of(chunk * order, order), order)
            out = dot(both, klo[at, :], NT) + dot(both, khi[at, :], NT)
            nsend[chunk] = out[rhs:] + out[:rhs]

        if i < 15:

            @pl.when(owned)
            def _():
                send(owned, lambda chunk=chunk: nsend.at[chunk], lambda: nred.at[slot], N_S + i, N_R, (2 * z + 1, x, y))

        else:

            @pl.when(owned & solver)
            def _():
                nred[31] = nsend[chunk]

            away = owned & (core == 0)

            @pl.when(away)
            def _():
                send(away, lambda chunk=chunk: nsend.at[chunk], lambda: nred.at[30], N_S + i, N_R, (2 * z + 1, x, y))

    place_here = place_of(r, c)
    owner = solver & (place_here < 12)

    @pl.when(solver)
    def _():
        pl.semaphore_wait(zready, 1)

    @pl.when(owner)
    def _():
        arrived(nred.at[0:31], N_R)
        total = nred[0]
        for s in range(1, 32):
            total = total + nred[s]
        zred[z] = total
        for i, d in enumerate(far):
            send(
                owner,
                lambda: zred.at[z],
                lambda: zred.at[z],
                Z_S + i,
                Z_R,
                (2 * lax.rem(z + d, planes) + 1, r, c),
            )

    @pl.when(at_low | at_high)
    def _():
        load_inv.wait()
        for k in range(2):
            arrived(aux.at[k, 0 : 6 - 3 * k], BULK_R + k)
            for n, (i, j) in enumerate(PLACES):
                si = slice(i * order, (i + 1) * order)
                sj = slice(j * order, (j + 1) * order)
                block = inv[i] if i == j and k == 1 else aux[k, n]
                dhi[k, sj, si], dlo[k, sj, si] = split2(block.T)

    flush()

    @pl.when(owner)
    def _():
        arrived(zred.at[0 : planes - 1], Z_R)
        total = zred[0]
        for s in range(1, planes):
            total = total + zred[s]
        mout[...] = total * (1.0 / total_rows)

    passing = owner & jnp.logical_not(at_low | at_high)
    goal_low = place_here < 6
    part = jnp.where(goal_low, place_here, place_here - 6)

    @pl.when(passing)
    def _():
        goal = (dp, jnp.where(goal_low, LOW[0], HIGH[0]), jnp.where(goal_low, LOW[1], HIGH[1]))
        send(passing, lambda: mout, lambda: min_.at[part], M_S, M_R + part, goal)

    def normal(k):
        base = 3 * (k % 2)
        for j in range(base, base + 3):
            if j == 0:
                min_[0] = mout[...]
            else:
                arrived(min_.at[j], M_R + j)
        joined = jnp.concatenate([min_[base], min_[base + 1], min_[base + 2]], axis=1)
        return joined + ridge_weight * pulled[k]

    @pl.when(at_low)
    def _():
        img[0] = upper(normal(0), dhi.at[0], dlo.at[0], order)
        spread(LOW, 0, at_low, img, IMG_S, IMG_R, [(2, 0), (3, 0)], 0, 2)
        t = normal(1) - product(img[0], thi[...], tlo[...])
        img[1] = upper(t, dhi.at[1], dlo.at[1], order)
        spread(LOW, 1, at_low, img, IMG_S + 15, IMG_R, [(2, 1), (3, 1)], 0, 2)
        spread(LOW, 0, at_low, img, IMG_S, IMG_R, [(2, 0), (3, 0)], 2, 15)
        spread(LOW, 1, at_low, img, IMG_S + 15, IMG_R, [(2, 1), (3, 1)], 2, 15)

    for k in range(2):
        multiply = solver & (c == k) & (r >= 2)

        @pl.when(multiply)
        def _():
            arrived(img.at[k], IMG_R + k)
            back_out[...] = product(img[k], thi[...], tlo[...])
            at = 2 * (r - 2) + k
            send(multiply, lambda: back_out, lambda at=at: back_in.at[at], BACK_S, BACK_R + at, (dp,) + HIGH)

    @pl.when(at_high)
    def _():
        for k in (2, 3):
            t = normal(k)
            if k == 3:
                t = t - product(img[2], thi[...], tlo[...])
            for j in range(2):
                at = 2 * (k - 2) + j
                arrived(back_in.at[at], BACK_R + at)
                t = t - back_in[at]
            img[k] = upper(t, dhi.at[k - 2], dlo.at[k - 2], order)
            spread(HIGH, k, at_high, img, IMG_S + 15 * (k - 2), IMG_R, [])

    for k in range(4):
        known = at_low | (solver & (c == k) & (r >= 2)) if k < 2 else at_high

        @pl.when(jnp.logical_not(known))
        def _():
            arrived(img.at[k], IMG_R + k)

        @pl.when(solver)
        def _():
            give_core0(solver, img, k, IMGF_S, IMG_R)

    load_res.wait()
    gamma = jnp.sum(rev[...] * rev[...], axis=1, keepdims=True)
    segs = [slice(k * width, (k + 1) * width) for k in range(4)]
    curvature = jnp.zeros((rhs, 1), f32)
    for k in range(4):
        image[:, segs[k]] = img[k]
        curvature += jnp.sum(div[:, segs[k]] * img[k], axis=1, keepdims=True)
    alpha = gamma / curvature
    gamma_next = jnp.zeros((rhs, 1), f32)
    for k in range(4):
        res = rev[:, segs[k]] - alpha * img[k]
        gamma_next += jnp.sum(res * res, axis=1, keepdims=True)
    alphas[...] = jnp.broadcast_to(alpha, alphas.shape)
    betas[...] = jnp.broadcast_to(gamma_next / gamma, betas.shape)

    flush()


def per_device(data, centres, scales, factor, block_inv, iterate, residual, direction):
    planes = lax.axis_size("dp") // 2
    total_rows = data.shape[1] * lax.axis_size("dp") * lax.axis_size("crow")
    inputs, width = centres.shape
    span = data.shape[1] // lax.axis_size("ccol")
    rhs, total = direction.shape
    order = block_inv.shape[1]
    whole = jax.ShapeDtypeStruct((rhs, total), f32)
    vmem = pltpu.VMEM
    hbm = pl.BlockSpec(memory_space=pl.ANY)
    square = (width, width)
    image, alphas, betas = pl.pallas_call(
        functools.partial(kernel, planes, total_rows),
        out_shape=(whole, whole, whole),
        in_specs=[hbm, hbm, pl.BlockSpec(memory_space=pltpu.SMEM)] + [hbm] * 4,
        out_specs=(pl.BlockSpec(memory_space=pltpu.VMEM),) * 3,
        scratch_shapes=[
            vmem(square, f32),
            vmem((3, order, order), f32),
            vmem(square, bf16),
            vmem(square, bf16),
            vmem(square, bf16),
            vmem(square, bf16),
            vmem((inputs, span), f32),
            vmem((4, inputs, width), f32),
            vmem((total, span), bf16),
            vmem((total, span), bf16),
            vmem((rhs, total), f32),
            vmem((rhs, total), f32),
            vmem((4, rhs, width), f32),
            vmem((rhs, width), f32),
            vmem((4, rhs, width), f32),
            vmem((12, rhs, order), f32),
            vmem((32, rhs, order), f32),
            vmem((planes, rhs, order), f32),
            vmem((rhs, order), f32),
            vmem((6, rhs, order), f32),
            vmem((4, rhs, width), f32),
            vmem((rhs, width), f32),
            vmem((4, rhs, width), f32),
            vmem((6, order, order), f32),
            vmem((2, 6, order, order), f32),
            vmem((2,) + square, bf16),
            vmem((2,) + square, bf16),
            pltpu.SemaphoreType.DMA((S.count,)),
            pltpu.SemaphoreType.REGULAR,
        ],
        compiler_params=pltpu.CompilerParams(
            collective_id=0, has_side_effects=True, vmem_limit_bytes=64 * 1024 * 1024 - 65536
        ),
    )(data, centres, scales, factor, block_inv, residual, direction)
    new_iterate = iterate + alphas * direction
    new_residual = residual - alphas * image
    new_direction = new_residual + betas * direction
    return new_iterate, new_residual, new_direction


def solution(mesh):
    placed = (
        P(None, ("dp", "crow")),
        P(None, "ccol"),
        P(),
        P("crow", "ccol"),
        P("crow", None, None),
        P(),
        P(),
        P(),
    )
    return jax.shard_map(
        per_device, mesh=mesh, in_specs=placed, out_specs=(P(), P(), P()), check_vma=False
    )
```

```python
import functools

import jax
import jax.numpy as jnp
from jax import lax
from jax.experimental import pallas as pl
from jax.experimental.pallas import tpu as pltpu
from jax.sharding import PartitionSpec as P

MESH = pl.DeviceIdType.MESH
f32 = jnp.float32
bf16 = jnp.bfloat16
HIGHEST = lax.Precision.HIGHEST
ridge_weight = 0.2

NN = (((1,), (0,)), ((), ()))
NT = (((1,), (1,)), ((), ()))
TN = (((0,), (0,)), ((), ()))


def dot(a, b, dims=NN, precision=None):
    return lax.dot_general(a, b, dims, precision=precision, preferred_element_type=f32)


def split2(v):
    high = v.astype(bf16)
    return high, (v - high.astype(f32)).astype(bf16)


def split3(v):
    high = v.astype(bf16)
    rest = v - high.astype(f32)
    mid = rest.astype(bf16)
    return high, mid, (rest - mid.astype(f32)).astype(bf16)


def product(v, high, low, dims=NN):
    rows = v.shape[0]
    both = jnp.concatenate(split2(v), axis=0)
    out = dot(both, low, dims) + dot(both, high, dims)
    return out[rows:] + out[:rows]


def lower(v, high, low, order):
    parts = [product(v[:, j:], high[j:, j : j + order], low[j:, j : j + order]) for j in range(0, v.shape[1], order)]
    return jnp.concatenate(parts, axis=1)


def upper(v, high, low, order):
    parts = []
    for j in range(0, v.shape[1], order):
        parts.append(product(v[:, : j + order], high[: j + order, j : j + order], low[: j + order, j : j + order]))
    return jnp.concatenate(parts, axis=1)


def ring_distance(d, n):
    d = d % n
    return min(d, n - d)


class Semaphores:
    def __init__(self):
        self.count = 0

    def take(self, n):
        first = self.count
        self.count += n
        return first


OWNERS = ((1, 0), (0, 0), (2, 0), (1, 1), (1, 3), (0, 1), (3, 2), (2, 2), (0, 2), (3, 3), (3, 1), (2, 3))
PLACES = ((1, 0), (2, 0), (2, 1), (0, 0), (1, 1), (2, 2))
LOW = (1, 0)
HIGH = (3, 2)

S = Semaphores()
LOAD = S.take(8)
CEN_R = S.take(4)
CEN_S = S.take(3)
CENF_S = S.take(4)
P_R = S.take(4)
P_S = S.take(16)
PF_S = S.take(4)
PROD_R = S.take(4)
PROD_S = S.take(1)
N_R = S.take(1)
N_S = S.take(16)
Z_R = S.take(1)
Z_S = S.take(16)
M_R = S.take(6)
M_S = S.take(1)
IMG_R = S.take(4)
IMG_S = S.take(30)
IMGF_S = S.take(4)
BACK_R = S.take(4)
BACK_S = S.take(1)
BULK_R = S.take(2)
BULK_S = S.take(1)


def kernel(
    planes,
    total_rows,
    data,
    centres,
    scales,
    factor,
    block_inv,
    residual,
    direction,
    image,
    alphas,
    betas,
    fac,
    inv,
    whi,
    wlo,
    thi,
    tlo,
    rows,
    cen,
    khi,
    klo,
    rev,
    div,
    pulled,
    prod_out,
    prod_in,
    nsend,
    nred,
    zred,
    mout,
    min_,
    img,
    back_out,
    back_in,
    blocks,
    aux,
    dhi,
    dlo,
    sems,
    zready,
):
    dp = lax.axis_index("dp")
    r = lax.axis_index("crow")
    c = lax.axis_index("ccol")
    core = lax.rem(dp, 2)
    z = dp // 2
    solver = core == 1
    width = fac.shape[0]
    span = rows.shape[1]
    order = inv.shape[1]
    pending = []

    def local(src, dst, k):
        return pltpu.make_async_copy(src, dst, sems.at[LOAD + k])

    def remote(src, dst, ss, rs, dev):
        return pltpu.make_async_remote_copy(
            src_ref=src,
            dst_ref=dst,
            send_sem=sems.at[ss],
            recv_sem=sems.at[rs],
            device_id=dev,
            device_id_type=MESH,
        )

    def arrived(dst, rs):
        pltpu.make_async_copy(dst, dst, sems.at[rs]).wait()

    def send(cond, src, dst, ss, rs, dev):
        remote(src(), dst(), ss, rs, dev).start()
        pending.append((cond, src, ss))

    def flush():
        groups = {}
        for cond, src, ss in pending:
            groups.setdefault(id(cond), (cond, []))[1].append((src, ss))
        pending.clear()
        for cond, sends in groups.values():

            @pl.when(cond)
            def _():
                for src, ss in sends:
                    arrived(src(), ss)

    load_fac = local(factor, fac, 0)
    load_inv = local(block_inv, inv, 1)
    load_dir = local(direction, div, 2)
    load_cen = local(centres, cen.at[c], 3)
    load_rows = local(data.at[:, pl.ds(pl.multiple_of(c * span, 128), span)], rows, 4)
    load_res = local(residual, rev, 5)
    diagonal = solver & (r == c)
    below = solver & (r > c)
    at_low = solver & (r == LOW[0]) & (c == LOW[1])
    at_high = solver & (r == HIGH[0]) & (c == HIGH[1])
    helpers = [(core == 0) & (r == k) & (c == k) for k in range(4)]
    holders = [solver & (r == k) & (c == k) for k in range(4)]

    @pl.when((r == c) | at_low | at_high)
    def _():
        load_inv.start()

    load_dir.start()

    @pl.when((r == c) | below)
    def _():
        load_fac.start()

    load_cen.start()
    load_rows.start()
    load_res.start()

    barrier = pltpu.get_barrier_semaphore()
    far = sorted(range(1, planes), key=lambda d: -ring_distance(d, planes))
    offsets = sorted(
        [(a, b) for a in range(4) for b in range(4)],
        key=lambda o: (-ring_distance(o[0], 4) - ring_distance(o[1], 4), o),
    )

    def signal(sem, dev):
        pl.semaphore_signal(sem, inc=1, device_id=dev, device_id_type=MESH)

    @pl.when(solver)
    def _():
        for a, b in offsets[:-1]:
            signal(barrier, (dp, lax.rem(r + a, 4), lax.rem(c + b, 4)))
        for d in far:
            signal(barrier, (2 * lax.rem(z + d, planes), r, c))
        signal(barrier, (dp - 1, r, c))

    for here, users in ((at_low, (0, 1)), (at_high, (2, 3))):

        @pl.when(here)
        def _():
            for k in users:
                signal(barrier, (dp - 1, k, k))

    @pl.when(core == 0)
    def _():
        signal(barrier, (dp + 1, r, c))

    load_dir.wait()

    first = holders[3]

    @pl.when(first)
    def _():
        load_inv.wait()
        load_fac.wait()
        b = [slice(k * order, (k + 1) * order) for k in range(3)]
        base = 3 * width
        d = [div[:, base + k * order : base + (k + 1) * order] for k in range(3)]
        p2 = dot(d[2], inv[2], NN, HIGHEST)
        p1 = dot(d[1] - dot(p2, fac[b[2], b[1]], NN, HIGHEST), inv[1], NN, HIGHEST)
        t0 = d[0] - dot(p2, fac[b[2], b[0]], NN, HIGHEST)
        p0 = dot(t0 - dot(p1, fac[b[1], b[0]], NN, HIGHEST), inv[0], NN, HIGHEST)
        pulled[3, :, b[0]] = p0
        pulled[3, :, b[1]] = p1
        pulled[3, :, b[2]] = p2

    def keep(v, i, j):
        si = slice(i * order, (i + 1) * order)
        sj = slice(j * order, (j + 1) * order)
        whi[si, sj], wlo[si, sj] = split2(v)
        thi[sj, si], tlo[sj, si] = split2(v.T)

    def invert():
        b = [slice(k * order, (k + 1) * order) for k in range(3)]
        mul = functools.partial(dot, precision=HIGHEST)
        a0, a1, a2 = inv[0], inv[1], inv[2]
        x10 = -mul(a1, mul(fac[b[1], b[0]], a0))
        x21 = -mul(a2, mul(fac[b[2], b[1]], a1))
        x20 = -mul(a2, mul(fac[b[2], b[0]], a0) + mul(fac[b[2], b[1]], x10))
        for i, row in enumerate(((a0,), (x10, a1), (x20, x21, a2))):
            for j, v in enumerate(row):
                blocks[PLACES.index((i, j))] = v
                whi[b[i], b[j]], wlo[b[i], b[j]] = split2(v)

    @pl.when((r == c) & jnp.logical_not(first))
    def _():
        load_inv.wait()
        load_fac.wait()
        invert()

    @pl.when(below)
    def _():
        load_fac.wait()
        for i in range(3):
            for j in range(3):
                keep(fac[i * order : (i + 1) * order, j * order : (j + 1) * order], i, j)

    @pl.when(solver)
    def _():
        pl.semaphore_wait(barrier, 16)

    @pl.when(core == 0)
    def _():
        pl.semaphore_wait(barrier, planes + jnp.where(r == c, 1, 0))
        signal(zready, (dp + 1, r, c))

    def spread(source, k, cond, buf, ss, rs, urgent, first=0, last=15):
        goals = [((source[0] + a) % 4, (source[1] + b) % 4) for a, b in offsets[:-1]]
        goals = urgent + [g for g in goals if g not in urgent]
        for i, (a, b) in enumerate(goals):
            if first <= i < last:
                send(cond, lambda: buf.at[k], lambda: buf.at[k], ss + i, rs + k, (dp, a, b))

    def give_inverse(k, cond):
        goal = LOW if k < 2 else HIGH
        n = 6 - 3 * (k % 2)
        src = lambda: blocks.at[0:n]
        send(cond, src, lambda: aux.at[k % 2, 0:n], BULK_S, BULK_R + k % 2, (dp + 1,) + goal)

    def give_core0(cond, buf, k, ss, rs):
        send(cond, lambda: buf.at[k], lambda: buf.at[k], ss + k, rs + k, (dp - 1, r, c))

    @pl.when(first)
    def _():
        spread((3, 3), 3, first, pulled, P_S, P_R, [(3, 2), (3, 1), (3, 0)])

    load_cen.wait()

    @pl.when(solver)
    def _():
        for i, d in enumerate((2, 1, 3)):
            send(solver, lambda: cen.at[c], lambda: cen.at[c], CEN_S + i, CEN_R + c, (dp, r, lax.rem(c + d, 4)))

    for k in range(4):

        @pl.when(helpers[k])
        def _():
            give_inverse(k, helpers[k])

    scale_col = jnp.zeros((rows.shape[0], 1), f32)
    place = lax.broadcasted_iota(jnp.int32, (rows.shape[0], 1), 0)
    for k in range(rows.shape[0]):
        scale_col = jnp.where(place == k, scales[k], scale_col)

    load_rows.wait()

    for i, d in enumerate((1, 3, 2)):
        src = lax.rem(c + d, 4)
        arrived(cen.at[src], CEN_R + src)

        @pl.when(solver)
        def _():
            send(solver, lambda src=src: cen.at[src], lambda src=src: cen.at[src], CENF_S + i, CEN_R + src, (dp - 1, r, c))

    def tiles():
        x = rows[...] / scale_col
        xh, xm, xl = split3(x)
        right = jnp.concatenate([xh, xm, xh, xl, xh, xm], axis=0)
        xn = -0.5 * jnp.sum(x * x, axis=0)[None, :]
        for k in range(4):
            for q in range(3):
                m = cen[k, :, q * order : (q + 1) * order] / scale_col
                mh, mm, ml = split3(m)
                left = jnp.concatenate([mh, mh, mm, mh, ml, mm], axis=0)
                mn = -0.5 * jnp.sum(m * m, axis=0)[:, None]
                v = jnp.exp(dot(left, right, TN) + mn + xn)
                at = slice(k * width + q * order, k * width + (q + 1) * order)
                khi[at, :], klo[at, :] = split2(v)

    late = solver & (r == 3)

    @pl.when(jnp.logical_not(late))
    def _():
        tiles()

    images = jnp.zeros((div.shape[0], span), f32)

    def place_of(x, y):
        chip = 4 * x + y
        q = jnp.int32(12)
        for k, (a, b) in enumerate(OWNERS):
            q = jnp.where(chip == 4 * a + b, k, q)
        return q

    for k in (3, 2, 1, 0):
        mine = holders[k]
        nearby = [(k, j) for j in range(k - 1, -1, -1)]

        if k < 3:

            @pl.when(mine)
            def _():
                t = div[:, k * width : (k + 1) * width]
                for j in range(3, k, -1):
                    arrived(prod_in.at[j], PROD_R + j)
                    t = t - prod_in[j]
                pulled[k] = lower(t, whi, wlo, order)
                spread((k, k), k, mine, pulled, P_S, P_R, nearby)

        @pl.when(jnp.logical_not(mine))
        def _():
            arrived(pulled.at[k], P_R + k)

        multiply = solver & (r == k) & (c < k)

        if k > 0:

            @pl.when(multiply)
            def _():
                prod_out[...] = product(pulled[k], whi[...], wlo[...])
                send(multiply, lambda: prod_out, lambda: prod_in.at[k], PROD_S, PROD_R + k, (dp, c, c))

        @pl.when(solver)
        def _():
            give_core0(solver, pulled, k, PF_S, P_R)

        if k == 3:

            @pl.when(late)
            def _():
                tiles()

        at = slice(k * width, (k + 1) * width)
        images = images + product(pulled[k], khi[at, :], klo[at, :])

    both = jnp.concatenate(split2(images), axis=0)
    rhs = div.shape[0]
    for i, (a, b) in enumerate(offsets):
        x = lax.rem(r + a, 4)
        y = lax.rem(c + b, 4)
        chunk = place_of(x, y)
        owned = chunk < 12
        slot = 2 * i + core

        @pl.when(owned)
        def _():
            at = pl.ds(pl.multiple_of(chunk * order, order), order)
            out = dot(both, klo[at, :], NT) + dot(both, khi[at, :], NT)
            nsend[chunk] = out[rhs:] + out[:rhs]

        if i < 15:

            @pl.when(owned)
            def _():
                send(owned, lambda chunk=chunk: nsend.at[chunk], lambda: nred.at[slot], N_S + i, N_R, (2 * z + 1, x, y))

        else:

            @pl.when(owned & solver)
            def _():
                nred[31] = nsend[chunk]

            away = owned & (core == 0)

            @pl.when(away)
            def _():
                send(away, lambda chunk=chunk: nsend.at[chunk], lambda: nred.at[30], N_S + i, N_R, (2 * z + 1, x, y))

    place_here = place_of(r, c)
    owner = solver & (place_here < 12)

    @pl.when(solver)
    def _():
        pl.semaphore_wait(zready, 1)

    @pl.when(owner)
    def _():
        arrived(nred.at[0:31], N_R)
        total = nred[0]
        for s in range(1, 32):
            total = total + nred[s]
        zred[z] = total
        for i, d in enumerate(far):
            send(
                owner,
                lambda: zred.at[z],
                lambda: zred.at[z],
                Z_S + i,
                Z_R,
                (2 * lax.rem(z + d, planes) + 1, r, c),
            )

    @pl.when(at_low | at_high)
    def _():
        load_inv.wait()
        for k in range(2):
            arrived(aux.at[k, 0 : 6 - 3 * k], BULK_R + k)
            for n, (i, j) in enumerate(PLACES):
                si = slice(i * order, (i + 1) * order)
                sj = slice(j * order, (j + 1) * order)
                block = inv[i] if i == j and k == 1 else aux[k, n]
                dhi[k, sj, si], dlo[k, sj, si] = split2(block.T)

    flush()

    @pl.when(owner)
    def _():
        arrived(zred.at[0 : planes - 1], Z_R)
        total = zred[0]
        for s in range(1, planes):
            total = total + zred[s]
        mout[...] = total * (1.0 / total_rows)

    passing = owner & jnp.logical_not(at_low | at_high)
    goal_low = place_here < 6
    part = jnp.where(goal_low, place_here, place_here - 6)

    @pl.when(passing)
    def _():
        goal = (dp, jnp.where(goal_low, LOW[0], HIGH[0]), jnp.where(goal_low, LOW[1], HIGH[1]))
        send(passing, lambda: mout, lambda: min_.at[part], M_S, M_R + part, goal)

    def normal(k):
        base = 3 * (k % 2)
        for j in range(base, base + 3):
            if j == 0:
                min_[0] = mout[...]
            else:
                arrived(min_.at[j], M_R + j)
        joined = jnp.concatenate([min_[base], min_[base + 1], min_[base + 2]], axis=1)
        return joined + ridge_weight * pulled[k]

    @pl.when(at_low)
    def _():
        img[0] = upper(normal(0), dhi.at[0], dlo.at[0], order)
        spread(LOW, 0, at_low, img, IMG_S, IMG_R, [(2, 0), (3, 0)], 0, 2)
        t = normal(1) - product(img[0], thi[...], tlo[...])
        img[1] = upper(t, dhi.at[1], dlo.at[1], order)
        spread(LOW, 1, at_low, img, IMG_S + 15, IMG_R, [(2, 1), (3, 1)], 0, 2)
        spread(LOW, 0, at_low, img, IMG_S, IMG_R, [(2, 0), (3, 0)], 2, 15)
        spread(LOW, 1, at_low, img, IMG_S + 15, IMG_R, [(2, 1), (3, 1)], 2, 15)

    for k in range(2):
        multiply = solver & (c == k) & (r >= 2)

        @pl.when(multiply)
        def _():
            arrived(img.at[k], IMG_R + k)
            back_out[...] = product(img[k], thi[...], tlo[...])
            at = 2 * (r - 2) + k
            send(multiply, lambda: back_out, lambda at=at: back_in.at[at], BACK_S, BACK_R + at, (dp,) + HIGH)

    @pl.when(at_high)
    def _():
        for k in (2, 3):
            t = normal(k)
            if k == 3:
                t = t - product(img[2], thi[...], tlo[...])
            for j in range(2):
                at = 2 * (k - 2) + j
                arrived(back_in.at[at], BACK_R + at)
                t = t - back_in[at]
            img[k] = upper(t, dhi.at[k - 2], dlo.at[k - 2], order)
            spread(HIGH, k, at_high, img, IMG_S + 15 * (k - 2), IMG_R, [])

    for k in range(4):
        known = at_low | (solver & (c == k) & (r >= 2)) if k < 2 else at_high

        @pl.when(jnp.logical_not(known))
        def _():
            arrived(img.at[k], IMG_R + k)

        @pl.when(solver)
        def _():
            give_core0(solver, img, k, IMGF_S, IMG_R)

    load_res.wait()
    gamma = jnp.sum(rev[...] * rev[...], axis=1, keepdims=True)
    segs = [slice(k * width, (k + 1) * width) for k in range(4)]
    curvature = jnp.zeros((rhs, 1), f32)
    for k in range(4):
        image[:, segs[k]] = img[k]
        curvature += jnp.sum(div[:, segs[k]] * img[k], axis=1, keepdims=True)
    alpha = gamma / curvature
    gamma_next = jnp.zeros((rhs, 1), f32)
    for k in range(4):
        res = rev[:, segs[k]] - alpha * img[k]
        gamma_next += jnp.sum(res * res, axis=1, keepdims=True)
    alphas[...] = jnp.broadcast_to(alpha, alphas.shape)
    betas[...] = jnp.broadcast_to(gamma_next / gamma, betas.shape)

    flush()


def per_device(data, centres, scales, factor, block_inv, iterate, residual, direction):
    planes = lax.axis_size("dp") // 2
    total_rows = data.shape[1] * lax.axis_size("dp") * lax.axis_size("crow")
    inputs, width = centres.shape
    span = data.shape[1] // lax.axis_size("ccol")
    rhs, total = direction.shape
    order = block_inv.shape[1]
    whole = jax.ShapeDtypeStruct((rhs, total), f32)
    vmem = pltpu.VMEM
    hbm = pl.BlockSpec(memory_space=pl.ANY)
    square = (width, width)
    image, alphas, betas = pl.pallas_call(
        functools.partial(kernel, planes, total_rows),
        out_shape=(whole, whole, whole),
        in_specs=[hbm, hbm, pl.BlockSpec(memory_space=pltpu.SMEM)] + [hbm] * 4,
        out_specs=(pl.BlockSpec(memory_space=pltpu.VMEM),) * 3,
        scratch_shapes=[
            vmem(square, f32),
            vmem((3, order, order), f32),
            vmem(square, bf16),
            vmem(square, bf16),
            vmem(square, bf16),
            vmem(square, bf16),
            vmem((inputs, span), f32),
            vmem((4, inputs, width), f32),
            vmem((total, span), bf16),
            vmem((total, span), bf16),
            vmem((rhs, total), f32),
            vmem((rhs, total), f32),
            vmem((4, rhs, width), f32),
            vmem((rhs, width), f32),
            vmem((4, rhs, width), f32),
            vmem((12, rhs, order), f32),
            vmem((32, rhs, order), f32),
            vmem((planes, rhs, order), f32),
            vmem((rhs, order), f32),
            vmem((6, rhs, order), f32),
            vmem((4, rhs, width), f32),
            vmem((rhs, width), f32),
            vmem((4, rhs, width), f32),
            vmem((6, order, order), f32),
            vmem((2, 6, order, order), f32),
            vmem((2,) + square, bf16),
            vmem((2,) + square, bf16),
            pltpu.SemaphoreType.DMA((S.count,)),
            pltpu.SemaphoreType.REGULAR,
        ],
        compiler_params=pltpu.CompilerParams(
            collective_id=0, has_side_effects=True, vmem_limit_bytes=64 * 1024 * 1024 - 65536
        ),
    )(data, centres, scales, factor, block_inv, residual, direction)
    new_iterate = iterate + alphas * direction
    new_residual = residual - alphas * image
    new_direction = new_residual + betas * direction
    return new_iterate, new_residual, new_direction


def solution(mesh):
    placed = (
        P(None, ("dp", "crow")),
        P(None, "ccol"),
        P(),
        P("crow", "ccol"),
        P("crow", None, None),
        P(),
        P(),
        P(),
    )
    return jax.shard_map(
        per_device, mesh=mesh, in_specs=placed, out_specs=(P(), P(), P()), check_vma=False
    )
```

```python
import functools

import jax
import jax.numpy as jnp
from jax import lax
from jax.experimental import pallas as pl
from jax.experimental.pallas import tpu as pltpu
from jax.sharding import PartitionSpec as P

MESH = pl.DeviceIdType.MESH
f32 = jnp.float32
bf16 = jnp.bfloat16
HIGHEST = lax.Precision.HIGHEST
ridge_weight = 0.2

NN = (((1,), (0,)), ((), ()))
NT = (((1,), (1,)), ((), ()))
TN = (((0,), (0,)), ((), ()))


def dot(a, b, dims=NN, precision=None):
    return lax.dot_general(a, b, dims, precision=precision, preferred_element_type=f32)


def split2(v):
    high = v.astype(bf16)
    return high, (v - high.astype(f32)).astype(bf16)


def split3(v):
    high = v.astype(bf16)
    rest = v - high.astype(f32)
    mid = rest.astype(bf16)
    return high, mid, (rest - mid.astype(f32)).astype(bf16)


def product(v, high, low, dims=NN):
    rows = v.shape[0]
    both = jnp.concatenate(split2(v), axis=0)
    out = dot(both, low, dims) + dot(both, high, dims)
    return out[rows:] + out[:rows]


def lower(v, high, low, order):
    parts = [product(v[:, j:], high[j:, j : j + order], low[j:, j : j + order]) for j in range(0, v.shape[1], order)]
    return jnp.concatenate(parts, axis=1)


def upper(v, high, low, order):
    parts = []
    for j in range(0, v.shape[1], order):
        parts.append(product(v[:, : j + order], high[: j + order, j : j + order], low[: j + order, j : j + order]))
    return jnp.concatenate(parts, axis=1)


def ring_distance(d, n):
    d = d % n
    return min(d, n - d)


class Semaphores:
    def __init__(self):
        self.count = 0

    def take(self, n):
        first = self.count
        self.count += n
        return first


OWNERS = ((1, 0), (0, 0), (2, 0), (1, 1), (1, 3), (0, 1), (3, 2), (2, 2), (0, 2), (3, 3), (3, 1), (2, 3))
PLACES = ((1, 0), (2, 0), (2, 1), (0, 0), (1, 1), (2, 2))
LOW = (1, 0)
HIGH = (3, 2)

S = Semaphores()
LOAD = S.take(8)
CEN_R = S.take(4)
CEN_S = S.take(3)
CENF_S = S.take(4)
P_R = S.take(4)
P_S = S.take(16)
PF_S = S.take(4)
PROD_R = S.take(12)
PROD_S = S.take(3)
PIECE_R = S.take(3)
PIECE_S = S.take(6)
N_R = S.take(1)
N_S = S.take(16)
Z_R = S.take(1)
Z_S = S.take(16)
M_R = S.take(6)
M_S = S.take(1)
IMG_R = S.take(4)
IMG_S = S.take(30)
IMGF_S = S.take(4)
BACK_R = S.take(12)
BACK_S = S.take(3)
BULK_R = S.take(2)
BULK_S = S.take(1)


def kernel(
    planes,
    total_rows,
    data,
    centres,
    scales,
    factor,
    block_inv,
    residual,
    direction,
    image,
    alphas,
    betas,
    fac,
    inv,
    whi,
    wlo,
    thi,
    tlo,
    rows,
    cen,
    khi,
    klo,
    rev,
    div,
    pulled,
    prod_out,
    prod_in,
    nsend,
    nred,
    zred,
    mout,
    min_,
    img,
    back_out,
    back_in,
    blocks,
    aux,
    dhi,
    dlo,
    sems,
    zready,
):
    dp = lax.axis_index("dp")
    r = lax.axis_index("crow")
    c = lax.axis_index("ccol")
    core = lax.rem(dp, 2)
    z = dp // 2
    solver = core == 1
    width = fac.shape[0]
    span = rows.shape[1]
    order = inv.shape[1]
    pending = []

    def local(src, dst, k):
        return pltpu.make_async_copy(src, dst, sems.at[LOAD + k])

    def remote(src, dst, ss, rs, dev):
        return pltpu.make_async_remote_copy(
            src_ref=src,
            dst_ref=dst,
            send_sem=sems.at[ss],
            recv_sem=sems.at[rs],
            device_id=dev,
            device_id_type=MESH,
        )

    def arrived(dst, rs):
        pltpu.make_async_copy(dst, dst, sems.at[rs]).wait()

    def send(cond, src, dst, ss, rs, dev):
        remote(src(), dst(), ss, rs, dev).start()
        pending.append((cond, src, ss))

    def flush():
        groups = {}
        for cond, src, ss in pending:
            groups.setdefault(id(cond), (cond, []))[1].append((src, ss))
        pending.clear()
        for cond, sends in groups.values():

            @pl.when(cond)
            def _():
                for src, ss in sends:
                    arrived(src(), ss)

    load_fac = local(factor, fac, 0)
    load_inv = local(block_inv, inv, 1)
    load_dir = local(direction, div, 2)
    load_cen = local(centres, cen.at[c], 3)
    load_rows = local(data.at[:, pl.ds(pl.multiple_of(c * span, 128), span)], rows, 4)
    load_res = local(residual, rev, 5)
    diagonal = solver & (r == c)
    below = solver & (r > c)
    at_low = solver & (r == LOW[0]) & (c == LOW[1])
    at_high = solver & (r == HIGH[0]) & (c == HIGH[1])
    helpers = [(core == 0) & (r == k) & (c == k) for k in range(4)]
    holders = [solver & (r == k) & (c == k) for k in range(4)]

    @pl.when((r == c) | at_low | at_high)
    def _():
        load_inv.start()

    load_dir.start()

    @pl.when((r == c) | below)
    def _():
        load_fac.start()

    load_cen.start()
    load_rows.start()
    load_res.start()

    barrier = pltpu.get_barrier_semaphore()
    far = sorted(range(1, planes), key=lambda d: -ring_distance(d, planes))
    offsets = sorted(
        [(a, b) for a in range(4) for b in range(4)],
        key=lambda o: (-ring_distance(o[0], 4) - ring_distance(o[1], 4), o),
    )

    def signal(sem, dev):
        pl.semaphore_signal(sem, inc=1, device_id=dev, device_id_type=MESH)

    @pl.when(solver)
    def _():
        for a, b in offsets[:-1]:
            signal(barrier, (dp, lax.rem(r + a, 4), lax.rem(c + b, 4)))
        for d in far:
            signal(barrier, (2 * lax.rem(z + d, planes), r, c))
        signal(barrier, (dp - 1, r, c))

    for here, users in ((at_low, (0, 1)), (at_high, (2, 3))):

        @pl.when(here)
        def _():
            for k in users:
                signal(barrier, (dp - 1, k, k))

    @pl.when(core == 0)
    def _():
        signal(barrier, (dp + 1, r, c))

    load_dir.wait()

    first = holders[3]

    @pl.when(first)
    def _():
        load_inv.wait()
        load_fac.wait()
        b = [slice(k * order, (k + 1) * order) for k in range(3)]
        base = 3 * width
        d = [div[:, base + k * order : base + (k + 1) * order] for k in range(3)]
        p2 = dot(d[2], inv[2], NN, HIGHEST)
        p1 = dot(d[1] - dot(p2, fac[b[2], b[1]], NN, HIGHEST), inv[1], NN, HIGHEST)
        t0 = d[0] - dot(p2, fac[b[2], b[0]], NN, HIGHEST)
        p0 = dot(t0 - dot(p1, fac[b[1], b[0]], NN, HIGHEST), inv[0], NN, HIGHEST)
        pulled[3, :, b[0]] = p0
        pulled[3, :, b[1]] = p1
        pulled[3, :, b[2]] = p2

    def keep(v, i, j):
        si = slice(i * order, (i + 1) * order)
        sj = slice(j * order, (j + 1) * order)
        whi[si, sj], wlo[si, sj] = split2(v)
        thi[sj, si], tlo[sj, si] = split2(v.T)

    def invert():
        b = [slice(k * order, (k + 1) * order) for k in range(3)]
        mul = functools.partial(dot, precision=HIGHEST)
        a0, a1, a2 = inv[0], inv[1], inv[2]
        x10 = -mul(a1, mul(fac[b[1], b[0]], a0))
        x21 = -mul(a2, mul(fac[b[2], b[1]], a1))
        x20 = -mul(a2, mul(fac[b[2], b[0]], a0) + mul(fac[b[2], b[1]], x10))
        for i, row in enumerate(((a0,), (x10, a1), (x20, x21, a2))):
            for j, v in enumerate(row):
                blocks[PLACES.index((i, j))] = v
                whi[b[i], b[j]], wlo[b[i], b[j]] = split2(v)

    @pl.when((r == c) & jnp.logical_not(first))
    def _():
        load_inv.wait()
        load_fac.wait()
        invert()

    @pl.when(below)
    def _():
        load_fac.wait()
        for i in range(3):
            for j in range(3):
                keep(fac[i * order : (i + 1) * order, j * order : (j + 1) * order], i, j)

    @pl.when(solver)
    def _():
        pl.semaphore_wait(barrier, 16)

    @pl.when(core == 0)
    def _():
        pl.semaphore_wait(barrier, planes + jnp.where(r == c, 1, 0))
        signal(zready, (dp + 1, r, c))

    def spread(source, k, cond, buf, ss, rs, urgent, first=0, last=15, skip=()):
        goals = [((source[0] + a) % 4, (source[1] + b) % 4) for a, b in offsets[:-1]]
        goals = urgent + [g for g in goals if g not in urgent]
        for i, (a, b) in enumerate(goals):
            if first <= i < last and (a, b) not in skip:
                send(cond, lambda: buf.at[k], lambda: buf.at[k], ss + i, rs + k, (dp, a, b))

    cut = [slice(i * order, (i + 1) * order) for i in range(3)]

    def pieces_product(take, emit, high, low, sequence):
        total = None
        for i in sequence[:2]:
            term = product(take(i), high[cut[i], :], low[cut[i], :])
            total = term if total is None else total + term
        i = sequence[2]
        v = take(i)
        for j in sequence:
            emit(j, total[:, cut[j]] + product(v, high[cut[i], cut[j]], low[cut[i], cut[j]]))

    def give_inverse(k, cond):
        goal = LOW if k < 2 else HIGH
        n = 6 - 3 * (k % 2)
        src = lambda: blocks.at[0:n]
        send(cond, src, lambda: aux.at[k % 2, 0:n], BULK_S, BULK_R + k % 2, (dp + 1,) + goal)

    def give_core0(cond, buf, k, ss, rs):
        send(cond, lambda: buf.at[k], lambda: buf.at[k], ss + k, rs + k, (dp - 1, r, c))

    @pl.when(first)
    def _():
        spread((3, 3), 3, first, pulled, P_S, P_R, [(3, 2), (3, 1), (3, 0)])

    load_cen.wait()

    @pl.when(solver)
    def _():
        for i, d in enumerate((2, 1, 3)):
            send(solver, lambda: cen.at[c], lambda: cen.at[c], CEN_S + i, CEN_R + c, (dp, r, lax.rem(c + d, 4)))

    for k in range(4):

        @pl.when(helpers[k])
        def _():
            give_inverse(k, helpers[k])

    scale_col = jnp.zeros((rows.shape[0], 1), f32)
    place = lax.broadcasted_iota(jnp.int32, (rows.shape[0], 1), 0)
    for k in range(rows.shape[0]):
        scale_col = jnp.where(place == k, scales[k], scale_col)

    load_rows.wait()

    for i, d in enumerate((1, 3, 2)):
        src = lax.rem(c + d, 4)
        arrived(cen.at[src], CEN_R + src)

        @pl.when(solver)
        def _():
            send(solver, lambda src=src: cen.at[src], lambda src=src: cen.at[src], CENF_S + i, CEN_R + src, (dp - 1, r, c))

    def tiles():
        x = rows[...] / scale_col
        xh, xm, xl = split3(x)
        right = jnp.concatenate([xh, xm, xh, xl, xh, xm], axis=0)
        xn = -0.5 * jnp.sum(x * x, axis=0)[None, :]
        for k in range(4):
            for q in range(3):
                m = cen[k, :, q * order : (q + 1) * order] / scale_col
                mh, mm, ml = split3(m)
                left = jnp.concatenate([mh, mh, mm, mh, ml, mm], axis=0)
                mn = -0.5 * jnp.sum(m * m, axis=0)[:, None]
                v = jnp.exp(dot(left, right, TN) + mn + xn)
                at = slice(k * width + q * order, k * width + (q + 1) * order)
                khi[at, :], klo[at, :] = split2(v)

    late = solver & (r == 3)

    @pl.when(jnp.logical_not(late))
    def _():
        tiles()

    images = jnp.zeros((div.shape[0], span), f32)

    def place_of(x, y):
        chip = 4 * x + y
        q = jnp.int32(12)
        for k, (a, b) in enumerate(OWNERS):
            q = jnp.where(chip == 4 * a + b, k, q)
        return q

    for k in (3, 2, 1, 0):
        mine = holders[k]
        nearby = [(k, j) for j in range(k - 1, -1, -1)]

        if k < 3:

            @pl.when(mine)
            def _():
                t = [div[:, k * width + i * order : k * width + (i + 1) * order] for i in range(3)]
                for j in range(3, k, -1):
                    for i in (2, 1, 0):
                        if j > k + 1:
                            arrived(prod_in.at[j, i], PROD_R + 3 * j + i)
                            t[i] = t[i] - prod_in[j, i]
                for i in (2, 1, 0):
                    arrived(prod_in.at[k + 1, i], PROD_R + 3 * (k + 1) + i)
                    t[i] = t[i] - prod_in[k + 1, i]
                    v = jnp.concatenate(t[i:], axis=1)
                    pulled[k, :, cut[i]] = product(v, whi[i * order :, cut[i]], wlo[i * order :, cut[i]])
                    if k > 0:
                        piece = lambda i=i: pulled.at[k, :, cut[i]]
                        send(mine, piece, piece, PIECE_S + i, PIECE_R + i, (dp, k, k - 1))
                spread((k, k), k, mine, pulled, P_S, P_R, nearby, skip=nearby[:1])

        multiply = solver & (r == k) & (c < k)
        pieced = solver & (r == k) & (c == k - 1) if k in (1, 2) else None
        whole = multiply if pieced is None else multiply & (c < k - 1)

        def give_product(cond):
            def emit(j, v):
                prod_out[j] = v
                send(cond, lambda: prod_out.at[j], lambda: prod_in.at[k, j], PROD_S + j, PROD_R + 3 * k + j, (dp, c, c))

            return emit

        if pieced is not None:

            @pl.when(pieced)
            def _():
                def take(i):
                    arrived(pulled.at[k, :, cut[i]], PIECE_R + i)
                    return pulled[k, :, cut[i]]

                pieces_product(take, give_product(pieced), whi, wlo, (2, 1, 0))

        known = mine if pieced is None else mine | pieced

        @pl.when(jnp.logical_not(known))
        def _():
            arrived(pulled.at[k], P_R + k)

        if k > 1:

            @pl.when(whole)
            def _():
                emit = give_product(whole)
                for j in (2, 1, 0):
                    emit(j, product(pulled[k], whi[:, cut[j]], wlo[:, cut[j]]))

        @pl.when(solver)
        def _():
            give_core0(solver, pulled, k, PF_S, P_R)

        if k == 3:

            @pl.when(late)
            def _():
                tiles()

        at = slice(k * width, (k + 1) * width)
        images = images + product(pulled[k], khi[at, :], klo[at, :])

    both = jnp.concatenate(split2(images), axis=0)
    rhs = div.shape[0]
    for i, (a, b) in enumerate(offsets):
        x = lax.rem(r + a, 4)
        y = lax.rem(c + b, 4)
        chunk = place_of(x, y)
        owned = chunk < 12
        slot = 2 * i + core

        @pl.when(owned)
        def _():
            at = pl.ds(pl.multiple_of(chunk * order, order), order)
            out = dot(both, klo[at, :], NT) + dot(both, khi[at, :], NT)
            nsend[chunk] = out[rhs:] + out[:rhs]

        if i < 15:

            @pl.when(owned)
            def _():
                send(owned, lambda chunk=chunk: nsend.at[chunk], lambda: nred.at[slot], N_S + i, N_R, (2 * z + 1, x, y))

        else:

            @pl.when(owned & solver)
            def _():
                nred[31] = nsend[chunk]

            away = owned & (core == 0)

            @pl.when(away)
            def _():
                send(away, lambda chunk=chunk: nsend.at[chunk], lambda: nred.at[30], N_S + i, N_R, (2 * z + 1, x, y))

    place_here = place_of(r, c)
    owner = solver & (place_here < 12)

    @pl.when(solver)
    def _():
        pl.semaphore_wait(zready, 1)

    @pl.when(owner)
    def _():
        arrived(nred.at[0:31], N_R)
        total = nred[0]
        for s in range(1, 32):
            total = total + nred[s]
        zred[z] = total
        for i, d in enumerate(far):
            send(
                owner,
                lambda: zred.at[z],
                lambda: zred.at[z],
                Z_S + i,
                Z_R,
                (2 * lax.rem(z + d, planes) + 1, r, c),
            )

    @pl.when(at_low | at_high)
    def _():
        load_inv.wait()
        for k in range(2):
            arrived(aux.at[k, 0 : 6 - 3 * k], BULK_R + k)
            for n, (i, j) in enumerate(PLACES):
                si = slice(i * order, (i + 1) * order)
                sj = slice(j * order, (j + 1) * order)
                block = inv[i] if i == j and k == 1 else aux[k, n]
                dhi[k, sj, si], dlo[k, sj, si] = split2(block.T)

    flush()

    @pl.when(owner)
    def _():
        arrived(zred.at[0 : planes - 1], Z_R)
        total = zred[0]
        for s in range(1, planes):
            total = total + zred[s]
        mout[...] = total * (1.0 / total_rows)

    passing = owner & jnp.logical_not(at_low | at_high)
    goal_low = place_here < 6
    part = jnp.where(goal_low, place_here, place_here - 6)

    @pl.when(passing)
    def _():
        goal = (dp, jnp.where(goal_low, LOW[0], HIGH[0]), jnp.where(goal_low, LOW[1], HIGH[1]))
        send(passing, lambda: mout, lambda: min_.at[part], M_S, M_R + part, goal)

    def normal(k):
        base = 3 * (k % 2)
        for j in range(base, base + 3):
            if j == 0:
                min_[0] = mout[...]
            else:
                arrived(min_.at[j], M_R + j)
        joined = jnp.concatenate([min_[base], min_[base + 1], min_[base + 2]], axis=1)
        return joined + ridge_weight * pulled[k]

    @pl.when(at_low)
    def _():
        img[0] = upper(normal(0), dhi.at[0], dlo.at[0], order)
        spread(LOW, 0, at_low, img, IMG_S, IMG_R, [(2, 0), (3, 0)], 0, 2)
        t = normal(1) - product(img[0], thi[...], tlo[...])
        for i in range(3):
            end = (i + 1) * order
            img[1, :, cut[i]] = product(t[:, :end], dhi[1, :end, cut[i]], dlo[1, :end, cut[i]])
            piece = lambda i=i: img.at[1, :, cut[i]]
            for n in range(2):
                send(at_low, piece, piece, PIECE_S + 3 * n + i, PIECE_R + i, (dp, 2 + n, 1))
        spread(LOW, 0, at_low, img, IMG_S, IMG_R, [(2, 0), (3, 0)], 2, 15)
        spread(LOW, 1, at_low, img, IMG_S + 15, IMG_R, [(2, 1), (3, 1)], 2, 15)

    for k in range(2):
        multiply = solver & (c == k) & (r >= 2)

        @pl.when(multiply)
        def _():
            at = 2 * (r - 2) + k
            if k == 0:
                arrived(img.at[k], IMG_R + k)

            def take(i):
                if k == 1:
                    arrived(img.at[k, :, cut[i]], PIECE_R + i)
                return img[k, :, cut[i]]

            def emit(j, v):
                back_out[j] = v
                goal = (dp,) + HIGH
                send(multiply, lambda: back_out.at[j], lambda: back_in.at[at, j], BACK_S + j, BACK_R + 3 * at + j, goal)

            pieces_product(take, emit, thi, tlo, (0, 1, 2))

    @pl.when(at_high)
    def _():
        for k in (2, 3):
            t = normal(k)
            if k == 3:
                t = t - product(img[2], thi[...], tlo[...])
            ready = []
            for i in range(3):
                part = t[:, cut[i]]
                for at in (2 * (k - 2), 2 * (k - 2) + 1):
                    arrived(back_in.at[at, i], BACK_R + 3 * at + i)
                    part = part - back_in[at, i]
                ready.append(part)
                end = (i + 1) * order
                v = jnp.concatenate(ready, axis=1)
                img[k, :, cut[i]] = product(v, dhi[k - 2, :end, cut[i]], dlo[k - 2, :end, cut[i]])
            spread(HIGH, k, at_high, img, IMG_S + 15 * (k - 2), IMG_R, [])

    for k in range(4):
        known = at_low | (solver & (c == k) & (r >= 2)) if k < 2 else at_high

        @pl.when(jnp.logical_not(known))
        def _():
            arrived(img.at[k], IMG_R + k)

        @pl.when(solver)
        def _():
            give_core0(solver, img, k, IMGF_S, IMG_R)

    load_res.wait()
    gamma = jnp.sum(rev[...] * rev[...], axis=1, keepdims=True)
    segs = [slice(k * width, (k + 1) * width) for k in range(4)]
    curvature = jnp.zeros((rhs, 1), f32)
    for k in range(4):
        image[:, segs[k]] = img[k]
        curvature += jnp.sum(div[:, segs[k]] * img[k], axis=1, keepdims=True)
    alpha = gamma / curvature
    gamma_next = jnp.zeros((rhs, 1), f32)
    for k in range(4):
        res = rev[:, segs[k]] - alpha * img[k]
        gamma_next += jnp.sum(res * res, axis=1, keepdims=True)
    alphas[...] = jnp.broadcast_to(alpha, alphas.shape)
    betas[...] = jnp.broadcast_to(gamma_next / gamma, betas.shape)

    flush()


def per_device(data, centres, scales, factor, block_inv, iterate, residual, direction):
    planes = lax.axis_size("dp") // 2
    total_rows = data.shape[1] * lax.axis_size("dp") * lax.axis_size("crow")
    inputs, width = centres.shape
    span = data.shape[1] // lax.axis_size("ccol")
    rhs, total = direction.shape
    order = block_inv.shape[1]
    whole = jax.ShapeDtypeStruct((rhs, total), f32)
    vmem = pltpu.VMEM
    hbm = pl.BlockSpec(memory_space=pl.ANY)
    square = (width, width)
    image, alphas, betas = pl.pallas_call(
        functools.partial(kernel, planes, total_rows),
        out_shape=(whole, whole, whole),
        in_specs=[hbm, hbm, pl.BlockSpec(memory_space=pltpu.SMEM)] + [hbm] * 4,
        out_specs=(pl.BlockSpec(memory_space=pltpu.VMEM),) * 3,
        scratch_shapes=[
            vmem(square, f32),
            vmem((3, order, order), f32),
            vmem(square, bf16),
            vmem(square, bf16),
            vmem(square, bf16),
            vmem(square, bf16),
            vmem((inputs, span), f32),
            vmem((4, inputs, width), f32),
            vmem((total, span), bf16),
            vmem((total, span), bf16),
            vmem((rhs, total), f32),
            vmem((rhs, total), f32),
            vmem((4, rhs, width), f32),
            vmem((3, rhs, order), f32),
            vmem((4, 3, rhs, order), f32),
            vmem((12, rhs, order), f32),
            vmem((32, rhs, order), f32),
            vmem((planes, rhs, order), f32),
            vmem((rhs, order), f32),
            vmem((6, rhs, order), f32),
            vmem((4, rhs, width), f32),
            vmem((3, rhs, order), f32),
            vmem((4, 3, rhs, order), f32),
            vmem((6, order, order), f32),
            vmem((2, 6, order, order), f32),
            vmem((2,) + square, bf16),
            vmem((2,) + square, bf16),
            pltpu.SemaphoreType.DMA((S.count,)),
            pltpu.SemaphoreType.REGULAR,
        ],
        compiler_params=pltpu.CompilerParams(
            collective_id=0, has_side_effects=True, vmem_limit_bytes=64 * 1024 * 1024 - 65536
        ),
    )(data, centres, scales, factor, block_inv, residual, direction)
    new_iterate = iterate + alphas * direction
    new_residual = residual - alphas * image
    new_direction = new_residual + betas * direction
    return new_iterate, new_residual, new_direction


def solution(mesh):
    placed = (
        P(None, ("dp", "crow")),
        P(None, "ccol"),
        P(),
        P("crow", "ccol"),
        P("crow", None, None),
        P(),
        P(),
        P(),
    )
    return jax.shard_map(
        per_device, mesh=mesh, in_specs=placed, out_specs=(P(), P(), P()), check_vma=False
    )
```

```python
import functools

import jax
import jax.numpy as jnp
from jax import lax
from jax.experimental import pallas as pl
from jax.experimental.pallas import tpu as pltpu
from jax.sharding import PartitionSpec as P

MESH = pl.DeviceIdType.MESH
f32 = jnp.float32
bf16 = jnp.bfloat16
HIGHEST = lax.Precision.HIGHEST
ridge_weight = 0.2

NN = (((1,), (0,)), ((), ()))
NT = (((1,), (1,)), ((), ()))
TN = (((0,), (0,)), ((), ()))


def dot(a, b, dims=NN, precision=None):
    return lax.dot_general(a, b, dims, precision=precision, preferred_element_type=f32)


def split2(v):
    high = v.astype(bf16)
    return high, (v - high.astype(f32)).astype(bf16)


def split3(v):
    high = v.astype(bf16)
    rest = v - high.astype(f32)
    mid = rest.astype(bf16)
    return high, mid, (rest - mid.astype(f32)).astype(bf16)


def product(v, high, low, dims=NN):
    rows = v.shape[0]
    both = jnp.concatenate(split2(v), axis=0)
    out = dot(both, low, dims) + dot(both, high, dims)
    return out[rows:] + out[:rows]


def lower(v, high, low, order):
    parts = [product(v[:, j:], high[j:, j : j + order], low[j:, j : j + order]) for j in range(0, v.shape[1], order)]
    return jnp.concatenate(parts, axis=1)


def upper(v, high, low, order):
    parts = []
    for j in range(0, v.shape[1], order):
        parts.append(product(v[:, : j + order], high[: j + order, j : j + order], low[: j + order, j : j + order]))
    return jnp.concatenate(parts, axis=1)


def ring_distance(d, n):
    d = d % n
    return min(d, n - d)


class Semaphores:
    def __init__(self):
        self.count = 0

    def take(self, n):
        first = self.count
        self.count += n
        return first


OWNERS = ((1, 0), (0, 0), (2, 0), (1, 1), (1, 3), (0, 1), (3, 2), (2, 2), (0, 2), (3, 3), (3, 1), (2, 3))
PLACES = ((1, 0), (2, 0), (2, 1), (0, 0), (1, 1), (2, 2))
LOW = (1, 0)
HIGH = (3, 2)

S = Semaphores()
LOAD = S.take(8)
CEN_R = S.take(4)
CEN_S = S.take(3)
CENF_S = S.take(4)
P_R = S.take(4)
P_S = S.take(16)
PF_S = S.take(4)
PROD_R = S.take(4)
PROD_S = S.take(1)
N_R = S.take(1)
N_S = S.take(16)
Z_R = S.take(1)
Z_S = S.take(16)
M_R = S.take(6)
M_S = S.take(1)
IMG_R = S.take(4)
IMG_S = S.take(30)
IMGF_S = S.take(4)
BACK_R = S.take(4)
BACK_S = S.take(1)
BULK_R = S.take(2)
BULK_S = S.take(1)


def kernel(
    planes,
    total_rows,
    data,
    centres,
    scales,
    factor,
    block_inv,
    residual,
    direction,
    image,
    alphas,
    betas,
    fac,
    inv,
    whi,
    wlo,
    thi,
    tlo,
    rows,
    cen,
    khi,
    klo,
    rev,
    div,
    pulled,
    prod_out,
    prod_in,
    nsend,
    nred,
    zred,
    mout,
    min_,
    img,
    back_out,
    back_in,
    blocks,
    aux,
    dhi,
    dlo,
    sems,
    zready,
):
    dp = lax.axis_index("dp")
    r = lax.axis_index("crow")
    c = lax.axis_index("ccol")
    core = lax.rem(dp, 2)
    z = dp // 2
    solver = core == 1
    width = fac.shape[0]
    span = rows.shape[1]
    order = inv.shape[1]
    pending = []

    def local(src, dst, k):
        return pltpu.make_async_copy(src, dst, sems.at[LOAD + k])

    def remote(src, dst, ss, rs, dev):
        return pltpu.make_async_remote_copy(
            src_ref=src,
            dst_ref=dst,
            send_sem=sems.at[ss],
            recv_sem=sems.at[rs],
            device_id=dev,
            device_id_type=MESH,
        )

    def arrived(dst, rs):
        pltpu.make_async_copy(dst, dst, sems.at[rs]).wait()

    def send(cond, src, dst, ss, rs, dev):
        remote(src(), dst(), ss, rs, dev).start()
        pending.append((cond, src, ss))

    def flush():
        groups = {}
        for cond, src, ss in pending:
            groups.setdefault(id(cond), (cond, []))[1].append((src, ss))
        pending.clear()
        for cond, sends in groups.values():

            @pl.when(cond)
            def _():
                for src, ss in sends:
                    arrived(src(), ss)

    load_fac = local(factor, fac, 0)
    under = (slice(order, width), slice(0, width - order))
    load_under = local(factor.at[under], fac.at[under], 6)
    load_inv = local(block_inv, inv, 1)
    load_dir = local(direction, div, 2)
    load_cen = local(centres, cen.at[c], 3)
    load_rows = local(data.at[:, pl.ds(pl.multiple_of(c * span, 128), span)], rows, 4)
    load_res = local(residual, rev, 5)
    diagonal = solver & (r == c)
    below = solver & (r > c)
    at_low = solver & (r == LOW[0]) & (c == LOW[1])
    at_high = solver & (r == HIGH[0]) & (c == HIGH[1])
    helpers = [(core == 0) & (r == k) & (c == k) for k in range(4)]
    holders = [solver & (r == k) & (c == k) for k in range(4)]

    @pl.when((r == c) | at_low | at_high)
    def _():
        load_inv.start()

    load_dir.start()

    @pl.when(r == c)
    def _():
        load_under.start()

    @pl.when(below)
    def _():
        load_fac.start()

    load_cen.start()
    load_rows.start()
    load_res.start()

    barrier = pltpu.get_barrier_semaphore()
    far = sorted(range(1, planes), key=lambda d: -ring_distance(d, planes))
    offsets = sorted(
        [(a, b) for a in range(4) for b in range(4)],
        key=lambda o: (-ring_distance(o[0], 4) - ring_distance(o[1], 4), o),
    )

    def signal(sem, dev):
        pl.semaphore_signal(sem, inc=1, device_id=dev, device_id_type=MESH)

    @pl.when(solver)
    def _():
        for d in (2, 1, 3):
            signal(barrier, (dp, r, lax.rem(c + d, 4)))
            signal(barrier, (dp, lax.rem(r + d, 4), c))
        for d in far:
            signal(barrier, (2 * lax.rem(z + d, planes), r, c))
        signal(barrier, (dp - 1, r, c))

    for here, users in ((at_low, (0, 1)), (at_high, (2, 3))):

        @pl.when(here)
        def _():
            for k in users:
                signal(barrier, (dp - 1, k, k))

    @pl.when(core == 0)
    def _():
        signal(barrier, (dp + 1, r, c))

    load_dir.wait()

    first = holders[3]

    @pl.when(first)
    def _():
        load_inv.wait()
        load_under.wait()
        b = [slice(k * order, (k + 1) * order) for k in range(3)]
        base = 3 * width
        d = [div[:, base + k * order : base + (k + 1) * order] for k in range(3)]
        p2 = dot(d[2], inv[2], NN, HIGHEST)
        p1 = dot(d[1] - dot(p2, fac[b[2], b[1]], NN, HIGHEST), inv[1], NN, HIGHEST)
        t0 = d[0] - dot(p2, fac[b[2], b[0]], NN, HIGHEST)
        p0 = dot(t0 - dot(p1, fac[b[1], b[0]], NN, HIGHEST), inv[0], NN, HIGHEST)
        pulled[3, :, b[0]] = p0
        pulled[3, :, b[1]] = p1
        pulled[3, :, b[2]] = p2

    def keep(v, i, j):
        si = slice(i * order, (i + 1) * order)
        sj = slice(j * order, (j + 1) * order)
        whi[si, sj], wlo[si, sj] = split2(v)
        thi[sj, si], tlo[sj, si] = split2(v.T)

    def invert():
        b = [slice(k * order, (k + 1) * order) for k in range(3)]
        mul = functools.partial(dot, precision=HIGHEST)
        a0, a1, a2 = inv[0], inv[1], inv[2]
        x10 = -mul(a1, mul(fac[b[1], b[0]], a0))
        x21 = -mul(a2, mul(fac[b[2], b[1]], a1))
        x20 = -mul(a2, mul(fac[b[2], b[0]], a0) + mul(fac[b[2], b[1]], x10))
        for i, row in enumerate(((a0,), (x10, a1), (x20, x21, a2))):
            for j, v in enumerate(row):
                blocks[PLACES.index((i, j))] = v
                whi[b[i], b[j]], wlo[b[i], b[j]] = split2(v)

    @pl.when((r == c) & jnp.logical_not(first))
    def _():
        load_inv.wait()
        load_under.wait()
        invert()

    @pl.when(below)
    def _():
        load_fac.wait()
        for i in range(3):
            for j in range(3):
                keep(fac[i * order : (i + 1) * order, j * order : (j + 1) * order], i, j)

    @pl.when(solver)
    def _():
        pl.semaphore_wait(barrier, 7)

    @pl.when(core == 0)
    def _():
        pl.semaphore_wait(barrier, planes + jnp.where(r == c, 1, 0))
        signal(zready, (dp + 1, r, c))

    def spread(source, k, cond, buf, ss, rs, urgent, first=0, last=15):
        goals = [((source[0] + a) % 4, (source[1] + b) % 4) for a, b in offsets[:-1]]
        goals = urgent + [g for g in goals if g not in urgent]
        for i, (a, b) in enumerate(goals):
            if first <= i < last:
                send(cond, lambda: buf.at[k], lambda: buf.at[k], ss + i, rs + k, (dp, a, b))

    def give_inverse(k, cond):
        goal = LOW if k < 2 else HIGH
        n = 6 - 3 * (k % 2)
        src = lambda: blocks.at[0:n]
        send(cond, src, lambda: aux.at[k % 2, 0:n], BULK_S, BULK_R + k % 2, (dp + 1,) + goal)

    def give_core0(cond, buf, k, ss, rs):
        send(cond, lambda: buf.at[k], lambda: buf.at[k], ss + k, rs + k, (dp - 1, r, c))

    @pl.when(first)
    def _():
        spread((3, 3), 3, first, pulled, P_S, P_R, [(3, 2), (3, 1), (3, 0)], 0, 3)

    load_cen.wait()

    @pl.when(solver)
    def _():
        for i, d in enumerate((2, 1, 3)):
            send(solver, lambda: cen.at[c], lambda: cen.at[c], CEN_S + i, CEN_R + c, (dp, r, lax.rem(c + d, 4)))

    for k in range(4):

        @pl.when(helpers[k])
        def _():
            give_inverse(k, helpers[k])

    scale_col = jnp.zeros((rows.shape[0], 1), f32)
    place = lax.broadcasted_iota(jnp.int32, (rows.shape[0], 1), 0)
    for k in range(rows.shape[0]):
        scale_col = jnp.where(place == k, scales[k], scale_col)

    load_rows.wait()

    for i, d in enumerate((1, 3, 2)):
        src = lax.rem(c + d, 4)
        arrived(cen.at[src], CEN_R + src)

        @pl.when(solver)
        def _():
            send(solver, lambda src=src: cen.at[src], lambda src=src: cen.at[src], CENF_S + i, CEN_R + src, (dp - 1, r, c))

    @pl.when(first)
    def _():
        spread((3, 3), 3, first, pulled, P_S, P_R, [(3, 2), (3, 1), (3, 0)], 3, 15)

    def tiles():
        x = rows[...] / scale_col
        xh, xm, xl = split3(x)
        right = jnp.concatenate([xh, xm, xh, xl, xh, xm], axis=0)
        xn = -0.5 * jnp.sum(x * x, axis=0)[None, :]
        for k in range(4):
            for q in range(3):
                m = cen[k, :, q * order : (q + 1) * order] / scale_col
                mh, mm, ml = split3(m)
                left = jnp.concatenate([mh, mh, mm, mh, ml, mm], axis=0)
                mn = -0.5 * jnp.sum(m * m, axis=0)[:, None]
                v = jnp.exp(dot(left, right, TN) + mn + xn)
                at = slice(k * width + q * order, k * width + (q + 1) * order)
                khi[at, :], klo[at, :] = split2(v)

    late = solver & (r == 3)

    @pl.when(jnp.logical_not(late))
    def _():
        tiles()

    images = jnp.zeros((div.shape[0], span), f32)

    def place_of(x, y):
        chip = 4 * x + y
        q = jnp.int32(12)
        for k, (a, b) in enumerate(OWNERS):
            q = jnp.where(chip == 4 * a + b, k, q)
        return q

    for k in (3, 2, 1, 0):
        mine = holders[k]
        nearby = [(k, j) for j in range(k - 1, -1, -1)]

        if k < 3:

            @pl.when(mine)
            def _():
                t = div[:, k * width : (k + 1) * width]
                for j in range(3, k, -1):
                    arrived(prod_in.at[j], PROD_R + j)
                    t = t - prod_in[j]
                pulled[k] = lower(t, whi, wlo, order)
                spread((k, k), k, mine, pulled, P_S, P_R, nearby)

        @pl.when(jnp.logical_not(mine))
        def _():
            arrived(pulled.at[k], P_R + k)

        multiply = solver & (r == k) & (c < k)

        if k > 0:

            @pl.when(multiply)
            def _():
                prod_out[...] = product(pulled[k], whi[...], wlo[...])
                send(multiply, lambda: prod_out, lambda: prod_in.at[k], PROD_S, PROD_R + k, (dp, c, c))

        @pl.when(solver)
        def _():
            give_core0(solver, pulled, k, PF_S, P_R)

        if k == 3:

            @pl.when(late)
            def _():
                tiles()

        at = slice(k * width, (k + 1) * width)
        images = images + product(pulled[k], khi[at, :], klo[at, :])

    both = jnp.concatenate(split2(images), axis=0)
    rhs = div.shape[0]
    for i, (a, b) in enumerate(offsets):
        x = lax.rem(r + a, 4)
        y = lax.rem(c + b, 4)
        chunk = place_of(x, y)
        owned = chunk < 12
        slot = 2 * i + core

        @pl.when(owned)
        def _():
            at = pl.ds(pl.multiple_of(chunk * order, order), order)
            out = dot(both, klo[at, :], NT) + dot(both, khi[at, :], NT)
            nsend[chunk] = out[rhs:] + out[:rhs]

        if i < 15:

            @pl.when(owned)
            def _():
                send(owned, lambda chunk=chunk: nsend.at[chunk], lambda: nred.at[slot], N_S + i, N_R, (2 * z + 1, x, y))

        else:

            @pl.when(owned & solver)
            def _():
                nred[31] = nsend[chunk]

            away = owned & (core == 0)

            @pl.when(away)
            def _():
                send(away, lambda chunk=chunk: nsend.at[chunk], lambda: nred.at[30], N_S + i, N_R, (2 * z + 1, x, y))

    place_here = place_of(r, c)
    owner = solver & (place_here < 12)

    @pl.when(solver)
    def _():
        pl.semaphore_wait(zready, 1)

    @pl.when(owner)
    def _():
        arrived(nred.at[0:31], N_R)
        total = nred[0]
        for s in range(1, 32):
            total = total + nred[s]
        zred[z] = total
        for i, d in enumerate(far):
            send(
                owner,
                lambda: zred.at[z],
                lambda: zred.at[z],
                Z_S + i,
                Z_R,
                (2 * lax.rem(z + d, planes) + 1, r, c),
            )

    @pl.when(at_low | at_high)
    def _():
        load_inv.wait()
        for k in range(2):
            arrived(aux.at[k, 0 : 6 - 3 * k], BULK_R + k)
            for n, (i, j) in enumerate(PLACES):
                si = slice(i * order, (i + 1) * order)
                sj = slice(j * order, (j + 1) * order)
                block = inv[i] if i == j and k == 1 else aux[k, n]
                dhi[k, sj, si], dlo[k, sj, si] = split2(block.T)

    flush()

    @pl.when(owner)
    def _():
        arrived(zred.at[0 : planes - 1], Z_R)
        total = zred[0]
        for s in range(1, planes):
            total = total + zred[s]
        mout[...] = total * (1.0 / total_rows)

    passing = owner & jnp.logical_not(at_low | at_high)
    goal_low = place_here < 6
    part = jnp.where(goal_low, place_here, place_here - 6)

    @pl.when(passing)
    def _():
        goal = (dp, jnp.where(goal_low, LOW[0], HIGH[0]), jnp.where(goal_low, LOW[1], HIGH[1]))
        send(passing, lambda: mout, lambda: min_.at[part], M_S, M_R + part, goal)

    def normal(k):
        base = 3 * (k % 2)
        for j in range(base, base + 3):
            if j == 0:
                min_[0] = mout[...]
            else:
                arrived(min_.at[j], M_R + j)
        joined = jnp.concatenate([min_[base], min_[base + 1], min_[base + 2]], axis=1)
        return joined + ridge_weight * pulled[k]

    @pl.when(at_low)
    def _():
        img[0] = upper(normal(0), dhi.at[0], dlo.at[0], order)
        spread(LOW, 0, at_low, img, IMG_S, IMG_R, [(2, 0), (3, 0)], 0, 2)
        t = normal(1) - product(img[0], thi[...], tlo[...])
        img[1] = upper(t, dhi.at[1], dlo.at[1], order)
        spread(LOW, 1, at_low, img, IMG_S + 15, IMG_R, [(2, 1), (3, 1)], 0, 2)
        spread(LOW, 0, at_low, img, IMG_S, IMG_R, [(2, 0), (3, 0)], 2, 15)
        spread(LOW, 1, at_low, img, IMG_S + 15, IMG_R, [(2, 1), (3, 1)], 2, 15)

    for k in range(2):
        multiply = solver & (c == k) & (r >= 2)

        @pl.when(multiply)
        def _():
            arrived(img.at[k], IMG_R + k)
            back_out[...] = product(img[k], thi[...], tlo[...])
            at = 2 * (r - 2) + k
            send(multiply, lambda: back_out, lambda at=at: back_in.at[at], BACK_S, BACK_R + at, (dp,) + HIGH)

    @pl.when(at_high)
    def _():
        for k in (2, 3):
            t = normal(k)
            if k == 3:
                t = t - product(img[2], thi[...], tlo[...])
            for j in range(2):
                at = 2 * (k - 2) + j
                arrived(back_in.at[at], BACK_R + at)
                t = t - back_in[at]
            img[k] = upper(t, dhi.at[k - 2], dlo.at[k - 2], order)
            spread(HIGH, k, at_high, img, IMG_S + 15 * (k - 2), IMG_R, [])

    for k in range(4):
        known = at_low | (solver & (c == k) & (r >= 2)) if k < 2 else at_high

        @pl.when(jnp.logical_not(known))
        def _():
            arrived(img.at[k], IMG_R + k)

        @pl.when(solver)
        def _():
            give_core0(solver, img, k, IMGF_S, IMG_R)

    load_res.wait()
    gamma = jnp.sum(rev[...] * rev[...], axis=1, keepdims=True)
    segs = [slice(k * width, (k + 1) * width) for k in range(4)]
    curvature = jnp.zeros((rhs, 1), f32)
    for k in range(4):
        image[:, segs[k]] = img[k]
        curvature += jnp.sum(div[:, segs[k]] * img[k], axis=1, keepdims=True)
    alpha = gamma / curvature
    gamma_next = jnp.zeros((rhs, 1), f32)
    for k in range(4):
        res = rev[:, segs[k]] - alpha * img[k]
        gamma_next += jnp.sum(res * res, axis=1, keepdims=True)
    alphas[...] = jnp.broadcast_to(alpha, alphas.shape)
    betas[...] = jnp.broadcast_to(gamma_next / gamma, betas.shape)

    flush()


def per_device(data, centres, scales, factor, block_inv, iterate, residual, direction):
    planes = lax.axis_size("dp") // 2
    total_rows = data.shape[1] * lax.axis_size("dp") * lax.axis_size("crow")
    inputs, width = centres.shape
    span = data.shape[1] // lax.axis_size("ccol")
    rhs, total = direction.shape
    order = block_inv.shape[1]
    whole = jax.ShapeDtypeStruct((rhs, total), f32)
    vmem = pltpu.VMEM
    hbm = pl.BlockSpec(memory_space=pl.ANY)
    square = (width, width)
    image, alphas, betas = pl.pallas_call(
        functools.partial(kernel, planes, total_rows),
        out_shape=(whole, whole, whole),
        in_specs=[hbm, hbm, pl.BlockSpec(memory_space=pltpu.SMEM)] + [hbm] * 4,
        out_specs=(pl.BlockSpec(memory_space=pltpu.VMEM),) * 3,
        scratch_shapes=[
            vmem(square, f32),
            vmem((3, order, order), f32),
            vmem(square, bf16),
            vmem(square, bf16),
            vmem(square, bf16),
            vmem(square, bf16),
            vmem((inputs, span), f32),
            vmem((4, inputs, width), f32),
            vmem((total, span), bf16),
            vmem((total, span), bf16),
            vmem((rhs, total), f32),
            vmem((rhs, total), f32),
            vmem((4, rhs, width), f32),
            vmem((rhs, width), f32),
            vmem((4, rhs, width), f32),
            vmem((12, rhs, order), f32),
            vmem((32, rhs, order), f32),
            vmem((planes, rhs, order), f32),
            vmem((rhs, order), f32),
            vmem((6, rhs, order), f32),
            vmem((4, rhs, width), f32),
            vmem((rhs, width), f32),
            vmem((4, rhs, width), f32),
            vmem((6, order, order), f32),
            vmem((2, 6, order, order), f32),
            vmem((2,) + square, bf16),
            vmem((2,) + square, bf16),
            pltpu.SemaphoreType.DMA((S.count,)),
            pltpu.SemaphoreType.REGULAR,
        ],
        compiler_params=pltpu.CompilerParams(
            collective_id=0, has_side_effects=True, vmem_limit_bytes=64 * 1024 * 1024 - 65536
        ),
    )(data, centres, scales, factor, block_inv, residual, direction)
    new_iterate = iterate + alphas * direction
    new_residual = residual - alphas * image
    new_direction = new_residual + betas * direction
    return new_iterate, new_residual, new_direction


def solution(mesh):
    placed = (
        P(None, ("dp", "crow")),
        P(None, "ccol"),
        P(),
        P("crow", "ccol"),
        P("crow", None, None),
        P(),
        P(),
        P(),
    )
    return jax.shard_map(
        per_device, mesh=mesh, in_specs=placed, out_specs=(P(), P(), P()), check_vma=False
    )
```

```python
import functools

import jax
import jax.numpy as jnp
from jax import lax
from jax.experimental import pallas as pl
from jax.experimental.pallas import tpu as pltpu
from jax.sharding import PartitionSpec as P

MESH = pl.DeviceIdType.MESH
f32 = jnp.float32
bf16 = jnp.bfloat16
HIGHEST = lax.Precision.HIGHEST
ridge_weight = 0.2

NN = (((1,), (0,)), ((), ()))
NT = (((1,), (1,)), ((), ()))
TN = (((0,), (0,)), ((), ()))


def dot(a, b, dims=NN, precision=None):
    return lax.dot_general(a, b, dims, precision=precision, preferred_element_type=f32)


def split2(v):
    high = v.astype(bf16)
    return high, (v - high.astype(f32)).astype(bf16)


def split3(v):
    high = v.astype(bf16)
    rest = v - high.astype(f32)
    mid = rest.astype(bf16)
    return high, mid, (rest - mid.astype(f32)).astype(bf16)


def product(v, high, low, dims=NN):
    rows = v.shape[0]
    both = jnp.concatenate(split2(v), axis=0)
    out = dot(both, low, dims) + dot(both, high, dims)
    return out[rows:] + out[:rows]


def lower(v, high, low, order):
    parts = [product(v[:, j:], high[j:, j : j + order], low[j:, j : j + order]) for j in range(0, v.shape[1], order)]
    return jnp.concatenate(parts, axis=1)


def upper(v, high, low, order):
    parts = []
    for j in range(0, v.shape[1], order):
        parts.append(product(v[:, : j + order], high[: j + order, j : j + order], low[: j + order, j : j + order]))
    return jnp.concatenate(parts, axis=1)


def ring_distance(d, n):
    d = d % n
    return min(d, n - d)


class Semaphores:
    def __init__(self):
        self.count = 0

    def take(self, n):
        first = self.count
        self.count += n
        return first


OWNERS = ((1, 0), (0, 0), (2, 0), (1, 1), (1, 3), (0, 1), (3, 2), (2, 2), (0, 2), (3, 3), (3, 1), (2, 3))
PLACES = ((1, 0), (2, 0), (2, 1), (0, 0), (1, 1), (2, 2))
LOW = (1, 0)
HIGH = (3, 2)

S = Semaphores()
LOAD = S.take(8)
CEN_R = S.take(4)
CEN_S = S.take(3)
CENF_S = S.take(4)
P_R = S.take(4)
P_S = S.take(16)
PF_S = S.take(4)
PROD_R = S.take(4)
PROD_S = S.take(1)
N_R = S.take(1)
N_S = S.take(16)
Z_R = S.take(1)
Z_S = S.take(16)
M_R = S.take(6)
M_S = S.take(1)
IMG_R = S.take(4)
IMG_S = S.take(30)
IMGF_S = S.take(4)
BACK_R = S.take(4)
BACK_S = S.take(1)
BULK_R = S.take(2)
BULK_S = S.take(1)
BOTH_S = S.take(15)


def kernel(
    planes,
    total_rows,
    data,
    centres,
    scales,
    factor,
    block_inv,
    residual,
    direction,
    image,
    alphas,
    betas,
    fac,
    inv,
    whi,
    wlo,
    thi,
    tlo,
    rows,
    cen,
    khi,
    klo,
    rev,
    div,
    pulled,
    prod_out,
    prod_in,
    nsend,
    nred,
    zred,
    mout,
    min_,
    img,
    back_out,
    back_in,
    blocks,
    aux,
    dhi,
    dlo,
    sems,
    zready,
):
    dp = lax.axis_index("dp")
    r = lax.axis_index("crow")
    c = lax.axis_index("ccol")
    core = lax.rem(dp, 2)
    z = dp // 2
    solver = core == 1
    width = fac.shape[0]
    span = rows.shape[1]
    order = inv.shape[1]
    pending = []

    def local(src, dst, k):
        return pltpu.make_async_copy(src, dst, sems.at[LOAD + k])

    def remote(src, dst, ss, rs, dev):
        return pltpu.make_async_remote_copy(
            src_ref=src,
            dst_ref=dst,
            send_sem=sems.at[ss],
            recv_sem=sems.at[rs],
            device_id=dev,
            device_id_type=MESH,
        )

    def arrived(dst, rs):
        pltpu.make_async_copy(dst, dst, sems.at[rs]).wait()

    def send(cond, src, dst, ss, rs, dev):
        remote(src(), dst(), ss, rs, dev).start()
        pending.append((cond, src, ss))

    def flush():
        groups = {}
        for cond, src, ss in pending:
            groups.setdefault(id(cond), (cond, []))[1].append((src, ss))
        pending.clear()
        for cond, sends in groups.values():

            @pl.when(cond)
            def _():
                for src, ss in sends:
                    arrived(src(), ss)

    load_fac = local(factor, fac, 0)
    under = (slice(order, width), slice(0, width - order))
    load_under = local(factor.at[under], fac.at[under], 6)
    load_inv = local(block_inv, inv, 1)
    load_dir = local(direction, div, 2)
    load_cen = local(centres, cen.at[c], 3)
    load_rows = local(data.at[:, pl.ds(pl.multiple_of(c * span, 128), span)], rows, 4)
    load_res = local(residual, rev, 5)
    diagonal = solver & (r == c)
    below = solver & (r > c)
    at_low = solver & (r == LOW[0]) & (c == LOW[1])
    at_high = solver & (r == HIGH[0]) & (c == HIGH[1])
    helpers = [(core == 0) & (r == k) & (c == k) for k in range(4)]
    holders = [solver & (r == k) & (c == k) for k in range(4)]

    @pl.when((r == c) | at_low | at_high)
    def _():
        load_inv.start()

    load_dir.start()

    @pl.when(r == c)
    def _():
        load_under.start()

    @pl.when(below)
    def _():
        load_fac.start()

    load_cen.start()
    load_rows.start()
    load_res.start()

    barrier = pltpu.get_barrier_semaphore()
    far = sorted(range(1, planes), key=lambda d: -ring_distance(d, planes))
    offsets = sorted(
        [(a, b) for a in range(4) for b in range(4)],
        key=lambda o: (-ring_distance(o[0], 4) - ring_distance(o[1], 4), o),
    )

    def signal(sem, dev):
        pl.semaphore_signal(sem, inc=1, device_id=dev, device_id_type=MESH)

    @pl.when(solver)
    def _():
        for d in (2, 1, 3):
            signal(barrier, (dp, r, lax.rem(c + d, 4)))
            signal(barrier, (dp, lax.rem(r + d, 4), c))
        for d in far:
            signal(barrier, (2 * lax.rem(z + d, planes), r, c))
        signal(barrier, (dp - 1, r, c))

    for here, users in ((at_low, (0, 1)), (at_high, (2, 3))):

        @pl.when(here)
        def _():
            for k in users:
                signal(barrier, (dp - 1, k, k))

    @pl.when(core == 0)
    def _():
        signal(barrier, (dp + 1, r, c))

    load_dir.wait()

    first = holders[3]

    @pl.when(first)
    def _():
        load_inv.wait()
        load_under.wait()
        b = [slice(k * order, (k + 1) * order) for k in range(3)]
        base = 3 * width
        d = [div[:, base + k * order : base + (k + 1) * order] for k in range(3)]
        p2 = dot(d[2], inv[2], NN, HIGHEST)
        p1 = dot(d[1] - dot(p2, fac[b[2], b[1]], NN, HIGHEST), inv[1], NN, HIGHEST)
        t0 = d[0] - dot(p2, fac[b[2], b[0]], NN, HIGHEST)
        p0 = dot(t0 - dot(p1, fac[b[1], b[0]], NN, HIGHEST), inv[0], NN, HIGHEST)
        pulled[3, :, b[0]] = p0
        pulled[3, :, b[1]] = p1
        pulled[3, :, b[2]] = p2

    def keep(v, i, j):
        si = slice(i * order, (i + 1) * order)
        sj = slice(j * order, (j + 1) * order)
        whi[si, sj], wlo[si, sj] = split2(v)
        thi[sj, si], tlo[sj, si] = split2(v.T)

    def invert():
        b = [slice(k * order, (k + 1) * order) for k in range(3)]
        mul = functools.partial(dot, precision=HIGHEST)
        a0, a1, a2 = inv[0], inv[1], inv[2]
        x10 = -mul(a1, mul(fac[b[1], b[0]], a0))
        x21 = -mul(a2, mul(fac[b[2], b[1]], a1))
        x20 = -mul(a2, mul(fac[b[2], b[0]], a0) + mul(fac[b[2], b[1]], x10))
        for i, row in enumerate(((a0,), (x10, a1), (x20, x21, a2))):
            for j, v in enumerate(row):
                blocks[PLACES.index((i, j))] = v
                whi[b[i], b[j]], wlo[b[i], b[j]] = split2(v)

    @pl.when((r == c) & jnp.logical_not(first))
    def _():
        load_inv.wait()
        load_under.wait()
        invert()

    @pl.when(below)
    def _():
        load_fac.wait()
        for i in range(3):
            for j in range(3):
                keep(fac[i * order : (i + 1) * order, j * order : (j + 1) * order], i, j)

    @pl.when(solver)
    def _():
        pl.semaphore_wait(barrier, 7)

    @pl.when(core == 0)
    def _():
        pl.semaphore_wait(barrier, planes + jnp.where(r == c, 1, 0))
        signal(zready, (dp + 1, r, c))

    def spread(source, k, cond, buf, ss, rs, urgent, first=0, last=15, both=False):
        goals = [((source[0] + a) % 4, (source[1] + b) % 4) for a, b in offsets[:-1]]
        goals = urgent + [g for g in goals if g not in urgent]
        for i, (a, b) in enumerate(goals):
            if both:
                send(cond, lambda: buf.at[k], lambda: buf.at[k], BOTH_S + i, rs + k, (dp - 1, a, b))
            if first <= i < last:
                send(cond, lambda: buf.at[k], lambda: buf.at[k], ss + i, rs + k, (dp, a, b))

    def give_inverse(k, cond):
        goal = LOW if k < 2 else HIGH
        n = 6 - 3 * (k % 2)
        src = lambda: blocks.at[0:n]
        send(cond, src, lambda: aux.at[k % 2, 0:n], BULK_S, BULK_R + k % 2, (dp + 1,) + goal)

    def give_core0(cond, buf, k, ss, rs):
        send(cond, lambda: buf.at[k], lambda: buf.at[k], ss + k, rs + k, (dp - 1, r, c))

    @pl.when(first)
    def _():
        spread((3, 3), 3, first, pulled, P_S, P_R, [(3, 2), (3, 1), (3, 0)], 0, 3)

    load_cen.wait()

    @pl.when(solver)
    def _():
        for i, d in enumerate((2, 1, 3)):
            send(solver, lambda: cen.at[c], lambda: cen.at[c], CEN_S + i, CEN_R + c, (dp, r, lax.rem(c + d, 4)))

    for k in range(4):

        @pl.when(helpers[k])
        def _():
            give_inverse(k, helpers[k])

    scale_col = jnp.zeros((rows.shape[0], 1), f32)
    place = lax.broadcasted_iota(jnp.int32, (rows.shape[0], 1), 0)
    for k in range(rows.shape[0]):
        scale_col = jnp.where(place == k, scales[k], scale_col)

    load_rows.wait()

    for i, d in enumerate((1, 3, 2)):
        src = lax.rem(c + d, 4)
        arrived(cen.at[src], CEN_R + src)

        @pl.when(solver)
        def _():
            send(solver, lambda src=src: cen.at[src], lambda src=src: cen.at[src], CENF_S + i, CEN_R + src, (dp - 1, r, c))

    @pl.when(first)
    def _():
        spread((3, 3), 3, first, pulled, P_S, P_R, [(3, 2), (3, 1), (3, 0)], 3, 15)

    def tiles():
        x = rows[...] / scale_col
        xh, xm, xl = split3(x)
        right = jnp.concatenate([xh, xm, xh, xl, xh, xm], axis=0)
        xn = -0.5 * jnp.sum(x * x, axis=0)[None, :]
        for k in range(4):
            for q in range(3):
                m = cen[k, :, q * order : (q + 1) * order] / scale_col
                mh, mm, ml = split3(m)
                left = jnp.concatenate([mh, mh, mm, mh, ml, mm], axis=0)
                mn = -0.5 * jnp.sum(m * m, axis=0)[:, None]
                v = jnp.exp(dot(left, right, TN) + mn + xn)
                at = slice(k * width + q * order, k * width + (q + 1) * order)
                khi[at, :], klo[at, :] = split2(v)

    late = solver & (r == 3)

    @pl.when(jnp.logical_not(late))
    def _():
        tiles()

    images = jnp.zeros((div.shape[0], span), f32)

    def place_of(x, y):
        chip = 4 * x + y
        q = jnp.int32(12)
        for k, (a, b) in enumerate(OWNERS):
            q = jnp.where(chip == 4 * a + b, k, q)
        return q

    for k in (3, 2, 1, 0):
        mine = holders[k]
        nearby = [(k, j) for j in range(k - 1, -1, -1)]

        if k < 3:

            @pl.when(mine)
            def _():
                t = div[:, k * width : (k + 1) * width]
                for j in range(3, k, -1):
                    arrived(prod_in.at[j], PROD_R + j)
                    t = t - prod_in[j]
                pulled[k] = lower(t, whi, wlo, order)
                spread((k, k), k, mine, pulled, P_S, P_R, nearby, both=k == 0)

        @pl.when(jnp.logical_not(mine))
        def _():
            arrived(pulled.at[k], P_R + k)

        multiply = solver & (r == k) & (c < k)

        if k > 0:

            @pl.when(multiply)
            def _():
                prod_out[...] = product(pulled[k], whi[...], wlo[...])
                send(multiply, lambda: prod_out, lambda: prod_in.at[k], PROD_S, PROD_R + k, (dp, c, c))

        passes = mine if k == 0 else solver

        @pl.when(passes)
        def _():
            give_core0(passes, pulled, k, PF_S, P_R)

        if k == 3:

            @pl.when(late)
            def _():
                tiles()

        at = slice(k * width, (k + 1) * width)
        images = images + product(pulled[k], khi[at, :], klo[at, :])

    both = jnp.concatenate(split2(images), axis=0)
    rhs = div.shape[0]
    for i, (a, b) in enumerate(offsets):
        x = lax.rem(r + a, 4)
        y = lax.rem(c + b, 4)
        chunk = place_of(x, y)
        owned = chunk < 12
        slot = 2 * i + core

        @pl.when(owned)
        def _():
            at = pl.ds(pl.multiple_of(chunk * order, order), order)
            out = dot(both, klo[at, :], NT) + dot(both, khi[at, :], NT)
            nsend[chunk] = out[rhs:] + out[:rhs]

        if i < 15:

            @pl.when(owned)
            def _():
                send(owned, lambda chunk=chunk: nsend.at[chunk], lambda: nred.at[slot], N_S + i, N_R, (2 * z + 1, x, y))

        else:

            @pl.when(owned & solver)
            def _():
                nred[31] = nsend[chunk]

            away = owned & (core == 0)

            @pl.when(away)
            def _():
                send(away, lambda chunk=chunk: nsend.at[chunk], lambda: nred.at[30], N_S + i, N_R, (2 * z + 1, x, y))

    place_here = place_of(r, c)
    owner = solver & (place_here < 12)

    @pl.when(solver)
    def _():
        pl.semaphore_wait(zready, 1)

    @pl.when(owner)
    def _():
        arrived(nred.at[0:31], N_R)
        total = nred[0]
        for s in range(1, 32):
            total = total + nred[s]
        zred[z] = total
        for i, d in enumerate(far):
            send(
                owner,
                lambda: zred.at[z],
                lambda: zred.at[z],
                Z_S + i,
                Z_R,
                (2 * lax.rem(z + d, planes) + 1, r, c),
            )

    @pl.when(at_low | at_high)
    def _():
        load_inv.wait()
        for k in range(2):
            arrived(aux.at[k, 0 : 6 - 3 * k], BULK_R + k)
            for n, (i, j) in enumerate(PLACES):
                si = slice(i * order, (i + 1) * order)
                sj = slice(j * order, (j + 1) * order)
                block = inv[i] if i == j and k == 1 else aux[k, n]
                dhi[k, sj, si], dlo[k, sj, si] = split2(block.T)

    flush()

    @pl.when(owner)
    def _():
        arrived(zred.at[0 : planes - 1], Z_R)
        total = zred[0]
        for s in range(1, planes):
            total = total + zred[s]
        mout[...] = total * (1.0 / total_rows)

    passing = owner & jnp.logical_not(at_low | at_high)
    goal_low = place_here < 6
    part = jnp.where(goal_low, place_here, place_here - 6)

    @pl.when(passing)
    def _():
        goal = (dp, jnp.where(goal_low, LOW[0], HIGH[0]), jnp.where(goal_low, LOW[1], HIGH[1]))
        send(passing, lambda: mout, lambda: min_.at[part], M_S, M_R + part, goal)

    def normal(k):
        base = 3 * (k % 2)
        for j in range(base, base + 3):
            if j == 0:
                min_[0] = mout[...]
            else:
                arrived(min_.at[j], M_R + j)
        joined = jnp.concatenate([min_[base], min_[base + 1], min_[base + 2]], axis=1)
        return joined + ridge_weight * pulled[k]

    @pl.when(at_low)
    def _():
        img[0] = upper(normal(0), dhi.at[0], dlo.at[0], order)
        spread(LOW, 0, at_low, img, IMG_S, IMG_R, [(2, 0), (3, 0)], 0, 2)
        t = normal(1) - product(img[0], thi[...], tlo[...])
        img[1] = upper(t, dhi.at[1], dlo.at[1], order)
        spread(LOW, 1, at_low, img, IMG_S + 15, IMG_R, [(2, 1), (3, 1)], 0, 2)
        spread(LOW, 0, at_low, img, IMG_S, IMG_R, [(2, 0), (3, 0)], 2, 15)
        spread(LOW, 1, at_low, img, IMG_S + 15, IMG_R, [(2, 1), (3, 1)], 2, 15)

    for k in range(2):
        multiply = solver & (c == k) & (r >= 2)

        @pl.when(multiply)
        def _():
            arrived(img.at[k], IMG_R + k)
            back_out[...] = product(img[k], thi[...], tlo[...])
            at = 2 * (r - 2) + k
            send(multiply, lambda: back_out, lambda at=at: back_in.at[at], BACK_S, BACK_R + at, (dp,) + HIGH)

    @pl.when(at_high)
    def _():
        for k in (2, 3):
            t = normal(k)
            if k == 3:
                t = t - product(img[2], thi[...], tlo[...])
            for j in range(2):
                at = 2 * (k - 2) + j
                arrived(back_in.at[at], BACK_R + at)
                t = t - back_in[at]
            img[k] = upper(t, dhi.at[k - 2], dlo.at[k - 2], order)
            spread(HIGH, k, at_high, img, IMG_S + 15 * (k - 2), IMG_R, [], both=k == 3)

    for k in range(4):
        known = at_low | (solver & (c == k) & (r >= 2)) if k < 2 else at_high

        @pl.when(jnp.logical_not(known))
        def _():
            arrived(img.at[k], IMG_R + k)

        passes = at_high if k == 3 else solver

        @pl.when(passes)
        def _():
            give_core0(passes, img, k, IMGF_S, IMG_R)

    load_res.wait()
    gamma = jnp.sum(rev[...] * rev[...], axis=1, keepdims=True)
    segs = [slice(k * width, (k + 1) * width) for k in range(4)]
    curvature = jnp.zeros((rhs, 1), f32)
    for k in range(4):
        image[:, segs[k]] = img[k]
        curvature += jnp.sum(div[:, segs[k]] * img[k], axis=1, keepdims=True)
    alpha = gamma / curvature
    gamma_next = jnp.zeros((rhs, 1), f32)
    for k in range(4):
        res = rev[:, segs[k]] - alpha * img[k]
        gamma_next += jnp.sum(res * res, axis=1, keepdims=True)
    alphas[...] = jnp.broadcast_to(alpha, alphas.shape)
    betas[...] = jnp.broadcast_to(gamma_next / gamma, betas.shape)

    flush()


def per_device(data, centres, scales, factor, block_inv, iterate, residual, direction):
    planes = lax.axis_size("dp") // 2
    total_rows = data.shape[1] * lax.axis_size("dp") * lax.axis_size("crow")
    inputs, width = centres.shape
    span = data.shape[1] // lax.axis_size("ccol")
    rhs, total = direction.shape
    order = block_inv.shape[1]
    whole = jax.ShapeDtypeStruct((rhs, total), f32)
    vmem = pltpu.VMEM
    hbm = pl.BlockSpec(memory_space=pl.ANY)
    square = (width, width)
    image, alphas, betas = pl.pallas_call(
        functools.partial(kernel, planes, total_rows),
        out_shape=(whole, whole, whole),
        in_specs=[hbm, hbm, pl.BlockSpec(memory_space=pltpu.SMEM)] + [hbm] * 4,
        out_specs=(pl.BlockSpec(memory_space=pltpu.VMEM),) * 3,
        scratch_shapes=[
            vmem(square, f32),
            vmem((3, order, order), f32),
            vmem(square, bf16),
            vmem(square, bf16),
            vmem(square, bf16),
            vmem(square, bf16),
            vmem((inputs, span), f32),
            vmem((4, inputs, width), f32),
            vmem((total, span), bf16),
            vmem((total, span), bf16),
            vmem((rhs, total), f32),
            vmem((rhs, total), f32),
            vmem((4, rhs, width), f32),
            vmem((rhs, width), f32),
            vmem((4, rhs, width), f32),
            vmem((12, rhs, order), f32),
            vmem((32, rhs, order), f32),
            vmem((planes, rhs, order), f32),
            vmem((rhs, order), f32),
            vmem((6, rhs, order), f32),
            vmem((4, rhs, width), f32),
            vmem((rhs, width), f32),
            vmem((4, rhs, width), f32),
            vmem((6, order, order), f32),
            vmem((2, 6, order, order), f32),
            vmem((2,) + square, bf16),
            vmem((2,) + square, bf16),
            pltpu.SemaphoreType.DMA((S.count,)),
            pltpu.SemaphoreType.REGULAR,
        ],
        compiler_params=pltpu.CompilerParams(
            collective_id=0, has_side_effects=True, vmem_limit_bytes=64 * 1024 * 1024 - 65536
        ),
    )(data, centres, scales, factor, block_inv, residual, direction)
    new_iterate = iterate + alphas * direction
    new_residual = residual - alphas * image
    new_direction = new_residual + betas * direction
    return new_iterate, new_residual, new_direction


def solution(mesh):
    placed = (
        P(None, ("dp", "crow")),
        P(None, "ccol"),
        P(),
        P("crow", "ccol"),
        P("crow", None, None),
        P(),
        P(),
        P(),
    )
    return jax.shard_map(
        per_device, mesh=mesh, in_specs=placed, out_specs=(P(), P(), P()), check_vma=False
    )
```

```python
import functools

import jax
import jax.numpy as jnp
from jax import lax
from jax.experimental import pallas as pl
from jax.experimental.pallas import tpu as pltpu
from jax.sharding import PartitionSpec as P

MESH = pl.DeviceIdType.MESH
f32 = jnp.float32
bf16 = jnp.bfloat16
HIGHEST = lax.Precision.HIGHEST
ridge_weight = 0.2

NN = (((1,), (0,)), ((), ()))
NT = (((1,), (1,)), ((), ()))
TN = (((0,), (0,)), ((), ()))


def dot(a, b, dims=NN, precision=None):
    return lax.dot_general(a, b, dims, precision=precision, preferred_element_type=f32)


def split2(v):
    high = v.astype(bf16)
    return high, (v - high.astype(f32)).astype(bf16)


def split3(v):
    high = v.astype(bf16)
    rest = v - high.astype(f32)
    mid = rest.astype(bf16)
    return high, mid, (rest - mid.astype(f32)).astype(bf16)


def product(v, high, low, dims=NN):
    rows = v.shape[0]
    both = jnp.concatenate(split2(v), axis=0)
    out = dot(both, low, dims) + dot(both, high, dims)
    return out[rows:] + out[:rows]


def lower(v, high, low, order):
    parts = [product(v[:, j:], high[j:, j : j + order], low[j:, j : j + order]) for j in range(0, v.shape[1], order)]
    return jnp.concatenate(parts, axis=1)


def upper(v, high, low, order):
    parts = []
    for j in range(0, v.shape[1], order):
        parts.append(product(v[:, : j + order], high[: j + order, j : j + order], low[: j + order, j : j + order]))
    return jnp.concatenate(parts, axis=1)


def ring_distance(d, n):
    d = d % n
    return min(d, n - d)


class Semaphores:
    def __init__(self):
        self.count = 0

    def take(self, n):
        first = self.count
        self.count += n
        return first


OWNERS = ((1, 0), (0, 0), (2, 0), (1, 1), (1, 3), (0, 1), (3, 2), (2, 2), (0, 2), (3, 3), (3, 1), (2, 3))
PLACES = ((1, 0), (2, 0), (2, 1), (0, 0), (1, 1), (2, 2))
LOW = (1, 0)
HIGH = (3, 2)

S = Semaphores()
LOAD = S.take(8)
CEN_R = S.take(4)
CEN_S = S.take(3)
CENF_S = S.take(4)
P_R = S.take(4)
P_S = S.take(16)
PF_S = S.take(4)
PROD_R = S.take(4)
PROD_S = S.take(1)
N_R = S.take(1)
N_S = S.take(16)
Z_R = S.take(1)
Z_S = S.take(16)
M_R = S.take(6)
M_S = S.take(1)
IMG_R = S.take(4)
IMG_S = S.take(30)
IMGF_S = S.take(4)
BACK_R = S.take(4)
BACK_S = S.take(1)
BULK_R = S.take(2)
BULK_S = S.take(1)


def kernel(
    planes,
    total_rows,
    data,
    centres,
    scales,
    factor,
    block_inv,
    residual,
    direction,
    image,
    alphas,
    betas,
    fac,
    inv,
    whi,
    wlo,
    thi,
    tlo,
    rows,
    cen,
    khi,
    klo,
    rev,
    div,
    pulled,
    prod_out,
    prod_in,
    nsend,
    nred,
    zred,
    mout,
    min_,
    img,
    back_out,
    back_in,
    blocks,
    aux,
    dhi,
    dlo,
    sems,
    zready,
):
    dp = lax.axis_index("dp")
    r = lax.axis_index("crow")
    c = lax.axis_index("ccol")
    core = lax.rem(dp, 2)
    z = dp // 2
    solver = core == 1
    width = fac.shape[0]
    span = rows.shape[1]
    order = inv.shape[1]
    pending = []

    def local(src, dst, k):
        return pltpu.make_async_copy(src, dst, sems.at[LOAD + k])

    def remote(src, dst, ss, rs, dev):
        return pltpu.make_async_remote_copy(
            src_ref=src,
            dst_ref=dst,
            send_sem=sems.at[ss],
            recv_sem=sems.at[rs],
            device_id=dev,
            device_id_type=MESH,
        )

    def arrived(dst, rs):
        pltpu.make_async_copy(dst, dst, sems.at[rs]).wait()

    def send(cond, src, dst, ss, rs, dev):
        remote(src(), dst(), ss, rs, dev).start()
        pending.append((cond, src, ss))

    def flush():
        groups = {}
        for cond, src, ss in pending:
            groups.setdefault(id(cond), (cond, []))[1].append((src, ss))
        pending.clear()
        for cond, sends in groups.values():

            @pl.when(cond)
            def _():
                for src, ss in sends:
                    arrived(src(), ss)

    load_fac = local(factor, fac, 0)
    under = (slice(order, width), slice(0, width - order))
    load_under = local(factor.at[under], fac.at[under], 6)
    load_inv = local(block_inv, inv, 1)
    load_dir = local(direction, div, 2)
    load_cen = local(centres, cen.at[c], 3)
    load_rows = local(data.at[:, pl.ds(pl.multiple_of(c * span, 128), span)], rows, 4)
    load_res = local(residual, rev, 5)
    diagonal = solver & (r == c)
    below = solver & (r > c)
    at_low = solver & (r == LOW[0]) & (c == LOW[1])
    at_high = solver & (r == HIGH[0]) & (c == HIGH[1])
    helpers = [(core == 0) & (r == k) & (c == k) for k in range(4)]
    holders = [solver & (r == k) & (c == k) for k in range(4)]

    @pl.when((r == c) | at_low | at_high)
    def _():
        load_inv.start()

    load_dir.start()

    @pl.when(r == c)
    def _():
        load_under.start()

    @pl.when(below)
    def _():
        load_fac.start()

    load_cen.start()
    load_rows.start()
    load_res.start()

    barrier = pltpu.get_barrier_semaphore()
    far = sorted(range(1, planes), key=lambda d: -ring_distance(d, planes))
    offsets = sorted(
        [(a, b) for a in range(4) for b in range(4)],
        key=lambda o: (-ring_distance(o[0], 4) - ring_distance(o[1], 4), o),
    )

    def signal(sem, dev):
        pl.semaphore_signal(sem, inc=1, device_id=dev, device_id_type=MESH)

    @pl.when(solver)
    def _():
        for d in (2, 1, 3):
            signal(barrier, (dp, r, lax.rem(c + d, 4)))
            signal(barrier, (dp, lax.rem(r + d, 4), c))
        for d in far:
            signal(barrier, (2 * lax.rem(z + d, planes), r, c))
        signal(barrier, (dp - 1, r, c))

    for here, users in ((at_low, (0, 1)), (at_high, (2, 3))):

        @pl.when(here)
        def _():
            for k in users:
                signal(barrier, (dp - 1, k, k))

    @pl.when(core == 0)
    def _():
        signal(barrier, (dp + 1, r, c))

    load_dir.wait()

    first = holders[3]

    @pl.when(first)
    def _():
        load_inv.wait()
        load_under.wait()
        b = [slice(k * order, (k + 1) * order) for k in range(3)]
        base = 3 * width
        d = [div[:, base + k * order : base + (k + 1) * order] for k in range(3)]
        p2 = dot(d[2], inv[2], NN, HIGHEST)
        p1 = dot(d[1] - dot(p2, fac[b[2], b[1]], NN, HIGHEST), inv[1], NN, HIGHEST)
        t0 = d[0] - dot(p2, fac[b[2], b[0]], NN, HIGHEST)
        p0 = dot(t0 - dot(p1, fac[b[1], b[0]], NN, HIGHEST), inv[0], NN, HIGHEST)
        pulled[3, :, b[0]] = p0
        pulled[3, :, b[1]] = p1
        pulled[3, :, b[2]] = p2

    def keep(v, i, j):
        si = slice(i * order, (i + 1) * order)
        sj = slice(j * order, (j + 1) * order)
        whi[si, sj], wlo[si, sj] = split2(v)
        thi[sj, si], tlo[sj, si] = split2(v.T)

    def invert():
        b = [slice(k * order, (k + 1) * order) for k in range(3)]
        mul = functools.partial(dot, precision=HIGHEST)
        a0, a1, a2 = inv[0], inv[1], inv[2]
        x10 = -mul(a1, mul(fac[b[1], b[0]], a0))
        x21 = -mul(a2, mul(fac[b[2], b[1]], a1))
        x20 = -mul(a2, mul(fac[b[2], b[0]], a0) + mul(fac[b[2], b[1]], x10))
        for i, row in enumerate(((a0,), (x10, a1), (x20, x21, a2))):
            for j, v in enumerate(row):
                blocks[PLACES.index((i, j))] = v
                whi[b[i], b[j]], wlo[b[i], b[j]] = split2(v)

    @pl.when((r == c) & jnp.logical_not(first))
    def _():
        load_inv.wait()
        load_under.wait()
        invert()

    @pl.when(below)
    def _():
        load_fac.wait()
        for i in range(3):
            for j in range(3):
                keep(fac[i * order : (i + 1) * order, j * order : (j + 1) * order], i, j)

    @pl.when(solver)
    def _():
        pl.semaphore_wait(barrier, 7)

    @pl.when(core == 0)
    def _():
        pl.semaphore_wait(barrier, planes + jnp.where(r == c, 1, 0))
        signal(zready, (dp + 1, r, c))

    def spread(source, k, cond, buf, ss, rs, urgent, first=0, last=15):
        goals = [((source[0] + a) % 4, (source[1] + b) % 4) for a, b in offsets[:-1]]
        goals = urgent + [g for g in goals if g not in urgent]
        for i, (a, b) in enumerate(goals):
            if first <= i < last:
                send(cond, lambda: buf.at[k], lambda: buf.at[k], ss + i, rs + k, (dp, a, b))

    def give_inverse(k, cond):
        goal = LOW if k < 2 else HIGH
        n = 6 - 3 * (k % 2)
        src = lambda: blocks.at[0:n]
        send(cond, src, lambda: aux.at[k % 2, 0:n], BULK_S, BULK_R + k % 2, (dp + 1,) + goal)

    def give_core0(cond, buf, k, ss, rs):
        send(cond, lambda: buf.at[k], lambda: buf.at[k], ss + k, rs + k, (dp - 1, r, c))

    @pl.when(first)
    def _():
        spread((3, 3), 3, first, pulled, P_S, P_R, [(3, 2), (3, 1), (3, 0)], 0, 3)

    load_cen.wait()

    @pl.when(solver)
    def _():
        for i, d in enumerate((2, 1, 3)):
            send(solver, lambda: cen.at[c], lambda: cen.at[c], CEN_S + i, CEN_R + c, (dp, r, lax.rem(c + d, 4)))

    for k in range(4):

        @pl.when(helpers[k])
        def _():
            give_inverse(k, helpers[k])

    scale_col = jnp.zeros((rows.shape[0], 1), f32)
    place = lax.broadcasted_iota(jnp.int32, (rows.shape[0], 1), 0)
    for k in range(rows.shape[0]):
        scale_col = jnp.where(place == k, scales[k], scale_col)

    load_rows.wait()

    for i, d in enumerate((1, 3, 2)):
        src = lax.rem(c + d, 4)
        arrived(cen.at[src], CEN_R + src)

        @pl.when(solver)
        def _():
            send(solver, lambda src=src: cen.at[src], lambda src=src: cen.at[src], CENF_S + i, CEN_R + src, (dp - 1, r, c))

    @pl.when(first)
    def _():
        spread((3, 3), 3, first, pulled, P_S, P_R, [(3, 2), (3, 1), (3, 0)], 3, 15)

    def tiles():
        x = rows[...] / scale_col
        xh, xm, xl = split3(x)
        right = jnp.concatenate([xh, xm, xh, xl, xh, xm], axis=0)
        xn = -0.5 * jnp.sum(x * x, axis=0)[None, :]
        for k in range(4):
            for q in range(3):
                m = cen[k, :, q * order : (q + 1) * order] / scale_col
                mh, mm, ml = split3(m)
                left = jnp.concatenate([mh, mh, mm, mh, ml, mm], axis=0)
                mn = -0.5 * jnp.sum(m * m, axis=0)[:, None]
                v = jnp.exp(dot(left, right, TN) + mn + xn)
                at = slice(k * width + q * order, k * width + (q + 1) * order)
                khi[at, :], klo[at, :] = split2(v)

    late = solver & (r == 3)

    @pl.when(jnp.logical_not(late))
    def _():
        tiles()

    images = jnp.zeros((div.shape[0], span), f32)

    def place_of(x, y):
        chip = 4 * x + y
        q = jnp.int32(12)
        for k, (a, b) in enumerate(OWNERS):
            q = jnp.where(chip == 4 * a + b, k, q)
        return q

    homes = [place_of(lax.rem(r + a, 4), lax.rem(c + b, 4)) for a, b in offsets]
    place_here = homes[15]

    for k in (3, 2, 1, 0):
        mine = holders[k]
        nearby = [(k, j) for j in range(k - 1, -1, -1)]

        if k < 3:

            @pl.when(mine)
            def _():
                t = div[:, k * width : (k + 1) * width]
                for j in range(3, k, -1):
                    arrived(prod_in.at[j], PROD_R + j)
                    t = t - prod_in[j]
                pulled[k] = lower(t, whi, wlo, order)
                spread((k, k), k, mine, pulled, P_S, P_R, nearby)

        @pl.when(jnp.logical_not(mine))
        def _():
            arrived(pulled.at[k], P_R + k)

        multiply = solver & (r == k) & (c < k)

        if k > 0:

            @pl.when(multiply)
            def _():
                prod_out[...] = product(pulled[k], whi[...], wlo[...])
                send(multiply, lambda: prod_out, lambda: prod_in.at[k], PROD_S, PROD_R + k, (dp, c, c))

        @pl.when(solver)
        def _():
            give_core0(solver, pulled, k, PF_S, P_R)

        if k == 3:

            @pl.when(late)
            def _():
                tiles()

        at = slice(k * width, (k + 1) * width)
        images = images + product(pulled[k], khi[at, :], klo[at, :])

    both = jnp.concatenate(split2(images), axis=0)
    rhs = div.shape[0]
    for i, (a, b) in enumerate(offsets):
        x = lax.rem(r + a, 4)
        y = lax.rem(c + b, 4)
        chunk = homes[i]
        owned = chunk < 12
        slot = 2 * i + core

        @pl.when(owned)
        def _():
            at = pl.ds(pl.multiple_of(chunk * order, order), order)
            out = dot(both, klo[at, :], NT) + dot(both, khi[at, :], NT)
            nsend[chunk] = out[rhs:] + out[:rhs]

        if i < 15:

            @pl.when(owned)
            def _():
                send(owned, lambda chunk=chunk: nsend.at[chunk], lambda: nred.at[slot], N_S + i, N_R, (2 * z + 1, x, y))

        else:

            @pl.when(owned & solver)
            def _():
                nred[31] = nsend[chunk]

            away = owned & (core == 0)

            @pl.when(away)
            def _():
                send(away, lambda chunk=chunk: nsend.at[chunk], lambda: nred.at[30], N_S + i, N_R, (2 * z + 1, x, y))

    owner = solver & (place_here < 12)

    @pl.when(solver)
    def _():
        pl.semaphore_wait(zready, 1)

    @pl.when(owner)
    def _():
        arrived(nred.at[0:31], N_R)
        total = nred[0]
        for s in range(1, 32):
            total = total + nred[s]
        zred[z] = total
        for i, d in enumerate(far):
            send(
                owner,
                lambda: zred.at[z],
                lambda: zred.at[z],
                Z_S + i,
                Z_R,
                (2 * lax.rem(z + d, planes) + 1, r, c),
            )

    @pl.when(at_low | at_high)
    def _():
        load_inv.wait()
        for k in range(2):
            arrived(aux.at[k, 0 : 6 - 3 * k], BULK_R + k)
            for n, (i, j) in enumerate(PLACES):
                si = slice(i * order, (i + 1) * order)
                sj = slice(j * order, (j + 1) * order)
                block = inv[i] if i == j and k == 1 else aux[k, n]
                dhi[k, sj, si], dlo[k, sj, si] = split2(block.T)

    flush()

    @pl.when(owner)
    def _():
        arrived(zred.at[0 : planes - 1], Z_R)
        total = zred[0]
        for s in range(1, planes):
            total = total + zred[s]
        mout[...] = total * (1.0 / total_rows)

    passing = owner & jnp.logical_not(at_low | at_high)
    goal_low = place_here < 6
    part = jnp.where(goal_low, place_here, place_here - 6)

    @pl.when(passing)
    def _():
        goal = (dp, jnp.where(goal_low, LOW[0], HIGH[0]), jnp.where(goal_low, LOW[1], HIGH[1]))
        send(passing, lambda: mout, lambda: min_.at[part], M_S, M_R + part, goal)

    def normal(k):
        base = 3 * (k % 2)
        for j in range(base, base + 3):
            if j == 0:
                min_[0] = mout[...]
            else:
                arrived(min_.at[j], M_R + j)
        joined = jnp.concatenate([min_[base], min_[base + 1], min_[base + 2]], axis=1)
        return joined + ridge_weight * pulled[k]

    @pl.when(at_low)
    def _():
        img[0] = upper(normal(0), dhi.at[0], dlo.at[0], order)
        spread(LOW, 0, at_low, img, IMG_S, IMG_R, [(2, 0), (3, 0)], 0, 2)
        t = normal(1) - product(img[0], thi[...], tlo[...])
        img[1] = upper(t, dhi.at[1], dlo.at[1], order)
        spread(LOW, 1, at_low, img, IMG_S + 15, IMG_R, [(2, 1), (3, 1)], 0, 2)
        spread(LOW, 0, at_low, img, IMG_S, IMG_R, [(2, 0), (3, 0)], 2, 15)
        spread(LOW, 1, at_low, img, IMG_S + 15, IMG_R, [(2, 1), (3, 1)], 2, 15)

    for k in range(2):
        multiply = solver & (c == k) & (r >= 2)

        @pl.when(multiply)
        def _():
            arrived(img.at[k], IMG_R + k)
            back_out[...] = product(img[k], thi[...], tlo[...])
            at = 2 * (r - 2) + k
            send(multiply, lambda: back_out, lambda at=at: back_in.at[at], BACK_S, BACK_R + at, (dp,) + HIGH)

    @pl.when(at_high)
    def _():
        for k in (2, 3):
            t = normal(k)
            if k == 3:
                t = t - product(img[2], thi[...], tlo[...])
            for j in range(2):
                at = 2 * (k - 2) + j
                arrived(back_in.at[at], BACK_R + at)
                t = t - back_in[at]
            img[k] = upper(t, dhi.at[k - 2], dlo.at[k - 2], order)
            spread(HIGH, k, at_high, img, IMG_S + 15 * (k - 2), IMG_R, [])

    segs = [slice(k * width, (k + 1) * width) for k in range(4)]
    curvature = jnp.zeros((rhs, 1), f32)
    for k in range(4):
        if k == 3:
            load_res.wait()
            gamma = jnp.sum(rev[...] * rev[...], axis=1, keepdims=True)
            for j in range(3):
                image[:, segs[j]] = img[j]
                curvature += jnp.sum(div[:, segs[j]] * img[j], axis=1, keepdims=True)
            flush()
        known = at_low | (solver & (c == k) & (r >= 2)) if k < 2 else at_high

        @pl.when(jnp.logical_not(known))
        def _():
            arrived(img.at[k], IMG_R + k)

        @pl.when(solver)
        def _():
            give_core0(solver, img, k, IMGF_S, IMG_R)

    image[:, segs[3]] = img[3]
    curvature += jnp.sum(div[:, segs[3]] * img[3], axis=1, keepdims=True)
    alpha = gamma / curvature
    gamma_next = jnp.zeros((rhs, 1), f32)
    for k in range(4):
        res = rev[:, segs[k]] - alpha * img[k]
        gamma_next += jnp.sum(res * res, axis=1, keepdims=True)
    alphas[...] = jnp.broadcast_to(alpha, alphas.shape)
    betas[...] = jnp.broadcast_to(gamma_next / gamma, betas.shape)

    flush()


def per_device(data, centres, scales, factor, block_inv, iterate, residual, direction):
    planes = lax.axis_size("dp") // 2
    total_rows = data.shape[1] * lax.axis_size("dp") * lax.axis_size("crow")
    inputs, width = centres.shape
    span = data.shape[1] // lax.axis_size("ccol")
    rhs, total = direction.shape
    order = block_inv.shape[1]
    whole = jax.ShapeDtypeStruct((rhs, total), f32)
    vmem = pltpu.VMEM
    hbm = pl.BlockSpec(memory_space=pl.ANY)
    square = (width, width)
    image, alphas, betas = pl.pallas_call(
        functools.partial(kernel, planes, total_rows),
        out_shape=(whole, whole, whole),
        in_specs=[hbm, hbm, pl.BlockSpec(memory_space=pltpu.SMEM)] + [hbm] * 4,
        out_specs=(pl.BlockSpec(memory_space=pltpu.VMEM),) * 3,
        scratch_shapes=[
            vmem(square, f32),
            vmem((3, order, order), f32),
            vmem(square, bf16),
            vmem(square, bf16),
            vmem(square, bf16),
            vmem(square, bf16),
            vmem((inputs, span), f32),
            vmem((4, inputs, width), f32),
            vmem((total, span), bf16),
            vmem((total, span), bf16),
            vmem((rhs, total), f32),
            vmem((rhs, total), f32),
            vmem((4, rhs, width), f32),
            vmem((rhs, width), f32),
            vmem((4, rhs, width), f32),
            vmem((12, rhs, order), f32),
            vmem((32, rhs, order), f32),
            vmem((planes, rhs, order), f32),
            vmem((rhs, order), f32),
            vmem((6, rhs, order), f32),
            vmem((4, rhs, width), f32),
            vmem((rhs, width), f32),
            vmem((4, rhs, width), f32),
            vmem((6, order, order), f32),
            vmem((2, 6, order, order), f32),
            vmem((2,) + square, bf16),
            vmem((2,) + square, bf16),
            pltpu.SemaphoreType.DMA((S.count,)),
            pltpu.SemaphoreType.REGULAR,
        ],
        compiler_params=pltpu.CompilerParams(
            collective_id=0, has_side_effects=True, vmem_limit_bytes=64 * 1024 * 1024 - 65536
        ),
    )(data, centres, scales, factor, block_inv, residual, direction)
    new_iterate = iterate + alphas * direction
    new_residual = residual - alphas * image
    new_direction = new_residual + betas * direction
    return new_iterate, new_residual, new_direction


def solution(mesh):
    placed = (
        P(None, ("dp", "crow")),
        P(None, "ccol"),
        P(),
        P("crow", "ccol"),
        P("crow", None, None),
        P(),
        P(),
        P(),
    )
    return jax.shard_map(
        per_device, mesh=mesh, in_specs=placed, out_specs=(P(), P(), P()), check_vma=False
    )
```

```python
import functools

import jax
import jax.numpy as jnp
from jax import lax
from jax.experimental import pallas as pl
from jax.experimental.pallas import tpu as pltpu
from jax.sharding import PartitionSpec as P

MESH = pl.DeviceIdType.MESH
f32 = jnp.float32
bf16 = jnp.bfloat16
HIGHEST = lax.Precision.HIGHEST
ridge_weight = 0.2

NN = (((1,), (0,)), ((), ()))
NT = (((1,), (1,)), ((), ()))
TN = (((0,), (0,)), ((), ()))


def dot(a, b, dims=NN, precision=None):
    return lax.dot_general(a, b, dims, precision=precision, preferred_element_type=f32)


def split2(v):
    high = v.astype(bf16)
    return high, (v - high.astype(f32)).astype(bf16)


def split3(v):
    high = v.astype(bf16)
    rest = v - high.astype(f32)
    mid = rest.astype(bf16)
    return high, mid, (rest - mid.astype(f32)).astype(bf16)


def product(v, high, low, dims=NN):
    rows = v.shape[0]
    both = jnp.concatenate(split2(v), axis=0)
    out = dot(both, low, dims) + dot(both, high, dims)
    return out[rows:] + out[:rows]


def lower(v, high, low, order):
    parts = [product(v[:, j:], high[j:, j : j + order], low[j:, j : j + order]) for j in range(0, v.shape[1], order)]
    return jnp.concatenate(parts, axis=1)


def upper(v, high, low, order):
    parts = []
    for j in range(0, v.shape[1], order):
        parts.append(product(v[:, : j + order], high[: j + order, j : j + order], low[: j + order, j : j + order]))
    return jnp.concatenate(parts, axis=1)


def ring_distance(d, n):
    d = d % n
    return min(d, n - d)


class Semaphores:
    def __init__(self):
        self.count = 0

    def take(self, n):
        first = self.count
        self.count += n
        return first


OWNERS = ((1, 0), (0, 0), (2, 0), (1, 1), (1, 3), (0, 1), (3, 2), (2, 2), (0, 2), (3, 3), (3, 1), (2, 3))
PLACES = ((1, 0), (2, 0), (2, 1), (0, 0), (1, 1), (2, 2))
LOW = (1, 0)
HIGH = (3, 2)

S = Semaphores()
LOAD = S.take(8)
CEN_R = S.take(4)
CEN_S = S.take(3)
CENF_S = S.take(4)
P_R = S.take(4)
P_S = S.take(16)
PF_S = S.take(4)
PROD_R = S.take(4)
PROD_S = S.take(1)
N_R = S.take(1)
N_S = S.take(16)
Z_R = S.take(1)
Z_S = S.take(16)
M_R = S.take(6)
M_S = S.take(1)
IMG_R = S.take(4)
IMG_S = S.take(30)
IMGF_S = S.take(4)
BACK_R = S.take(4)
BACK_S = S.take(1)
BULK_R = S.take(2)
BULK_S = S.take(1)


def kernel(
    planes,
    total_rows,
    data,
    centres,
    scales,
    factor,
    block_inv,
    residual,
    direction,
    image,
    alphas,
    betas,
    fac,
    inv,
    whi,
    wlo,
    thi,
    tlo,
    rows,
    cen,
    khi,
    klo,
    rev,
    div,
    pulled,
    prod_out,
    prod_in,
    nsend,
    nred,
    zred,
    mout,
    min_,
    img,
    back_out,
    back_in,
    blocks,
    aux,
    dhi,
    dlo,
    sems,
    zready,
):
    dp = lax.axis_index("dp")
    r = lax.axis_index("crow")
    c = lax.axis_index("ccol")
    core = lax.rem(dp, 2)
    z = dp // 2
    solver = core == 1
    width = fac.shape[0]
    span = rows.shape[1]
    order = inv.shape[1]
    pending = []

    def local(src, dst, k):
        return pltpu.make_async_copy(src, dst, sems.at[LOAD + k])

    def remote(src, dst, ss, rs, dev):
        return pltpu.make_async_remote_copy(
            src_ref=src,
            dst_ref=dst,
            send_sem=sems.at[ss],
            recv_sem=sems.at[rs],
            device_id=dev,
            device_id_type=MESH,
        )

    def arrived(dst, rs):
        pltpu.make_async_copy(dst, dst, sems.at[rs]).wait()

    def send(cond, src, dst, ss, rs, dev):
        remote(src(), dst(), ss, rs, dev).start()
        pending.append((cond, src, ss))

    def flush():
        groups = {}
        for cond, src, ss in pending:
            groups.setdefault(id(cond), (cond, []))[1].append((src, ss))
        pending.clear()
        for cond, sends in groups.values():

            @pl.when(cond)
            def _():
                for src, ss in sends:
                    arrived(src(), ss)

    load_fac = local(factor, fac, 0)
    under = (slice(order, width), slice(0, width - order))
    load_under = local(factor.at[under], fac.at[under], 6)
    load_inv = local(block_inv, inv, 1)
    load_dir = local(direction, div, 2)
    load_cen = local(centres, cen.at[c], 3)
    load_rows = local(data.at[:, pl.ds(pl.multiple_of(c * span, 128), span)], rows, 4)
    load_res = local(residual, rev, 5)
    diagonal = solver & (r == c)
    below = solver & (r > c)
    at_low = solver & (r == LOW[0]) & (c == LOW[1])
    at_high = solver & (r == HIGH[0]) & (c == HIGH[1])
    helpers = [(core == 0) & (r == k) & (c == k) for k in range(4)]
    holders = [solver & (r == k) & (c == k) for k in range(4)]

    @pl.when((r == c) | at_low | at_high)
    def _():
        load_inv.start()

    load_dir.start()

    @pl.when(r == c)
    def _():
        load_under.start()

    @pl.when(below)
    def _():
        load_fac.start()

    load_cen.start()
    load_rows.start()
    load_res.start()

    barrier = pltpu.get_barrier_semaphore()
    far = sorted(range(1, planes), key=lambda d: -ring_distance(d, planes))
    offsets = sorted(
        [(a, b) for a in range(4) for b in range(4)],
        key=lambda o: (-ring_distance(o[0], 4) - ring_distance(o[1], 4), o),
    )

    def signal(sem, dev):
        pl.semaphore_signal(sem, inc=1, device_id=dev, device_id_type=MESH)

    @pl.when(solver)
    def _():
        for d in (2, 1, 3):
            signal(barrier, (dp, r, lax.rem(c + d, 4)))
            signal(barrier, (dp, lax.rem(r + d, 4), c))
        for d in far:
            signal(barrier, (2 * lax.rem(z + d, planes), r, c))
        signal(barrier, (dp - 1, r, c))

    for here, users in ((at_low, (0, 1)), (at_high, (2, 3))):

        @pl.when(here)
        def _():
            for k in users:
                signal(barrier, (dp - 1, k, k))

    @pl.when(core == 0)
    def _():
        signal(barrier, (dp + 1, r, c))

    load_dir.wait()

    first = holders[3]

    @pl.when(first)
    def _():
        load_inv.wait()
        load_under.wait()
        b = [slice(k * order, (k + 1) * order) for k in range(3)]
        base = 3 * width
        d = [div[:, base + k * order : base + (k + 1) * order] for k in range(3)]
        p2 = dot(d[2], inv[2], NN, HIGHEST)
        p1 = dot(d[1] - dot(p2, fac[b[2], b[1]], NN, HIGHEST), inv[1], NN, HIGHEST)
        t0 = d[0] - dot(p2, fac[b[2], b[0]], NN, HIGHEST)
        p0 = dot(t0 - dot(p1, fac[b[1], b[0]], NN, HIGHEST), inv[0], NN, HIGHEST)
        pulled[3, :, b[0]] = p0
        pulled[3, :, b[1]] = p1
        pulled[3, :, b[2]] = p2

    def keep(v, i, j):
        si = slice(i * order, (i + 1) * order)
        sj = slice(j * order, (j + 1) * order)
        whi[si, sj], wlo[si, sj] = split2(v)
        thi[sj, si], tlo[sj, si] = split2(v.T)

    def invert():
        b = [slice(k * order, (k + 1) * order) for k in range(3)]
        mul = functools.partial(dot, precision=HIGHEST)
        a0, a1, a2 = inv[0], inv[1], inv[2]
        x10 = -mul(a1, mul(fac[b[1], b[0]], a0))
        x21 = -mul(a2, mul(fac[b[2], b[1]], a1))
        x20 = -mul(a2, mul(fac[b[2], b[0]], a0) + mul(fac[b[2], b[1]], x10))
        for i, row in enumerate(((a0,), (x10, a1), (x20, x21, a2))):
            for j, v in enumerate(row):
                blocks[PLACES.index((i, j))] = v
                whi[b[i], b[j]], wlo[b[i], b[j]] = split2(v)

    @pl.when((r == c) & jnp.logical_not(first))
    def _():
        load_inv.wait()
        load_under.wait()
        invert()

    @pl.when(below)
    def _():
        load_fac.wait()
        for i in range(3):
            for j in range(3):
                keep(fac[i * order : (i + 1) * order, j * order : (j + 1) * order], i, j)

    @pl.when(solver)
    def _():
        pl.semaphore_wait(barrier, 7)

    @pl.when(core == 0)
    def _():
        pl.semaphore_wait(barrier, planes + jnp.where(r == c, 1, 0))
        signal(zready, (dp + 1, r, c))

    def spread(source, k, cond, buf, ss, rs, urgent, first=0, last=15):
        goals = [((source[0] + a) % 4, (source[1] + b) % 4) for a, b in offsets[:-1]]
        goals = urgent + [g for g in goals if g not in urgent]
        for i, (a, b) in enumerate(goals):
            if first <= i < last:
                send(cond, lambda: buf.at[k], lambda: buf.at[k], ss + i, rs + k, (dp, a, b))

    def give_inverse(k, cond):
        goal = LOW if k < 2 else HIGH
        n = 6 - 3 * (k % 2)
        src = lambda: blocks.at[0:n]
        send(cond, src, lambda: aux.at[k % 2, 0:n], BULK_S, BULK_R + k % 2, (dp + 1,) + goal)

    def give_core0(cond, buf, k, ss, rs):
        send(cond, lambda: buf.at[k], lambda: buf.at[k], ss + k, rs + k, (dp - 1, r, c))

    @pl.when(first)
    def _():
        spread((3, 3), 3, first, pulled, P_S, P_R, [(3, 2), (3, 1), (3, 0)], 0, 3)

    load_cen.wait()

    @pl.when(solver)
    def _():
        for i, d in enumerate((2, 1, 3)):
            send(solver, lambda: cen.at[c], lambda: cen.at[c], CEN_S + i, CEN_R + c, (dp, r, lax.rem(c + d, 4)))

    for k in range(4):

        @pl.when(helpers[k])
        def _():
            give_inverse(k, helpers[k])

    scale_col = jnp.zeros((rows.shape[0], 1), f32)
    place = lax.broadcasted_iota(jnp.int32, (rows.shape[0], 1), 0)
    for k in range(rows.shape[0]):
        scale_col = jnp.where(place == k, scales[k], scale_col)

    load_rows.wait()

    for i, d in enumerate((1, 3, 2)):
        src = lax.rem(c + d, 4)
        arrived(cen.at[src], CEN_R + src)

        @pl.when(solver)
        def _():
            send(solver, lambda src=src: cen.at[src], lambda src=src: cen.at[src], CENF_S + i, CEN_R + src, (dp - 1, r, c))

    @pl.when(first)
    def _():
        spread((3, 3), 3, first, pulled, P_S, P_R, [(3, 2), (3, 1), (3, 0)], 3, 15)

    def tiles():
        x = rows[...] / scale_col
        xh, xm, xl = split3(x)
        right = jnp.concatenate([xh, xm, xh, xl, xh, xm], axis=0)
        xn = -0.5 * jnp.sum(x * x, axis=0)[None, :]
        for k in range(4):
            for q in range(3):
                m = cen[k, :, q * order : (q + 1) * order] / scale_col
                mh, mm, ml = split3(m)
                left = jnp.concatenate([mh, mh, mm, mh, ml, mm], axis=0)
                mn = -0.5 * jnp.sum(m * m, axis=0)[:, None]
                v = jnp.exp(dot(left, right, TN) + mn + xn)
                at = slice(k * width + q * order, k * width + (q + 1) * order)
                khi[at, :], klo[at, :] = split2(v)

    late = solver & (r == 3)

    @pl.when(jnp.logical_not(late))
    def _():
        tiles()

    images = jnp.zeros((div.shape[0], span), f32)

    def place_of(x, y):
        chip = 4 * x + y
        q = jnp.int32(12)
        for k, (a, b) in enumerate(OWNERS):
            q = jnp.where(chip == 4 * a + b, k, q)
        return q

    homes = [place_of(lax.rem(r + a, 4), lax.rem(c + b, 4)) for a, b in offsets]
    place_here = homes[15]

    for k in (3, 2, 1, 0):
        mine = holders[k]
        nearby = [(k, j) for j in range(k - 1, -1, -1)]

        if k < 3:

            @pl.when(mine)
            def _():
                t = div[:, k * width : (k + 1) * width]
                for j in range(3, k, -1):
                    arrived(prod_in.at[j], PROD_R + j)
                    t = t - prod_in[j]
                pulled[k] = lower(t, whi, wlo, order)
                spread((k, k), k, mine, pulled, P_S, P_R, nearby)

        @pl.when(jnp.logical_not(mine))
        def _():
            arrived(pulled.at[k], P_R + k)

        multiply = solver & (r == k) & (c < k)

        if k > 0:

            @pl.when(multiply)
            def _():
                prod_out[...] = product(pulled[k], whi[...], wlo[...])
                send(multiply, lambda: prod_out, lambda: prod_in.at[k], PROD_S, PROD_R + k, (dp, c, c))

        @pl.when(solver)
        def _():
            give_core0(solver, pulled, k, PF_S, P_R)

        if k == 3:

            @pl.when(late)
            def _():
                tiles()

        at = slice(k * width, (k + 1) * width)
        images = images + product(pulled[k], khi[at, :], klo[at, :])

    both = jnp.concatenate(split2(images), axis=0)
    rhs = div.shape[0]
    for i, (a, b) in enumerate(offsets):
        x = lax.rem(r + a, 4)
        y = lax.rem(c + b, 4)
        chunk = homes[i]
        owned = chunk < 12
        slot = 2 * i + core

        @pl.when(owned)
        def _():
            at = pl.ds(pl.multiple_of(chunk * order, order), order)
            out = dot(both, klo[at, :], NT) + dot(both, khi[at, :], NT)
            nsend[chunk] = out[rhs:] + out[:rhs]

        if i < 15:

            @pl.when(owned)
            def _():
                send(owned, lambda chunk=chunk: nsend.at[chunk], lambda: nred.at[slot], N_S + i, N_R, (2 * z + 1, x, y))

        else:

            @pl.when(owned & solver)
            def _():
                nred[31] = nsend[chunk]

            away = owned & (core == 0)

            @pl.when(away)
            def _():
                send(away, lambda chunk=chunk: nsend.at[chunk], lambda: nred.at[30], N_S + i, N_R, (2 * z + 1, x, y))

    owner = solver & (place_here < 12)

    @pl.when(solver)
    def _():
        pl.semaphore_wait(zready, 1)

    @pl.when(owner)
    def _():
        arrived(nred.at[0:31], N_R)
        total = nred[0]
        for s in range(1, 32):
            total = total + nred[s]
        zred[z] = total
        for i, d in enumerate(far):
            send(
                owner,
                lambda: zred.at[z],
                lambda: zred.at[z],
                Z_S + i,
                Z_R,
                (2 * lax.rem(z + d, planes) + 1, r, c),
            )

    @pl.when(at_low | at_high)
    def _():
        load_inv.wait()
        for k in range(2):
            arrived(aux.at[k, 0 : 6 - 3 * k], BULK_R + k)
            for n, (i, j) in enumerate(PLACES):
                si = slice(i * order, (i + 1) * order)
                sj = slice(j * order, (j + 1) * order)
                block = inv[i] if i == j and k == 1 else aux[k, n]
                dhi[k, sj, si], dlo[k, sj, si] = split2(block.T)

    flush()

    @pl.when(owner)
    def _():
        arrived(zred.at[0 : planes - 1], Z_R)
        total = zred[0]
        for s in range(1, planes):
            total = total + zred[s]
        mout[...] = total * (1.0 / total_rows)

    passing = owner & jnp.logical_not(at_low | at_high)
    goal_low = place_here < 6
    part = jnp.where(goal_low, place_here, place_here - 6)

    @pl.when(passing)
    def _():
        goal = (dp, jnp.where(goal_low, LOW[0], HIGH[0]), jnp.where(goal_low, LOW[1], HIGH[1]))
        send(passing, lambda: mout, lambda: min_.at[part], M_S, M_R + part, goal)

    def normal(k):
        base = 3 * (k % 2)
        for j in range(base, base + 3):
            if j == 0:
                min_[0] = mout[...]
            else:
                arrived(min_.at[j], M_R + j)
        joined = jnp.concatenate([min_[base], min_[base + 1], min_[base + 2]], axis=1)
        return joined + ridge_weight * pulled[k]

    @pl.when(at_low)
    def _():
        img[0] = upper(normal(0), dhi.at[0], dlo.at[0], order)
        spread(LOW, 0, at_low, img, IMG_S, IMG_R, [(2, 0), (3, 0)], 0, 2)
        t = normal(1) - product(img[0], thi[...], tlo[...])
        img[1] = upper(t, dhi.at[1], dlo.at[1], order)
        spread(LOW, 1, at_low, img, IMG_S + 15, IMG_R, [(2, 1), (3, 1)], 0, 2)
        spread(LOW, 0, at_low, img, IMG_S, IMG_R, [(2, 0), (3, 0)], 2, 15)
        spread(LOW, 1, at_low, img, IMG_S + 15, IMG_R, [(2, 1), (3, 1)], 2, 15)

    for k in range(2):
        multiply = solver & (c == k) & (r >= 2)

        @pl.when(multiply)
        def _():
            arrived(img.at[k], IMG_R + k)
            back_out[...] = product(img[k], thi[...], tlo[...])
            at = 2 * (r - 2) + k
            send(multiply, lambda: back_out, lambda at=at: back_in.at[at], BACK_S, BACK_R + at, (dp,) + HIGH)

    @pl.when(at_high)
    def _():
        for k in (2, 3):
            t = normal(k)
            if k == 3:
                t = t - product(img[2], thi[...], tlo[...])
            for j in range(2):
                at = 2 * (k - 2) + j
                arrived(back_in.at[at], BACK_R + at)
                t = t - back_in[at]
            img[k] = upper(t, dhi.at[k - 2], dlo.at[k - 2], order)
        for k in (3, 2):
            spread(HIGH, k, at_high, img, IMG_S + 15 * (k - 2), IMG_R, [])

    segs = [slice(k * width, (k + 1) * width) for k in range(4)]
    curvature = jnp.zeros((rhs, 1), f32)
    for k in range(4):
        if k == 3:
            load_res.wait()
            gamma = jnp.sum(rev[...] * rev[...], axis=1, keepdims=True)
            for j in range(3):
                image[:, segs[j]] = img[j]
                curvature += jnp.sum(div[:, segs[j]] * img[j], axis=1, keepdims=True)
            flush()
        known = at_low | (solver & (c == k) & (r >= 2)) if k < 2 else at_high

        @pl.when(jnp.logical_not(known))
        def _():
            arrived(img.at[k], IMG_R + k)

        @pl.when(solver)
        def _():
            give_core0(solver, img, k, IMGF_S, IMG_R)

    image[:, segs[3]] = img[3]
    curvature += jnp.sum(div[:, segs[3]] * img[3], axis=1, keepdims=True)
    alpha = gamma / curvature
    gamma_next = jnp.zeros((rhs, 1), f32)
    for k in range(4):
        res = rev[:, segs[k]] - alpha * img[k]
        gamma_next += jnp.sum(res * res, axis=1, keepdims=True)
    alphas[...] = jnp.broadcast_to(alpha, alphas.shape)
    betas[...] = jnp.broadcast_to(gamma_next / gamma, betas.shape)

    flush()


def per_device(data, centres, scales, factor, block_inv, iterate, residual, direction):
    planes = lax.axis_size("dp") // 2
    total_rows = data.shape[1] * lax.axis_size("dp") * lax.axis_size("crow")
    inputs, width = centres.shape
    span = data.shape[1] // lax.axis_size("ccol")
    rhs, total = direction.shape
    order = block_inv.shape[1]
    whole = jax.ShapeDtypeStruct((rhs, total), f32)
    vmem = pltpu.VMEM
    hbm = pl.BlockSpec(memory_space=pl.ANY)
    square = (width, width)
    image, alphas, betas = pl.pallas_call(
        functools.partial(kernel, planes, total_rows),
        out_shape=(whole, whole, whole),
        in_specs=[hbm, hbm, pl.BlockSpec(memory_space=pltpu.SMEM)] + [hbm] * 4,
        out_specs=(pl.BlockSpec(memory_space=pltpu.VMEM),) * 3,
        scratch_shapes=[
            vmem(square, f32),
            vmem((3, order, order), f32),
            vmem(square, bf16),
            vmem(square, bf16),
            vmem(square, bf16),
            vmem(square, bf16),
            vmem((inputs, span), f32),
            vmem((4, inputs, width), f32),
            vmem((total, span), bf16),
            vmem((total, span), bf16),
            vmem((rhs, total), f32),
            vmem((rhs, total), f32),
            vmem((4, rhs, width), f32),
            vmem((rhs, width), f32),
            vmem((4, rhs, width), f32),
            vmem((12, rhs, order), f32),
            vmem((32, rhs, order), f32),
            vmem((planes, rhs, order), f32),
            vmem((rhs, order), f32),
            vmem((6, rhs, order), f32),
            vmem((4, rhs, width), f32),
            vmem((rhs, width), f32),
            vmem((4, rhs, width), f32),
            vmem((6, order, order), f32),
            vmem((2, 6, order, order), f32),
            vmem((2,) + square, bf16),
            vmem((2,) + square, bf16),
            pltpu.SemaphoreType.DMA((S.count,)),
            pltpu.SemaphoreType.REGULAR,
        ],
        compiler_params=pltpu.CompilerParams(
            collective_id=0, has_side_effects=True, vmem_limit_bytes=64 * 1024 * 1024 - 65536
        ),
    )(data, centres, scales, factor, block_inv, residual, direction)
    new_iterate = iterate + alphas * direction
    new_residual = residual - alphas * image
    new_direction = new_residual + betas * direction
    return new_iterate, new_residual, new_direction


def solution(mesh):
    placed = (
        P(None, ("dp", "crow")),
        P(None, "ccol"),
        P(),
        P("crow", "ccol"),
        P("crow", None, None),
        P(),
        P(),
        P(),
    )
    return jax.shard_map(
        per_device, mesh=mesh, in_specs=placed, out_specs=(P(), P(), P()), check_vma=False
    )
```
